32 devices in a mesh: group: 2 (over x), member: 8 (over z, y), role: 2 (over core).
Axes of the slice: x: 2, y: 2, z: 4, core: 2. Of those that a mesh axis runs over, the one named last changes fastest.
Arguments:
- frames: bfloat16 [16, 2, 256, 1024], P(('group', 'member'), 'role'), may hold values from -6 to 6
- cotangent: bfloat16 [16, 2, 256, 1024], P(('group', 'member'), 'role'), may hold values from -6 to 6
- w_qkv: bfloat16 [1024, 3072], replicated, may hold values from -0.1875 to 0.1875
- w_out: bfloat16 [1024, 1024], replicated, may hold values from -1 to 1
- w_up: bfloat16 [1024, 4096], replicated, may hold values from -0.1875 to 0.1875
- w_down: bfloat16 [4096, 1024], replicated, may hold values from -0.09375 to 0.09375
- gains: bfloat16 [7, 2, 1024], replicated, may hold values from 0.25 to 1.75
- shifts: bfloat16 [7, 2, 1024], replicated, may hold values from -3 to 3
- prompt_len: int32 [16], P(('group', 'member')), may hold values from 64 to 256, as said below
- section: int32 [16], P(('group', 'member')), may hold values from 0 to 6
Outputs:
- output: bfloat16 [16, 2, 256, 1024], P(('group', 'member'), 'role')
- input_grad: float32 [16, 2, 256, 1024], P(('group', 'member'), 'role')
- grad_params: float32 [12611584], P(('member', 'role'))
The draws below stay inside these ranges and needn't reach their ends.
Inputs may be any that keep to these rules, and one draw needn't show every extreme that they name: `prompt_len`: some utterance has a prompt of 256 frames.
All inputs are finite; a program needn't handle non-finite values.
Results may differ from the reference program's by a relative error of at most 0.01.
Values may be sent and summed in bfloat16 or wider, within the bound.
No kernel may reach another device: no remote copies, remote signals or barrier semaphores. Data moves between devices by JAX's collectives and lax.ppermute only.
A program may use at most 256 MiB of HBM per device.

```python
import jax
import jax.numpy as jnp
from jax import lax

D = 1024
HEADS = 16
FF = 4096
SECTIONS = 7
HEAD = 64
TOK_DEV = 256
SEQS = 16


def draw_prompt_len(key, part):
    length_key, chosen_key = jax.random.split(key)
    lengths = jax.random.randint(length_key, (SEQS,), max(1, TOK_DEV // 4), TOK_DEV + 1)
    chosen = jax.random.randint(chosen_key, (), 0, SEQS)
    return jnp.where(jnp.arange(SEQS) == chosen, TOK_DEV, lengths).astype(jnp.int32)


def plant(array, key, low, largest):
    extent = array.shape
    index_at = [jax.random.randint(jax.random.fold_in(key, axis), (), 0, extent[axis]) for axis in range(len(extent))]
    array = array.at[tuple(index_at)].set(low)
    longest = extent.index(max(extent))
    index_at[longest] = (index_at[longest] + 1) % extent[longest]
    return array.at[tuple(index_at)].set(largest)


def levels(own_key, shape, cuts, smallest, high):
    def one(axis_at, blocks):
        draws = jax.random.uniform(jax.random.fold_in(jax.random.fold_in(own_key, 6), axis_at), (blocks,), jnp.float32, smallest / len(cuts), high / len(cuts))
        return jnp.repeat(jnp.exp(draws), shape[axis_at] // blocks).reshape((-1,) + (1,) * (len(shape) - axis_at - 1))

    loudness = one(*cuts[0])
    for cut in cuts[1:]:
        loudness = loudness * one(*cut)
    return loudness


def noise(rng, shape, scale, bound, shards=(), kind=jnp.bfloat16):
    values = scale * jax.random.normal(rng, shape, jnp.float32)
    if shards:
        values = values * levels(rng, shape, shards, -0.22, 0.18)
    return jnp.clip(values, -bound, bound).astype(kind)


def setup_inputs(seed: int = 0) -> dict:
    streams_of = jax.random.split(jax.random.key(seed), 11)
    frames = noise(streams_of[0], (SEQS, 2, TOK_DEV, D), 1.0, 6.0, ((0, 16), (1, 2)))
    cotangent = noise(streams_of[1], (SEQS, 2, TOK_DEV, D), 1.0, 6.0, ((0, 16), (1, 2)))
    w_qkv = noise(streams_of[2], (D, 3 * D), D ** -0.5, 0.1875)
    w_out = noise(streams_of[3], (D, D), (max(1, D * 8 // TOK_DEV)) ** -0.5, 1.0)
    w_up = noise(streams_of[4], (D, FF), D ** -0.5, 0.1875)
    w_down = noise(streams_of[5], (FF, D), FF ** -0.5, 0.09375)
    gains = jnp.clip(1.0 + 0.15 * jax.random.normal(streams_of[6], (SECTIONS, 2, D), jnp.float32), 0.25, 1.75).astype(jnp.bfloat16)
    shifts = noise(streams_of[7], (SECTIONS, 2, D), 0.5, 3.0)
    prompt_len = draw_prompt_len(jax.random.fold_in(streams_of[10], 71), 0)
    section = plant(jax.random.randint(streams_of[9], (SEQS,), 0, SECTIONS), jax.random.fold_in(streams_of[9], 1), 0, SECTIONS - 1).astype(jnp.int32)
    return {"frames": frames, "cotangent": cotangent, "w_qkv": w_qkv, "w_out": w_out, "w_up": w_up, "w_down": w_down, "gains": gains, "shifts": shifts, "prompt_len": prompt_len, "section": section}


@jax.custom_vjp
def low(v):
    return lax.optimization_barrier(v.astype(jnp.bfloat16)).astype(jnp.float32)

@jax.custom_vjp
def low_back(v):
    return v

def low_keep(v):
    return (low(v), None)

def low_pass(kept, grad):
    return (grad,)

def back_keep(v):
    return (v, None)

def back_low(kept, grad):
    return (low(grad),)
low.defvjp(low_keep, low_pass)
low_back.defvjp(back_keep, back_low)
precise = lax.Precision.HIGHEST

def matmul(left_side, right_side):
    return jnp.dot(left_side, right_side, precision=precise, preferred_element_type=jnp.float32)

def normalize(values):
    center = values - lax.optimization_barrier(jnp.mean(values, axis=-1, keepdims=True))
    spread = lax.optimization_barrier(jnp.mean(center * center, axis=-1, keepdims=True))
    return center * lax.rsqrt(spread + 1e-05)

def utterance(frame_rows, w_qkv, w_out, w_up, w_down, gains, shifts, select, allowed):
    gain_rows = jnp.einsum('s,sjd->jd', select, gains, precision=precise)
    shift_rows = jnp.einsum('s,sjd->jd', select, shifts, precision=precise)
    hidden_one = low(normalize(frame_rows) * gain_rows[0] + shift_rows[0])
    qkv_all = low(low_back(matmul(hidden_one, w_qkv)))
    row_count = frame_rows.shape[0]
    heads_q = qkv_all[:, :D].reshape(row_count, HEADS, HEAD)
    heads_k = qkv_all[:, D:2 * D].reshape(row_count, HEADS, HEAD)
    heads_v = qkv_all[:, 2 * D:].reshape(row_count, HEADS, HEAD)
    scores = jnp.einsum('ihd,jhd->hij', heads_q, heads_k, precision=precise) * HEAD ** (-0.5)
    scores = low_back(scores)
    scores = jnp.where(allowed[None], scores, -1e+30)
    row_max = lax.optimization_barrier(jnp.max(scores, axis=-1, keepdims=True))
    exponent = jnp.exp(scores - row_max)
    prob_low = low(exponent / lax.optimization_barrier(jnp.sum(exponent, axis=-1, keepdims=True)))
    attended = jnp.einsum('hij,jhd->ihd', prob_low, heads_v, precision=precise).reshape(row_count, D)
    attended = low(low_back(attended))
    residual = frame_rows + low_back(matmul(attended, w_out))
    hidden_two = low(normalize(residual) * gain_rows[1] + shift_rows[1])
    upward = low_back(matmul(hidden_two, w_up))
    active = low(jax.nn.gelu(upward, approximate=False))
    return residual + low_back(matmul(active, w_down))

def reference(frames, cotangent, w_qkv, w_out, w_up, w_down, gains, shifts, prompt_len, section):
    weights = (w_qkv.astype(jnp.float32), w_out.astype(jnp.float32), w_up.astype(jnp.float32), w_down.astype(jnp.float32), gains.astype(jnp.float32), shifts.astype(jnp.float32))
    frame_all = frames.astype(jnp.float32).reshape(SEQS, 2 * TOK_DEV, D)
    cot_all = cotangent.astype(jnp.float32).reshape(SEQS, 2 * TOK_DEV, D)
    positions = jnp.arange(2 * TOK_DEV, dtype=jnp.int32)

    def one_step(running, per_seq):
        frame_rows, cot_rows, length, section_id = per_seq
        select = (jnp.arange(SECTIONS, dtype=jnp.int32) == section_id).astype(jnp.float32)
        query_target = positions[:, None] >= TOK_DEV
        key_target = positions[None, :] >= TOK_DEV
        allowed = jnp.where(key_target, query_target, positions[None, :] < length)

        def forward(rows_in, qkv_in, out_in, up_in, down_in, gains_in, shifts_in):
            return utterance(rows_in, qkv_in, out_in, up_in, down_in, gains_in, shifts_in, select, allowed)
        result, pullback = jax.vjp(forward, frame_rows, weights[0], weights[1], weights[2], weights[3], weights[4], weights[5])
        grad_terms = pullback(cot_rows)
        running = tuple((total + term for total, term in zip(running, grad_terms[1:])))
        return (running, (result.astype(jnp.bfloat16), grad_terms[0]))
    zero_grads = tuple((jnp.zeros_like(weight) for weight in weights))
    totals, (outputs, input_grads) = lax.scan(one_step, zero_grads, (frame_all, cot_all, prompt_len, section))
    grad_params = jnp.concatenate([total.reshape(-1) for total in totals])
    return (outputs.reshape(SEQS, 2, TOK_DEV, D), input_grads.reshape(SEQS, 2, TOK_DEV, D), grad_params)
```

```python
import jax
import jax.numpy as jnp
import numpy as np
from jax import lax
from jax.sharding import PartitionSpec as P

HEADS = 16
LANE = 128
F32 = jnp.float32
BF16 = jnp.bfloat16


def dot(left, right, dims):
    return lax.dot_general(left, right, (dims, ((), ())), preferred_element_type=F32)


def mm(left, right):
    return dot(left, right, ((1,), (0,)))


def mm_nt(left, right):
    return dot(left, right, ((1,), (1,)))


def mm_tn(left, right):
    return dot(left, right, ((0,), (0,)))


def swap(value, axis, distance=1):
    count = lax.axis_size(axis)
    return lax.ppermute(value, axis, [(i, i ^ distance) for i in range(count)])


def norm_stats(values):
    center = values - jnp.mean(values, axis=-1, keepdims=True)
    rstd = lax.rsqrt(jnp.mean(center * center, axis=-1, keepdims=True) + 1e-05)
    return center * rstd, rstd


def norm_back(unit, rstd, gain, grad):
    grad_unit = grad * gain
    inner = grad_unit - jnp.mean(grad_unit, axis=-1, keepdims=True)
    return rstd * (inner - unit * jnp.mean(grad_unit * unit, axis=-1, keepdims=True))


class Layout:
    def __init__(self, width, ff, sections, members, outer):
        self.width, self.ff, self.members, self.outer = width, ff, members, outer
        shapes = {"q": (width, 3 * width), "o": (width, width), "u": (width, ff), "d": (ff, width), "s": (4 * sections, width)}
        start, self.spans = 0, {}
        for name, (rows, columns) in shapes.items():
            self.spans[name] = (start, rows, columns)
            start += rows * columns
        self.total = start
        self.share = start // members
        self.piece = {"q": (width, 3 * width // 4), "o": (width // 4, width), "u": (width, ff // 4), "d": (ff // 4, width)}

    def span(self, member, name):
        start, rows, columns = self.spans[name]
        low = max(member * self.share, start) - start
        high = min((member + 1) * self.share, start + rows * columns) - start
        return (low, high) if low < high else None

    def piece_rows(self, member, name):
        found = self.span(member, name)
        if found is None:
            return None
        columns = self.spans[name][2]
        low, high = found[0] // columns, -(-found[1] // columns)
        if name == "o":
            rows = self.piece["o"][0]
            held = [r % rows for r in range(low, high)]
            low, high = min(held), max(held) + 1
        if name == "d":
            held = [r // (4 * LANE) * LANE + r % LANE for r in range(low, high)]
            low, high = min(held), max(held) + 1
        return (low // 16 * 16, -(-high // 16) * 16)

    def segments(self, member, names):
        found = [(name, self.piece_rows(member, name)) for name in names]
        return [(name, rows) for name, rows in found if rows is not None]

    def natural(self, member, name, pieces):
        low, high = self.span(member, name)
        first, last = self.piece_rows(member, name)
        columns = self.spans[name][2]
        rows = last - first
        if name == "q":
            stack = jnp.stack([jnp.stack([pieces[x][r].reshape(rows, 3, -1) for x in range(2)], 2) for r in range(2)], 2)
            base = first * columns
        elif name == "u":
            stack = jnp.stack([jnp.stack([pieces[x][r].reshape(rows, -1, LANE) for r in range(2)], 2) for x in range(2)], 2)
            base = first * columns
        elif name == "o":
            total = self.piece["o"][0]
            pad = ((first, total - last), (0, 0))
            stack = jnp.stack([jnp.stack([jnp.pad(pieces[x][r], pad) for x in range(2)]) for r in range(2)])
            base = 0
        else:
            begin, end = first // LANE * LANE, -(-last // LANE) * LANE
            pad = ((first - begin, end - last), (0, 0))
            stack = jnp.stack([jnp.stack([jnp.pad(pieces[x][r], pad).reshape(-1, LANE, columns) for r in range(2)], 1) for x in range(2)], 1)
            base = begin * 4 * columns
        return stack.reshape(-1)[low - base : high - base]


def reduce_blocks(layout, pieces, small, outer, inner, role):
    count = layout.outer
    pair_x = lax.axis_index("group") % 2
    groups = lax.axis_size("group")
    finals = [None] * layout.members
    for block in reversed(range(count)):
        even, odd = 2 * block, 2 * block + 1
        received = []
        for names in (("o", "u", "d"), ("q",)):
            segments = [layout.segments(m, names) for m in (even, odd)]
            if not any(segments):
                continue
            columns = layout.piece[names[0]][1]
            sizes = [sum(b - a for _, (a, b) in s) for s in segments]
            rows = max(sizes)
            buffers = []
            for s, size in zip(segments, sizes):
                parts = [pieces[name][a:b] for name, (a, b) in s]
                if size < rows:
                    parts.append(jnp.zeros((rows - size, columns), BF16))
                buffers.append(jnp.concatenate(parts, 0) if len(parts) > 1 else parts[0])
            keep = jnp.where(inner == 0, buffers[0], buffers[1])
            send = jnp.where(inner == 0, buffers[1], buffers[0])
            total = (keep.astype(F32) + swap(send, "member").astype(F32)).astype(BF16)
            for hop in range(max(block, count - 1 - block)):
                pairs = []
                if hop < block:
                    pairs += [(2 * hop + y, 2 * hop + 2 + y) for y in range(2)]
                if hop < count - 1 - block:
                    down = 2 * (count - 1 - hop)
                    pairs += [(down + y, down - 2 + y) for y in range(2)]
                came = lax.ppermute(total, "member", pairs)
                total = (total.astype(F32) + came.astype(F32)).astype(BF16)
            step = 2
            while step < groups:
                total = (total.astype(F32) + swap(total, "group", step).astype(F32)).astype(BF16)
                step *= 2
            mate = swap(total, "group")
            across = [swap(total, "role"), swap(mate, "role")]
            by_x = [[jnp.where(pair_x == x, own, other) for x in range(2)] for own, other in ((total, mate), across)]
            quad = [[jnp.where(role == r, by_x[0][x], by_x[1][x]) for r in range(2)] for x in range(2)]
            received.append((segments, quad))
        for which, member in enumerate((even, odd)):
            found = {}
            for segments, quad in received:
                at = 0
                for name, (a, b) in segments[which]:
                    found[name] = [[quad[x][r][at : at + b - a] for r in range(2)] for x in range(2)]
                    at += b - a
            finals[member] = found
    half = layout.share // 2

    def assemble(member):
        def branch(found, small):
            parts = [layout.natural(member, name, found[member][name]).astype(F32) for name in ("q", "o", "u", "d") if name in found[member]]
            tail = layout.span(member, "s")
            if tail is not None:
                parts.append(small.reshape(-1)[tail[0] : tail[1]])
            flat = jnp.concatenate(parts)
            return lax.dynamic_slice(flat, (role * half,), (half,))

        return branch

    return lax.switch(2 * outer + inner, [assemble(m) for m in range(layout.members)], finals, small)


def attention(q, k, v, allowed):
    rows = q.shape[0]
    heads = q.shape[1] // 64
    split = lambda t: t.reshape(t.shape[0], heads, 64)
    scores = jnp.einsum("ihd,jhd->hij", split(q), split(k), preferred_element_type=F32) * 0.125
    scores = jnp.where(allowed[None], scores, -1e30)
    exponent = jnp.exp(scores - jnp.max(scores, axis=-1, keepdims=True))
    return exponent / jnp.sum(exponent, axis=-1, keepdims=True)


def local(frames, cotangent, w_qkv, w_out, w_up, w_down, gains, shifts, prompt_len, section):
    rows, width = frames.shape[2], frames.shape[3]
    ff, sections = w_up.shape[1], gains.shape[0]
    role, group, member = lax.axis_index("role"), lax.axis_index("group"), lax.axis_index("member")
    x = group % 2
    members = lax.axis_size("member")
    layout = Layout(width, ff, sections, members, members // 2)
    outer, inner = member // 2, member % 2

    def whole(own):
        other = swap(own, "role")
        return jnp.concatenate([jnp.where(role == 0, own, other), jnp.where(role == 0, other, own)], 0)

    own_frames, own_cot = frames[0, 0], cotangent[0, 0]
    inputs = [whole(own_frames), whole(swap(own_frames, "group"))]
    grads_y = [whole(own_cot), whole(swap(own_cot, "group"))]
    lengths = [prompt_len[0], swap(prompt_len, "group")[0]]
    section_ids = [section[0], swap(section, "group")[0]]

    half, quarter = width // 2, width // 4
    w_qkv_own = lax.dynamic_slice(w_qkv.reshape(width, 3, 2, 2, quarter), (0, 0, role, 0, 0), (width, 3, 1, 2, quarter))
    w_qkv_own = w_qkv_own.reshape(width, 3 * half)
    w_out_own = lax.dynamic_slice(w_out, (role * half, 0), (half, width))
    blocks = ff // (4 * LANE)
    w_up_blocks = w_up.reshape(width, blocks, 2, 2, LANE)
    w_down_blocks = w_down.reshape(blocks, 2, 2, LANE, width)

    def ff_part(x_at):
        up = lax.dynamic_slice(w_up_blocks, (0, 0, x_at, role, 0), (width, blocks, 1, 1, LANE)).reshape(width, ff // 4)
        down = lax.dynamic_slice(w_down_blocks, (0, x_at, role, 0, 0), (blocks, 1, 1, LANE, width)).reshape(ff // 4, width)
        return up, down

    position = jnp.arange(2 * rows)
    hidden_one, qkvs, probs, atts, residuals, gain_rows, shift_rows, units_one = [], [], [], [], [], [], [], []
    units_two, hidden_two, alloweds = [], [], []
    for at in range(2):
        select = (jnp.arange(sections, dtype=jnp.int32) == section_ids[at]).astype(F32)
        gain_rows.append(jnp.sum(select[:, None, None] * gains.astype(F32), 0))
        shift_rows.append(jnp.sum(select[:, None, None] * shifts.astype(F32), 0))
        values = inputs[at].astype(F32)
        unit, rstd = norm_stats(values)
        units_one.append((unit, rstd))
        h1 = (unit * gain_rows[at][0] + shift_rows[at][0]).astype(BF16)
        hidden_one.append(h1)
        qkv = mm(h1, w_qkv_own).astype(BF16)
        qkvs.append(qkv)
        allowed = jnp.where(position[None, :] < rows, position[None, :] < lengths[at], position[:, None] >= rows)
        alloweds.append(allowed)
        q, k, v = (qkv[:, i * half : (i + 1) * half] for i in range(3))
        prob = attention(q, k, v, allowed)
        probs.append(prob)
        att = jnp.einsum("hij,jhd->ihd", prob.astype(BF16), v.reshape(2 * rows, -1, 64), preferred_element_type=F32)
        att = att.reshape(2 * rows, half).astype(BF16)
        atts.append(att)
        part = mm(att, w_out_own).astype(BF16)
        residual = values + (part.astype(F32) + swap(part, "role").astype(F32))
        residuals.append(residual)
        unit, rstd = norm_stats(residual)
        units_two.append((unit, rstd))
        hidden_two.append((unit * gain_rows[at][1] + shift_rows[at][1]).astype(BF16))

    both_hidden = jnp.concatenate(hidden_two, 0)
    both_dy = jnp.concatenate(grads_y, 0)
    out_part, grad_hidden = 0.0, 0.0
    for which in range(2):
        up_w, down_w = ff_part(x ^ which)
        up = mm(both_hidden, up_w)
        cdf = 0.5 * (1.0 + lax.erf(up * np.float32(0.5**0.5)))
        act = (up * cdf).astype(BF16)
        slope = cdf + up * jnp.exp(-0.5 * up * up) * np.float32(1 / np.sqrt(2 * np.pi))
        dup = (mm_nt(both_dy, down_w) * slope).astype(BF16)
        if which == 0:
            grad_down = mm_tn(act, both_dy).astype(BF16)
            grad_up = mm_tn(both_hidden, dup).astype(BF16)
        out_part = out_part + mm(act[: 2 * rows], down_w)
        grad_hidden = grad_hidden + mm_nt(dup, up_w)

    def own_rows(value):
        return lax.dynamic_slice(value, (role * rows, 0), (rows, value.shape[1]))

    def other_rows(value):
        return lax.dynamic_slice(value, ((1 - role) * rows, 0), (rows, value.shape[1]))

    output = own_rows(residuals[0]) + (own_rows(out_part) + swap(other_rows(out_part).astype(BF16), "role").astype(F32))
    output = output.astype(BF16)

    grad_hidden = grad_hidden.astype(BF16)
    grad_hidden = grad_hidden.astype(F32) + swap(grad_hidden, "role").astype(F32)
    grad_residuals, grad_q, grad_branches = [], [], []
    for at in range(2):
        unit, rstd = units_two[at]
        dh2 = grad_hidden[2 * rows * at : 2 * rows * (at + 1)]
        if at == 0:
            own_dh2 = own_rows(dh2)
            grad_gain_two = jnp.sum(own_dh2 * own_rows(unit), 0)
            grad_shift_two = jnp.sum(own_dh2, 0)
        dr1 = grads_y[at].astype(F32) + norm_back(unit, rstd, gain_rows[at][1], dh2)
        grad_residuals.append(dr1)
        da = dr1.astype(BF16)
        grad_branches.append(da)
        datt = mm_nt(da, w_out_own).astype(BF16).reshape(2 * rows, -1, 64)
        q, k, v = (qkvs[at][:, i * half : (i + 1) * half].reshape(2 * rows, -1, 64) for i in range(3))
        prob = probs[at]
        dv = jnp.einsum("hij,ihd->jhd", prob.astype(BF16), datt, preferred_element_type=F32)
        dprob = jnp.einsum("ihd,jhd->hij", datt, v, preferred_element_type=F32)
        delta = jnp.sum(prob * dprob, axis=-1, keepdims=True)
        dscore = (prob * (dprob - delta)).astype(BF16)
        dq = jnp.einsum("hij,jhd->ihd", dscore, k, preferred_element_type=F32) * 0.125
        dk = jnp.einsum("hij,ihd->jhd", dscore, q, preferred_element_type=F32) * 0.125
        grad_q.append(jnp.concatenate([t.reshape(2 * rows, half) for t in (dq, dk, dv)], 1).astype(BF16))

    both_att = jnp.concatenate(atts, 0)
    own_att = lax.dynamic_slice(both_att, (0, x * quarter), (4 * rows, quarter))
    grad_out = mm_tn(own_att, jnp.concatenate(grad_branches, 0)).astype(BF16)
    both_dqkv = jnp.concatenate(grad_q, 0).reshape(4 * rows, 3, 2, quarter)
    own_dqkv = lax.dynamic_slice(both_dqkv, (0, 0, x, 0), (4 * rows, 3, 1, quarter)).reshape(4 * rows, 3 * quarter)
    grad_qkv = mm_tn(jnp.concatenate(hidden_one, 0), own_dqkv).astype(BF16)

    dh1_part = mm_nt(grad_q[0], w_qkv_own)
    dh1 = own_rows(dh1_part) + swap(other_rows(dh1_part).astype(BF16), "role").astype(F32)
    unit, rstd = (own_rows(t) for t in units_one[0])
    input_grad = own_rows(grad_residuals[0]) + norm_back(unit, rstd, gain_rows[0][0], dh1)

    vectors = jnp.stack([jnp.stack([jnp.sum(dh1 * unit, 0), grad_gain_two]), jnp.stack([jnp.sum(dh1, 0), grad_shift_two])])
    select = (jnp.arange(sections, dtype=jnp.int32) == section_ids[0]).astype(F32)
    small = select[None, :, None, None] * vectors[:, None]
    small = small.reshape(4 * sections, width)
    for axis in ("role", "group", "member"):
        distance = 1
        while distance < lax.axis_size(axis):
            small = small + swap(small, axis, distance)
            distance *= 2

    pieces = {"q": grad_qkv, "o": grad_out, "u": grad_up, "d": grad_down}
    shard = reduce_blocks(layout, pieces, small, outer, inner, role)
    return output[None, None], input_grad[None, None], shard


def solution(mesh):
    rows = P(("group", "member"), "role", None, None)
    per_seq = P(("group", "member"))
    return jax.shard_map(
        local,
        mesh=mesh,
        in_specs=(rows, rows, P(), P(), P(), P(), P(), P(), per_seq, per_seq),
        out_specs=(rows, rows, P(("member", "role"))),
        check_vma=False,
    )
```

```python
import functools

import jax
import jax.numpy as jnp
import numpy as np
from jax import lax
from jax.experimental import pallas as pl
from jax.experimental.pallas import tpu as pltpu
from jax.sharding import PartitionSpec as P

HEADS = 16
LANE = 128
HEAD = 64
F32 = jnp.float32
BF16 = jnp.bfloat16


def dot(left, right, dims):
    return lax.dot_general(left, right, (dims, ((), ())), preferred_element_type=F32)


def mm(left, right):
    return dot(left, right, ((1,), (0,)))


def mm_nt(left, right):
    return dot(left, right, ((1,), (1,)))


def mm_tn(left, right):
    return dot(left, right, ((0,), (0,)))


def swap(value, axis, distance=1):
    count = lax.axis_size(axis)
    return lax.ppermute(value, axis, [(i, i ^ distance) for i in range(count)])


def norm_stats(values):
    center = values - jnp.mean(values, axis=-1, keepdims=True)
    rstd = lax.rsqrt(jnp.mean(center * center, axis=-1, keepdims=True) + 1e-05)
    return center * rstd, rstd


def norm_back(unit, rstd, gain, grad):
    grad_unit = grad * gain
    inner = grad_unit - jnp.mean(grad_unit, axis=-1, keepdims=True)
    return rstd * (inner - unit * jnp.mean(grad_unit * unit, axis=-1, keepdims=True))


def full(shape, dtype):
    return jax.ShapeDtypeStruct(shape, dtype)


def params(mib):
    return pltpu.CompilerParams(vmem_limit_bytes=mib * 2**20)


def cost(flops, moved):
    return pl.CostEstimate(flops=int(flops), bytes_accessed=int(moved), transcendentals=0)


HBM = pl.BlockSpec(memory_space=pl.ANY)
SMEM = pl.BlockSpec(memory_space=pltpu.SMEM)
VMEM = pl.BlockSpec(memory_space=pltpu.VMEM)


def copy_all(pairs, sems):
    copies = [pltpu.make_async_copy(source, target, sems.at[i]) for i, (source, target) in enumerate(pairs)]
    for each in copies:
        each.start()
    return copies


def head_masks(dtype, scale):
    lane = lax.broadcasted_iota(jnp.int32, (1, LANE), 1)
    return [jnp.where(lane // HEAD == h, scale, 0.0).astype(dtype) for h in range(2)]


def live_scores(key, query, length):
    scores = mm_nt(key, query)
    return jnp.where(lax.broadcasted_iota(jnp.int32, scores.shape, 0) < length, scores, -1e30)


def attend_kernel(scalars, x_ref, gs_ref, w_qkv, w_out, ht_ref, qkv_ref, att_ref, part_ref, lse_ref, w_buf, o_buf, h_buf, sems):
    role, length = scalars[0], scalars[1]
    width, half = w_out.shape[1], w_out.shape[0] // 2
    rows = x_ref.shape[0] // 2
    col = pl.multiple_of(role * half, LANE)
    copies = copy_all(
        [(w_qkv.at[:, pl.ds(i * width + col, half)], w_buf.at[:, pl.ds(i * half, half)]) for i in range(3)]
        + [(w_out.at[pl.ds(col, half), :], o_buf)],
        sems,
    )
    for at in range(0, 2 * rows, LANE):
        unit, _ = norm_stats(x_ref[at : at + LANE, :].astype(F32))
        hidden = (unit * gs_ref[0:1, :] + gs_ref[1:2, :]).astype(BF16)
        h_buf[at : at + LANE, :] = hidden
        ht_ref[:, at : at + LANE] = hidden.T
    for i in range(3):
        copies[i].wait()
        qkv_ref[:, i * half : (i + 1) * half] = mm(h_buf[...], w_buf[:, i * half : (i + 1) * half]).astype(BF16)

    def pair(at, carry):
        c = pl.multiple_of(at * LANE, LANE)
        q, k, v = (qkv_ref[:, pl.ds(i * half + c, LANE)] for i in range(3))
        q_masks, v_masks = head_masks(BF16, 0.125), head_masks(BF16, 1.0)
        for group in range(2):
            total = 0.0
            for h in range(2):
                query = q[group * rows : (group + 1) * rows] * q_masks[h]
                scores = [live_scores(k[:rows], query, length)]
                if group:
                    scores.append(mm_nt(k[rows:], query))
                top = jnp.max(scores[0], axis=0, keepdims=True)
                if group:
                    top = jnp.maximum(top, jnp.max(scores[1], axis=0, keepdims=True))
                powers = [jnp.exp(s - top) for s in scores]
                below = sum(jnp.sum(p, axis=0, keepdims=True) for p in powers)
                lse_ref[pl.ds(2 * at + h, 1), group * rows : (group + 1) * rows] = top + jnp.log(below)
                inverse = 1.0 / below
                for which, p in enumerate(powers):
                    prob = (p * inverse).astype(BF16)
                    total = total + mm_tn(prob, v[which * rows : (which + 1) * rows] * v_masks[h])
            att_ref[group * rows : (group + 1) * rows, pl.ds(c, LANE)] = total.astype(BF16)
        return carry

    lax.fori_loop(0, half // LANE, pair, 0)
    copies[3].wait()
    part_ref[...] = mm(att_ref[...], o_buf[...]).astype(BF16)


def attend(scalars, values, gs, w_qkv, w_out):
    rows, width = values.shape
    half = width // 2
    return pl.pallas_call(
        attend_kernel,
        in_specs=[SMEM, VMEM, VMEM, HBM, HBM],
        out_specs=[VMEM] * 5,
        out_shape=[full((width, rows), BF16), full((rows, 3 * half), BF16), full((rows, half), BF16), full((rows, width), BF16), full((half // HEAD, rows), F32)],
        scratch_shapes=[pltpu.VMEM((width, 3 * half), BF16), pltpu.VMEM((half, width), BF16), pltpu.VMEM((rows, width), BF16), pltpu.SemaphoreType.DMA((4,))],
        compiler_params=params(48),
        cost_estimate=cost(2 * rows * width * 4 * half * 2, 12e6),
        name="attend",
    )(scalars, values, gs, w_qkv, w_out)


def unit_copies(w_up, w_down, up_buf, down_buf, first):
    blocks = w_up.shape[1] // (4 * LANE)
    pairs = []
    for b in range(blocks):
        at = pl.multiple_of((4 * b + first) * LANE, LANE)
        pairs.append((w_up.at[:, pl.ds(at, LANE)], up_buf.at[:, pl.ds(b * LANE, LANE)]))
    for b in range(blocks):
        at = pl.multiple_of((4 * b + first) * LANE, LANE)
        pairs.append((w_down.at[pl.ds(at, LANE), :], down_buf.at[pl.ds(b * LANE, LANE), :]))
    return pairs


def gelu_parts(up):
    cdf = 0.5 + 0.5 * lax.erf(up * np.float32(0.5**0.5))
    slope = cdf + up * (jnp.exp(-0.5 * up * up) * np.float32(1 / np.sqrt(2 * np.pi)))
    return up * cdf, slope


def own_kernel(scalars, xa, xb, pa, ra, pb, rb, dya, dyb, gs_ref, w_up, w_down,
               h_ref, gd_ref, gu_ref, act_ref, dup_ref, res_ref,
               x_buf, p_buf, r_buf, dy_buf, up_buf, down_buf, ht_buf, sems):
    role, x = scalars[0], scalars[2]
    rows = xa.shape[0]
    quarter = up_buf.shape[1]
    copies = copy_all(
        [(s, t.at[pl.ds(u * rows, rows), :]) for u, trio in enumerate(((xa, pa, ra), (xb, pb, rb))) for s, t in zip(trio, (x_buf, p_buf, r_buf))]
        + unit_copies(w_up, w_down, up_buf, down_buf, role + 2 * x)
        + [(dya, dy_buf.at[pl.ds(0, rows), :]), (dyb, dy_buf.at[pl.ds(rows, rows), :])],
        sems,
    )
    for u in range(2):
        for i in range(3):
            copies[3 * u + i].wait()

        def norm(i, carry):
            at = pl.multiple_of(u * rows + i * LANE, LANE)
            here = pl.ds(at, LANE)
            residual = x_buf[here, :].astype(F32) + (p_buf[here, :].astype(F32) + r_buf[here, :].astype(F32))
            unit, _ = norm_stats(residual)
            hidden = (unit * gs_ref[u, 2:3, :] + gs_ref[u, 3:4, :]).astype(BF16)
            h_ref[here, :] = hidden
            ht_buf[:, here] = hidden.T
            if u == 0:
                @pl.when(i // (rows // LANE // 2) == role)
                def _():
                    res_ref[pl.ds(pl.multiple_of((i % (rows // LANE // 2)) * LANE, LANE), LANE), :] = residual
            return carry

        lax.fori_loop(0, rows // LANE, norm, 0)
    for each in copies[6:]:
        each.wait()

    def block(i, carry):
        cols = pl.ds(pl.multiple_of(i * 256, 256), 256)
        act, slope = gelu_parts(mm(h_ref[...], up_buf[:, cols]))
        act = act.astype(BF16)
        act_ref[:, cols] = act[:rows]
        dup = (mm_nt(dy_buf[...], down_buf[cols, :]) * slope).astype(BF16)
        dup_ref[:, cols] = dup
        gd_ref[cols, :] = mm_tn(act, dy_buf[...]).astype(BF16)
        gu_ref[:, cols] = mm(ht_buf[...], dup).astype(BF16)
        return carry

    lax.fori_loop(0, quarter // 256, block, 0)


def own_units(scalars, values, parts, came, dys, gs, w_up, w_down):
    rows, width = values[0].shape
    quarter = w_up.shape[1] // 4
    count = 6 + 2 * (quarter // LANE) + 2
    big = lambda *s: pltpu.VMEM(s, BF16)
    return pl.pallas_call(
        own_kernel,
        in_specs=[SMEM] + [HBM] * 8 + [VMEM] + [HBM] * 2,
        out_specs=[VMEM] * 6,
        out_shape=[full((2 * rows, width), BF16), full((quarter, width), BF16), full((width, quarter), BF16), full((rows, quarter), BF16), full((2 * rows, quarter), BF16), full((rows // 2, width), F32)],
        scratch_shapes=[big(2 * rows, width)] * 4 + [big(width, quarter), big(quarter, width), big(width, 2 * rows), pltpu.SemaphoreType.DMA((count,))],
        compiler_params=params(56),
        cost_estimate=cost(2 * 2 * rows * width * quarter * 4, 20e6),
        name="own_units",
    )(scalars, values[0], values[1], parts[0], came[0], parts[1], came[1], dys[0], dys[1], gs, w_up, w_down)


def rest_kernel(scalars, h_any, dya, dyb, act_any, dup_any, res_ref, w_up, w_down, dh_ref, keep_ref, send_ref,
                h_buf, dy_buf, act_own, act_buf, dup_own, dup_buf, up_own, down_own, up_buf, down_buf, sems):
    role, x = scalars[0], scalars[2]
    rows = dya.shape[0]
    quarter = up_buf.shape[1]
    blocks = quarter // LANE
    copies = copy_all(
        [(h_any, h_buf)]
        + unit_copies(w_up, w_down, up_buf, down_buf, role + 2 * (1 - x))
        + [(dya, dy_buf.at[pl.ds(0, rows), :]), (dyb, dy_buf.at[pl.ds(rows, rows), :]), (act_any, act_own), (dup_any, dup_own)]
        + unit_copies(w_up, w_down, up_own, down_own, role + 2 * x),
        sems,
    )
    first = 1 + 2 * blocks + 2
    for each in copies[:first]:
        each.wait()

    def block(i, carry):
        cols = pl.ds(pl.multiple_of(i * 256, 256), 256)
        act, slope = gelu_parts(mm(h_buf[...], up_buf[:, cols]))
        act_buf[:, cols] = act[:rows].astype(BF16)
        dup_buf[:, cols] = (mm_nt(dy_buf[...], down_buf[cols, :]) * slope).astype(BF16)
        return carry

    lax.fori_loop(0, quarter // 256, block, 0)
    for each in copies[first:]:
        each.wait()

    def back(i, carry):
        here = pl.ds(pl.multiple_of(i * 256, 256), 256)
        dh_ref[here, :] = (mm_nt(dup_own[here, :], up_own[...]) + mm_nt(dup_buf[here, :], up_buf[...])).astype(BF16)
        return carry

    lax.fori_loop(0, 2 * rows // 256, back, 0)
    keep = pl.ds(pl.multiple_of(role * (rows // 2), rows // 2), rows // 2)
    send = pl.ds(pl.multiple_of((1 - role) * (rows // 2), rows // 2), rows // 2)
    keep_ref[...] = res_ref[...] + (mm(act_own[keep, :], down_own[...]) + mm(act_buf[keep, :], down_buf[...]))
    send_ref[...] = (mm(act_own[send, :], down_own[...]) + mm(act_buf[send, :], down_buf[...])).astype(BF16)


def rest_units(scalars, hidden, dys, act, dup, residual, w_up, w_down):
    rows, width = dys[0].shape
    quarter = w_up.shape[1] // 4
    count = 5 + 4 * (quarter // LANE)
    big = lambda *s: pltpu.VMEM(s, BF16)
    return pl.pallas_call(
        rest_kernel,
        in_specs=[SMEM] + [HBM] * 5 + [VMEM] + [HBM] * 2,
        out_specs=[VMEM] * 3,
        out_shape=[full((2 * rows, width), BF16), full((rows // 2, width), F32), full((rows // 2, width), BF16)],
        scratch_shapes=[big(2 * rows, width)] * 2 + [big(rows, quarter)] * 2 + [big(2 * rows, quarter)] * 2 + [big(width, quarter), big(quarter, width)] * 2 + [pltpu.SemaphoreType.DMA((count,))],
        compiler_params=params(56),
        cost_estimate=cost(2 * 2 * rows * width * quarter * 5, 24e6),
        name="rest_units",
    )(scalars, hidden, dys[0], dys[1], act, dup, residual, w_up, w_down)


def pair_back(qkv, lse, datt, c, c_d, rows, half, length):
    q, k, v = (qkv[:, pl.ds(i * half + c, LANE)] for i in range(3))
    grad = datt[:, pl.ds(c_d, LANE)]
    scaled, plain = head_masks(BF16, 0.125), head_masks(BF16, 1.0)
    dq = []
    dk, dv = [0.0, 0.0], [0.0, 0.0]
    for group in range(2):
        here = slice(group * rows, (group + 1) * rows)
        dq_here = 0.0
        for h in range(2):
            query, above = q[here] * scaled[h], grad[here] * plain[h]
            log_total = lse(h, here)
            probs, dprobs = [], []
            delta = 0.0
            for which in range(group + 1):
                there = slice(which * rows, (which + 1) * rows)
                scores = live_scores(k[there], query, length) if which == 0 else mm_nt(k[there], query)
                prob = jnp.exp(scores - log_total)
                dprob = mm_nt(v[there], above)
                delta = delta + jnp.sum(prob * dprob, axis=0, keepdims=True)
                dv[which] = dv[which] + mm(prob.astype(BF16), above)
                probs.append(prob)
                dprobs.append(dprob)
            for which in range(group + 1):
                there = slice(which * rows, (which + 1) * rows)
                dscore = (probs[which] * (dprobs[which] - delta)).astype(BF16)
                dk[which] = dk[which] + mm(dscore, query)
                dq_here = dq_here + mm_tn(dscore, k[there] * scaled[h])
        dq.append(dq_here)
    return dq, dk, dv


def back_kernel(scalars, xa, xb, pa, ra, pb, rb, dh_any, dhr_any, dya, dyb, gs_ref, w_out, att_a, att_b, qkv_a, qkv_b, lse_a, lse_b, ht_a, ht_b,
                gq_ref, go_ref, dr_ref, vec_ref, datt_ref, dqa_ref,
                x_buf, p_buf, r_buf, dh_buf, dhr_buf, dy_buf, da_buf, o_buf, datt_buf, att_buf, qkv_buf, ht_buf, dq_buf, sems):
    role, x = scalars[0], scalars[2]
    rows2, width = xa.shape
    rows, half = rows2 // 2, width // 2
    quarter = half // 2
    own = pl.multiple_of(x * quarter, LANE)
    col = pl.multiple_of(role * half, LANE)
    lse = (lse_a, lse_b)
    pairs = []
    for u, (xs, ps, rs, dys) in enumerate(((xa, pa, ra, dya), (xb, pb, rb, dyb))):
        here = pl.ds(u * rows2, rows2)
        pairs += [(xs, x_buf.at[here, :]), (ps, p_buf.at[here, :]), (rs, r_buf.at[here, :]), (dys, dy_buf.at[here, :]),
                  (dh_any.at[here, :], dh_buf.at[here, :]), (dhr_any.at[here, :], dhr_buf.at[here, :])]
    pairs.append((w_out.at[pl.ds(col, half), :], o_buf))
    for u, (a, q, h) in enumerate(((att_a, qkv_a, ht_a), (att_b, qkv_b, ht_b))):
        here = pl.ds(u * rows2, rows2)
        pairs += [(q, qkv_buf.at[here, :]), (a.at[:, pl.ds(own, quarter)], att_buf.at[here, :]), (h, ht_buf.at[:, here])]
    copies = copy_all(pairs, sems)
    vec_ref[...] = jnp.zeros_like(vec_ref)
    for u in range(2):
        for i in range(6):
            copies[6 * u + i].wait()

        def norm(i, carry):
            here = pl.ds(pl.multiple_of(u * rows2 + i * LANE, LANE), LANE)
            residual = x_buf[here, :].astype(F32) + (p_buf[here, :].astype(F32) + r_buf[here, :].astype(F32))
            unit, rstd = norm_stats(residual)
            dh2 = dh_buf[here, :].astype(F32) + dhr_buf[here, :].astype(F32)
            grad = dy_buf[here, :].astype(F32) + norm_back(unit, rstd, gs_ref[u, 2:3, :], dh2)
            da_buf[here, :] = grad.astype(BF16)
            if u == 0:
                per = rows // LANE
                @pl.when(i // per == role)
                def _():
                    dr_ref[pl.ds(pl.multiple_of((i % per) * LANE, LANE), LANE), :] = grad
                    vec_ref[0:1, :] += jnp.sum(dh2 * unit, axis=0, keepdims=True)
                    vec_ref[1:2, :] += jnp.sum(dh2, axis=0, keepdims=True)
            return carry

        lax.fori_loop(0, rows2 // LANE, norm, 0)
        if u == 0:
            copies[12].wait()
            datt_buf[:rows2, :] = mm_nt(da_buf[:rows2, :], o_buf[...]).astype(BF16)
            datt_ref[...] = datt_buf[:rows2, :]
        else:
            mine = o_buf[pl.ds(pl.multiple_of(x * quarter, quarter), quarter), :]
            datt_buf[rows2:, pl.ds(own, quarter)] = mm_nt(da_buf[rows2:, :], mine).astype(BF16)
    for each in copies[13:]:
        each.wait()
    go_ref[...] = mm_tn(att_buf[...], da_buf[...]).astype(BF16)
    for u in range(2):
        base = u * rows2
        length = scalars[1] if u == 0 else scalars[3]

        def one(at, carry):
            c = pl.multiple_of(own + at * LANE, LANE)
            to = pl.multiple_of(at * LANE, LANE)
            first = (own + at * LANE) // HEAD
            look = lambda h, here: lse[u][pl.ds(first + h, 1), here]
            dq, dk, dv = pair_back(qkv_buf.at[pl.ds(base, rows2), :], look, datt_buf.at[pl.ds(base, rows2), :], c, c, rows, half, length)
            for i, halves in enumerate((dq, dk, dv)):
                for g in range(2):
                    dq_buf[base + g * rows : base + (g + 1) * rows, pl.ds(i * quarter + to, LANE)] = halves[g].astype(BF16)
            return carry

        lax.fori_loop(0, quarter // LANE, one, 0)
    dqa_ref[...] = dq_buf[:rows2, :]
    for i in range(3):
        cols = slice(i * quarter, (i + 1) * quarter)
        gq_ref[:, cols] = mm(ht_buf[...], dq_buf[:, cols]).astype(BF16)


def back(scalars, values, parts, came, dh, dh_came, dys, gs, w_out, atts, qkvs, lses, hts):
    rows2, width = values[0].shape
    half = width // 2
    big = lambda *s: pltpu.VMEM(s, BF16)
    tokens = 2 * rows2
    return pl.pallas_call(
        back_kernel,
        in_specs=[SMEM] + [HBM] * 10 + [VMEM] + [HBM] * 5 + [VMEM] * 2 + [HBM] * 2,
        out_specs=[VMEM] * 6,
        out_shape=[full((width, 3 * half // 2), BF16), full((half // 2, width), BF16), full((rows2 // 2, width), F32), full((8, width), F32), full((rows2, half), BF16), full((rows2, 3 * half // 2), BF16)],
        scratch_shapes=[big(tokens, width)] * 7 + [big(half, width), big(tokens, half), big(tokens, half // 2), big(tokens, 3 * half), big(width, tokens), big(tokens, 3 * half // 2), pltpu.SemaphoreType.DMA((19,))],
        compiler_params=params(56),
        cost_estimate=cost(15e9, 24e6),
        name="back",
    )(scalars, values[0], values[1], parts[0], came[0], parts[1], came[1], dh, dh_came, dys[0], dys[1], gs, w_out, atts[0], atts[1], qkvs[0], qkvs[1], lses[0], lses[1], hts[0], hts[1])


def last_kernel(scalars, qkv_ref, lse_ref, datt_ref, dqa_ref, w_qkv, keep_ref, send_ref, w_own, w_buf, dq_buf, sems):
    role, x, length = scalars[0], scalars[2], scalars[1]
    rows2, half = datt_ref.shape
    rows, quarter, width = rows2 // 2, half // 2, 2 * half
    mine = pl.multiple_of(x * quarter, LANE)
    other = pl.multiple_of((1 - x) * quarter, LANE)
    col = pl.multiple_of(role * half, LANE)
    copies = copy_all(
        [(w_qkv.at[:, pl.ds(i * width + col + from_, quarter)], to.at[:, pl.ds(i * quarter, quarter)]) for from_, to in ((mine, w_own), (other, w_buf)) for i in range(3)],
        sems,
    )

    def one(at, carry):
        c = pl.multiple_of(other + at * LANE, LANE)
        to = pl.multiple_of(at * LANE, LANE)
        first = (other + at * LANE) // HEAD
        look = lambda h, here: lse_ref[pl.ds(first + h, 1), here]
        dq, dk, dv = pair_back(qkv_ref, look, datt_ref, c, c, rows, half, length)
        for i, halves in enumerate((dq, dk, dv)):
            for g in range(2):
                dq_buf[g * rows : (g + 1) * rows, pl.ds(i * quarter + to, LANE)] = halves[g].astype(BF16)
        return carry

    lax.fori_loop(0, quarter // LANE, one, 0)
    for each in copies:
        each.wait()
    keep = pl.ds(pl.multiple_of(role * rows, rows), rows)
    send = pl.ds(pl.multiple_of((1 - role) * rows, rows), rows)
    keep_ref[...] = mm_nt(dqa_ref[keep, :], w_own[...]) + mm_nt(dq_buf[keep, :], w_buf[...])
    send_ref[...] = (mm_nt(dqa_ref[send, :], w_own[...]) + mm_nt(dq_buf[send, :], w_buf[...])).astype(BF16)


def last(scalars, qkv, lse, datt, dqa, w_qkv):
    rows2, half = datt.shape
    width = 2 * half
    big = lambda *s: pltpu.VMEM(s, BF16)
    return pl.pallas_call(
        last_kernel,
        in_specs=[SMEM] + [VMEM] * 4 + [HBM],
        out_specs=[VMEM] * 2,
        out_shape=[full((rows2 // 2, width), F32), full((rows2 // 2, width), BF16)],
        scratch_shapes=[big(width, 3 * half // 2)] * 2 + [big(rows2, 3 * half // 2), pltpu.SemaphoreType.DMA((6,))],
        compiler_params=params(48),
        cost_estimate=cost(5e9, 10e6),
        name="last",
    )(scalars, qkv, lse, datt, dqa, w_qkv)


class Layout:
    def __init__(self, width, ff, sections, members):
        self.width, self.ff, self.members = width, ff, members
        shapes = {"q": (width, 3 * width), "o": (width, width), "u": (width, ff), "d": (ff, width), "s": (4 * sections, width)}
        start, self.spans = 0, {}
        for name, (rows, columns) in shapes.items():
            self.spans[name] = (start, rows, columns)
            start += rows * columns
        self.total = start
        self.share = start // members
        self.segments = [self.parts_of(m) for m in range(members)]
        self.rows = max(s[-1]["at"] + s[-1]["wire"] for s in self.segments)

    def span(self, member, name):
        start, rows, columns = self.spans[name]
        low = max(member * self.share, start) - start
        high = min((member + 1) * self.share, start + rows * columns) - start
        return (low, high) if low < high else None

    def parts_of(self, member):
        parts, at = [], 0
        for name in ("q", "o", "u", "d"):
            found = self.span(member, name)
            if found is None:
                continue
            columns = self.spans[name][2]
            low, high = found[0] // columns, -(-found[1] // columns)
            if name == "o":
                held = [r % (self.width // 4) for r in range(low, high)]
                low, high = min(held), max(held) + 1
            if name == "d":
                held = [r // (4 * LANE) * LANE + r % LANE for r in range(low, high)]
                low, high = min(held), max(held) + 1
            low, high = low // 16 * 16, -(-high // 16) * 16
            count = high - low
            wire = -(-(3 * count // 4) // 16) * 16 if name == "q" else count
            parts.append({"name": name, "low": low, "high": high, "at": at, "wire": wire})
            at += wire
        return parts

    def table(self):
        rows = []
        for share in range(2 * self.members):
            entry = [share * (self.share // 2) // LANE]
            held = {p["name"]: p for p in self.segments[share // 2]}
            for name in ("q", "o", "u", "d"):
                p = held.get(name)
                entry += [p["low"], p["high"], p["at"], p["wire"]] if p else [0, 0, 0, 0]
            rows.append(entry + [0] * (24 - len(entry)))
        return np.asarray(rows, np.int32)

    def wire(self, member, pieces):
        out = []
        for p in self.segments[member]:
            piece = pieces[p["name"]][p["low"] : p["high"]]
            if p["name"] == "q":
                n1 = p["wire"]
                n2 = p["high"] - p["low"] - n1
                quarter = piece.shape[1] // 3
                side = [piece[n1:, i * quarter : (i + 1) * quarter] for i in range(3)]
                if n1 > 3 * n2:
                    side.append(jnp.zeros((n1 - 3 * n2, quarter), BF16))
                piece = jnp.concatenate([piece[:n1], jnp.concatenate(side, 0)], 1)
            out.append(piece)
        short = self.rows - sum(o.shape[0] for o in out)
        if short:
            out.append(jnp.zeros((short, self.width), BF16))
        return jnp.concatenate(out, 0) if len(out) > 1 else out[0]


def after(value, *first):
    return lax.optimization_barrier((value, *first))[0]


def add(left, right):
    return (left.astype(F32) + right.astype(F32)).astype(BF16)


def tree_pairs(block, level, count):
    size = 2 << level
    pairs = []
    for low in range(0, count, size):
        middle, high = low + size // 2, low + size
        left, right = min(max(block, low), middle - 1), min(max(block, middle), high - 1)
        source, target = (right, left) if block < middle else (left, right)
        pairs += [(2 * source + y, 2 * target + y) for y in range(2)]
    return pairs


def place_kernel(spans, table, own, mate, across, diagonal, small_ref, out_ref, wire, flat, sems):
    me, unit0 = table[24], table[0]
    units = out_ref.shape[0]
    width = wire.shape[2]
    chunks = width // LANE
    front = 512
    x, role = me // 2, me % 2
    where = (me, role + 2 * (1 - x), (1 - role) + 2 * x, (1 - role) + 2 * (1 - x))
    copies = copy_all([(source, wire.at[at]) for source, at in zip((own, mate, across, diagonal), where)], sems.at[pl.ds(0, 4)])
    for each in copies:
        each.wait()

    def rows_of(name, per_row):
        at = 1 + 4 * "qoud".index(name)
        low, high = table[at], table[at + 1]
        base = unit0 - spans[name][0] // LANE
        first = jnp.maximum(low // 16, jnp.maximum(base, 0) // per_row // 16)
        last = jnp.minimum(high // 16, (jnp.maximum(base + units, 0) + per_row * 16 - 1) // (per_row * 16))
        return low, first, last, table[at + 2], table[at + 3], base

    low, first, last, at, n1, base = rows_of("q", 3 * chunks)
    n2 = table[2] - table[1] - n1

    def qkv(g, carry):
        row = g * 16 - low
        to = front + g * 16 * 3 * chunks - base
        beside = row >= n1
        half = chunks // 4
        for section in range(3):
            source = jnp.where(beside, at + section * n2 + row - n1, at + row)
            for h in range(half):
                column = pl.multiple_of(jnp.where(beside, 3 * width // 4 + h * LANE, section * (width // 4) + h * LANE), LANE)
                for piece in range(4):
                    unit = section * chunks + (piece % 2) * (chunks // 2) + (piece // 2) * half + h
                    flat[pl.ds(to + unit, 16, stride=3 * chunks), :] = wire[piece, pl.ds(pl.multiple_of(source, 16), 16), pl.ds(column, LANE)].astype(F32)
        return carry

    lax.fori_loop(first, jnp.maximum(first, last), qkv, 0)
    per = spans["u"][2] // LANE
    low, first, last, at, _, base = rows_of("u", per)

    def up(g, carry):
        source = pl.multiple_of(at + g * 16 - low, 16)
        to = front + g * 16 * per - base
        for h in range(chunks):
            for piece in range(4):
                flat[pl.ds(to + 4 * h + piece, 16, stride=per), :] = wire[piece, pl.ds(source, 16), h * LANE : (h + 1) * LANE].astype(F32)
        return carry

    lax.fori_loop(first, jnp.maximum(first, last), up, 0)

    for name in ("o", "d"):
        slot = 1 + 4 * "qoud".index(name)
        low, high, at = table[slot], table[slot + 1], table[slot + 2]
        base = unit0 - spans[name][0] // LANE

        def rows(g, carry):
            row = g * 16
            source = pl.multiple_of(at + row - low, 16)
            for piece in range(4):
                if name == "o":
                    line = (piece % 2) * (width // 2) + (piece // 2) * (width // 4) + row
                else:
                    line = (row // LANE) * (4 * LANE) + piece * LANE + row % LANE
                to = line * chunks - base

                @pl.when((to + 16 * chunks > 0) & (to < units))
                def _():
                    for h in range(chunks):
                        flat[pl.ds(front + to + h, 16, stride=chunks), :] = wire[piece, pl.ds(source, 16), h * LANE : (h + 1) * LANE].astype(F32)

            return carry

        lax.fori_loop(low // 16, high // 16, rows, 0)

    tail = spans["s"][0] // LANE - unit0

    @pl.when(tail < units)
    def _():
        for g in range(small_ref.shape[0] // 8):
            for h in range(chunks):
                flat[pl.ds(front + tail + g * 8 * chunks + h, 8, stride=chunks), :] = small_ref[g * 8 : (g + 1) * 8, h * LANE : (h + 1) * LANE]

    done = pltpu.make_async_copy(flat.at[pl.ds(front, units), :], out_ref, sems.at[4])
    done.start()
    done.wait()


def place(layout, table, quad, small):
    rows, width = quad[0].shape
    units = layout.share // 2 // LANE
    return pl.pallas_call(
        functools.partial(place_kernel, layout.spans),
        in_specs=[SMEM] + [HBM] * 4 + [VMEM],
        out_specs=HBM,
        out_shape=full((units, LANE), F32),
        scratch_shapes=[pltpu.VMEM((4, rows, width), BF16), pltpu.VMEM((-(-units // 8) * 8 + 1024, LANE), F32), pltpu.SemaphoreType.DMA((5,))],
        compiler_params=params(32),
        cost_estimate=cost(0, 12e6),
        name="place",
    )(table, *quad, small)


def local(frames, cotangent, w_qkv, w_out, w_up, w_down, gains, shifts, prompt_len, section):
    rows, width = frames.shape[2], frames.shape[3]
    ff, sections = w_up.shape[1], gains.shape[0]
    role, group, member = lax.axis_index("role"), lax.axis_index("group"), lax.axis_index("member")
    x = group % 2
    members, groups = lax.axis_size("member"), lax.axis_size("group")
    layout = Layout(width, ff, sections, members)
    outer, inner = member // 2, member % 2
    count = members // 2

    def whole(own):
        other = swap(own, "role")
        return jnp.concatenate([jnp.where(role == 0, own, other), jnp.where(role == 0, other, own)], 0)

    own_frames, own_cot = frames[0, 0], cotangent[0, 0]
    values = [whole(own_frames), whole(swap(own_frames, "group"))]
    dys = [whole(own_cot), whole(swap(own_cot, "group"))]
    lengths = [prompt_len[0], swap(prompt_len, "group")[0]]
    section_ids = [section[0], swap(section, "group")[0]]

    def rows_of(table, at):
        return lax.dynamic_slice(table, (at, 0, 0), (1, 2, width))[0].astype(F32)

    gs = []
    for at in section_ids:
        gain, shift = rows_of(gains, at), rows_of(shifts, at)
        gs.append(jnp.stack([gain[0], shift[0], gain[1], shift[1]]))
    both_gs = jnp.stack(gs)
    scalars = jnp.stack([role, lengths[0], x, lengths[1]]).astype(jnp.int32)
    scalars_b = jnp.stack([role, lengths[1], x, lengths[0]]).astype(jnp.int32)

    totals, pieces = {}, {}
    early, late = [], []
    for block in reversed(range(count)):
        names = {p["name"] for m in (2 * block, 2 * block + 1) for p in layout.segments[m]}
        (early if names <= {"u", "d"} else late).append(block)
    halves = lambda value: [value[: layout.rows // 32 * 16], value[layout.rows // 32 * 16 :]]
    sent = []

    def exchange(block, cut):
        even, odd = layout.wire(2 * block, pieces), layout.wire(2 * block + 1, pieces)
        keep = jnp.where(inner == 0, even, odd)
        send = jnp.where(inner == 0, odd, even)
        totals[block] = []
        for k, s in zip(cut(keep), cut(send)):
            if sent:
                s = after(s, sent[-1])
            sent.append(swap(s, "member"))
            totals[block].append(add(k, sent[-1]))

    levels = count.bit_length() - 1

    def climb(block, level):
        totals[block] = [add(t, lax.ppermute(t, "member", tree_pairs(block, level, count))) for t in totals[block]]

    hts, qkvs, atts, parts, lses = zip(*(attend(s, v, g, w_qkv, w_out) for s, v, g in zip((scalars, scalars_b), values, gs)))
    came = [swap(part, "role") for part in parts]
    hidden, pieces["d"], pieces["u"], act, dup, residual = own_units(scalars, values, parts, came, dys, both_gs, w_up, w_down)
    for block in early:
        exchange(block, lambda value: [value])
    dh, out_keep, out_send = rest_units(scalars, hidden, dys, act, dup, residual, w_up, w_down)
    output = (out_keep + swap(out_send, "role").astype(F32)).astype(BF16)
    dh_came = swap(dh, "role")
    if early:
        dh_came = after(dh_came, *totals[early[0]])
    pieces["q"], pieces["o"], dr1, vec_two, datt, dqa = back(scalars, values, parts, came, dh, dh_came, dys, both_gs, w_out, atts, qkvs, lses, hts)
    for block in late:
        exchange(block, halves)
    if early:
        climb(early[0], 0)
        datt = after(datt, *totals[early[0]], *totals[early[1 % len(early)]])
    dh1_keep, dh1_send = last(scalars, qkvs[0], lses[0], datt, dqa, w_qkv)
    dh1 = dh1_keep + swap(dh1_send, "role").astype(F32)
    unit, rstd = norm_stats(own_frames.astype(F32))
    input_grad = dr1 + norm_back(unit, rstd, gs[0][0:1], dh1)

    vectors = jnp.stack([jnp.stack([jnp.sum(dh1 * unit, 0), vec_two[0]]), jnp.stack([jnp.sum(dh1, 0), vec_two[1]])])
    select = (jnp.arange(sections, dtype=jnp.int32) == section_ids[0]).astype(F32)
    small = select[None, :, None, None] * vectors[:, None]
    small = jnp.pad(small.reshape(4 * sections, width), ((0, -4 * sections % 8), (0, 0)))
    for axis in ("role", "group", "member"):
        distance = 1
        while distance < lax.axis_size(axis):
            small = small + swap(small, axis, distance)
            distance *= 2

    for block in early + late:
        for level in range(1 if early and block == early[0] else 0, levels):
            climb(block, level)
    finals = None
    for block in early + late:
        here = totals[block] if len(totals[block]) == 2 else halves(totals[block][0])
        finals = here if finals is None else [jnp.where(outer == block, h, f) for h, f in zip(here, finals)]
    distance = 2
    while distance < groups:
        finals = [add(f, swap(f, "group", distance)) for f in finals]
        distance *= 2
    mates = [swap(f, "group") for f in finals]
    own, mate = jnp.concatenate(finals, 0), jnp.concatenate(mates, 0)
    quad = [own, mate, swap(own, "role"), swap(mate, "role")]
    table = lax.dynamic_slice(jnp.asarray(layout.table()), (2 * member + role, 0), (1, 24))[0]
    table = jnp.concatenate([table, (role + 2 * x)[None].astype(jnp.int32), jnp.zeros((7,), jnp.int32)])
    shard = place(layout, table, quad, small).reshape(-1)
    return output[None, None], input_grad[None, None], shard


def solution(mesh):
    rows = P(("group", "member"), "role", None, None)
    per_seq = P(("group", "member"))
    return jax.shard_map(
        local,
        mesh=mesh,
        in_specs=(rows, rows, P(), P(), P(), P(), P(), P(), per_seq, per_seq),
        out_specs=(rows, rows, P(("member", "role"))),
        check_vma=False,
    )
```

```python
import functools

import jax
import jax.numpy as jnp
import numpy as np
from jax import lax
from jax.experimental import pallas as pl
from jax.experimental.pallas import tpu as pltpu
from jax.sharding import PartitionSpec as P

HEADS = 16
LANE = 128
HEAD = 64
F32 = jnp.float32
BF16 = jnp.bfloat16


def dot(left, right, dims):
    return lax.dot_general(left, right, (dims, ((), ())), preferred_element_type=F32)


def mm(left, right):
    return dot(left, right, ((1,), (0,)))


def mm_nt(left, right):
    return dot(left, right, ((1,), (1,)))


def mm_tn(left, right):
    return dot(left, right, ((0,), (0,)))


def swap(value, axis, distance=1):
    count = lax.axis_size(axis)
    return lax.ppermute(value, axis, [(i, i ^ distance) for i in range(count)])


def norm_stats(values):
    center = values - jnp.mean(values, axis=-1, keepdims=True)
    rstd = lax.rsqrt(jnp.mean(center * center, axis=-1, keepdims=True) + 1e-05)
    return center * rstd, rstd


def norm_back(unit, rstd, gain, grad):
    grad_unit = grad * gain
    inner = grad_unit - jnp.mean(grad_unit, axis=-1, keepdims=True)
    return rstd * (inner - unit * jnp.mean(grad_unit * unit, axis=-1, keepdims=True))


def full(shape, dtype):
    return jax.ShapeDtypeStruct(shape, dtype)


def params(mib):
    return pltpu.CompilerParams(vmem_limit_bytes=mib * 2**20)


def cost(flops, moved):
    return pl.CostEstimate(flops=int(flops), bytes_accessed=int(moved), transcendentals=0)


HBM = pl.BlockSpec(memory_space=pltpu.HBM)
SMEM = pl.BlockSpec(memory_space=pltpu.SMEM)
VMEM = pl.BlockSpec(memory_space=pltpu.VMEM)


def copy_all(pairs, sems):
    copies = [pltpu.make_async_copy(source, target, sems.at[i]) for i, (source, target) in enumerate(pairs)]
    for each in copies:
        each.start()
    return copies


def head_masks(dtype, scale):
    lane = lax.broadcasted_iota(jnp.int32, (1, LANE), 1)
    return [jnp.where(lane // HEAD == h, scale, 0.0).astype(dtype) for h in range(2)]


def live_scores(key, query, length):
    scores = mm_nt(key, query)
    return jnp.where(lax.broadcasted_iota(jnp.int32, scores.shape, 0) < length, scores, -1e30)


def emit(regions, pieces, target, sems, first):
    return [
        pltpu.make_async_copy(
            pieces[name].at[pl.ds(row, rows), pl.ds(column, columns)],
            target.at[pl.ds(to_row, rows), pl.ds(to_column, columns)],
            sems.at[first + i],
        )
        for i, (name, row, column, rows, columns, to_row, to_column) in enumerate(regions)
    ]


def wire_copies(plan, inner, pieces, targets, sems, act):
    for parity in range(2):

        @pl.when(inner == parity)
        def _():
            at = to = 0
            for chunk in plan:
                for regions in (chunk["regions"][parity], chunk["regions"][1 - parity]):
                    for each in emit(regions, pieces, targets[to], sems, at):
                        getattr(each, act)()
                    at += chunk["most"]
                    to += 1


def plan_shapes(plan, width):
    return [full((chunk["high"] - chunk["low"], width), BF16) for chunk in plan for _ in range(2)]


def plan_sems(plan):
    return sum(2 * chunk["most"] for chunk in plan)


def table_rows(gains_ref, shifts_ref, section, which):
    return gains_ref[section, which : which + 1, :].astype(F32), shifts_ref[section, which : which + 1, :].astype(F32)


def attend_kernel(scalars, facts, own_any, other_any, gains_ref, shifts_ref, w_qkv, w_out, ht_any, qkv_any, att_any, part_any, lse_ref,
                  x_buf, w_buf, o_buf, h_buf, ht_ref, qkv_ref, att_ref, part_ref, sems):
    role, length = scalars[0], facts[0]
    gain, shift = table_rows(gains_ref, shifts_ref, facts[1], 0)
    width, half = w_out.shape[1], w_out.shape[0] // 2
    rows = own_any.shape[0]
    col = pl.multiple_of(role * half, LANE)
    mine, theirs = (pl.ds(pl.multiple_of(r * rows, rows), rows) for r in (role, 1 - role))
    copies = copy_all(
        [(own_any, x_buf.at[mine, :]), (other_any, x_buf.at[theirs, :])]
        + [(w_qkv.at[:, pl.ds(i * width + col, half)], w_buf.at[:, pl.ds(i * half, half)]) for i in range(3)]
        + [(w_out.at[pl.ds(col, half), :], o_buf)],
        sems,
    )
    copies[0].wait()
    copies[1].wait()
    for at in range(0, 2 * rows, LANE):
        unit, _ = norm_stats(x_buf[at : at + LANE, :].astype(F32))
        hidden = (unit * gain + shift).astype(BF16)
        h_buf[at : at + LANE, :] = hidden
        ht_ref[:, at : at + LANE] = hidden.T
    writes = [pltpu.make_async_copy(s, t, sems.at[6 + i]) for i, (s, t) in enumerate(((ht_ref, ht_any), (qkv_ref, qkv_any), (att_ref, att_any), (part_ref, part_any)))]
    writes[0].start()
    for i in range(3):
        copies[2 + i].wait()
        qkv_ref[:, i * half : (i + 1) * half] = mm(h_buf[...], w_buf[:, i * half : (i + 1) * half]).astype(BF16)
    writes[1].start()

    def pair(at, carry):
        c = pl.multiple_of(at * LANE, LANE)
        q, k, v = (qkv_ref[:, pl.ds(i * half + c, LANE)] for i in range(3))
        q_masks, v_masks = head_masks(BF16, 0.125), head_masks(BF16, 1.0)
        for group in range(2):
            total = 0.0
            for h in range(2):
                query = q[group * rows : (group + 1) * rows] * q_masks[h]
                scores = [live_scores(k[:rows], query, length)]
                if group:
                    scores.append(mm_nt(k[rows:], query))
                top = jnp.max(scores[0], axis=0, keepdims=True)
                if group:
                    top = jnp.maximum(top, jnp.max(scores[1], axis=0, keepdims=True))
                powers = [jnp.exp(s - top) for s in scores]
                below = sum(jnp.sum(p, axis=0, keepdims=True) for p in powers)
                lse_ref[pl.ds(2 * at + h, 1), group * rows : (group + 1) * rows] = top + jnp.log(below)
                inverse = 1.0 / below
                for which, p in enumerate(powers):
                    prob = (p * inverse).astype(BF16)
                    total = total + mm_tn(prob, v[which * rows : (which + 1) * rows] * v_masks[h])
            att_ref[group * rows : (group + 1) * rows, pl.ds(c, LANE)] = total.astype(BF16)
        return carry

    lax.fori_loop(0, half // LANE, pair, 0)
    writes[2].start()
    copies[5].wait()
    part_ref[...] = mm(att_ref[...], o_buf[...]).astype(BF16)
    writes[3].start()
    for each in writes:
        each.wait()


def attend(scalars, facts, halves, gains, shifts, w_qkv, w_out):
    rows, width = 2 * halves[0].shape[0], halves[0].shape[1]
    half = width // 2
    outs = [(width, rows), (rows, 3 * half), (rows, half), (rows, width)]
    return pl.pallas_call(
        attend_kernel,
        in_specs=[SMEM, SMEM, HBM, HBM, VMEM, VMEM, HBM, HBM],
        out_specs=[HBM] * 4 + [VMEM],
        out_shape=[full(s, BF16) for s in outs] + [full((half // HEAD, rows), F32)],
        scratch_shapes=[pltpu.VMEM((rows, width), BF16), pltpu.VMEM((width, 3 * half), BF16), pltpu.VMEM((half, width), BF16), pltpu.VMEM((rows, width), BF16)]
        + [pltpu.VMEM(s, BF16) for s in outs] + [pltpu.SemaphoreType.DMA((10,))],
        compiler_params=params(60),
        cost_estimate=cost(12e9, 8e6),
        name="attend",
    )(scalars, facts, *halves, gains, shifts, w_qkv, w_out)


def unit_copies(w_up, w_down, up_buf, down_buf, first):
    blocks = w_up.shape[1] // (4 * LANE)
    pairs = []
    for b in range(blocks):
        at = pl.multiple_of((4 * b + first) * LANE, LANE)
        pairs.append((w_up.at[:, pl.ds(at, LANE)], up_buf.at[:, pl.ds(b * LANE, LANE)]))
    for b in range(blocks):
        at = pl.multiple_of((4 * b + first) * LANE, LANE)
        pairs.append((w_down.at[pl.ds(at, LANE), :], down_buf.at[pl.ds(b * LANE, LANE), :]))
    return pairs


def gelu_parts(up):
    cdf = 0.5 + 0.5 * lax.erf(up * np.float32(0.5**0.5))
    slope = cdf + up * (jnp.exp(-0.5 * up * up) * np.float32(1 / np.sqrt(2 * np.pi)))
    return up * cdf, slope


def both_halves(role, rows, pairs):
    out = []
    for own, other, buffer, first in pairs:
        for source, r in ((own, role), (other, 1 - role)):
            out.append((source, buffer.at[pl.ds(pl.multiple_of(first + r * rows, rows), rows), :]))
    return out


def own_kernel(plan, scalars, facts_a, facts_b, xa, xao, xb, xbo, pa, ra, pb, rb, dya, dyao, dyb, dybo, gains_ref, shifts_ref, w_up, w_down, *refs):
    h_any, act_any, dup_any, res_any, gu_any = refs[:5]
    targets = refs[5:-14]
    x_buf, p_buf, r_buf, dy_buf, up_buf, down_buf, ht_buf, h_ref, gd_ref, gu_ref, act_ref, dup_ref, res_ref, sems = refs[-14:]
    role, x, inner = scalars[0], scalars[1], scalars[2]
    half_rows = xa.shape[0]
    rows = 2 * half_rows
    quarter = up_buf.shape[1]
    sources = both_halves(role, half_rows, [(xa, xao, x_buf, 0)]) + [(pa, p_buf.at[pl.ds(0, rows), :]), (ra, r_buf.at[pl.ds(0, rows), :])]
    sources += both_halves(role, half_rows, [(xb, xbo, x_buf, rows)]) + [(pb, p_buf.at[pl.ds(rows, rows), :]), (rb, r_buf.at[pl.ds(rows, rows), :])]
    sources += unit_copies(w_up, w_down, up_buf, down_buf, role + 2 * x)
    sources += both_halves(role, half_rows, [(dya, dyao, dy_buf, 0), (dyb, dybo, dy_buf, rows)])
    copies = copy_all(sources, sems)
    count = len(sources)
    for u in range(2):
        gain, shift = table_rows(gains_ref, shifts_ref, (facts_a, facts_b)[u][1], 1)
        for i in range(4):
            copies[4 * u + i].wait()

        def norm(i, carry):
            at = pl.multiple_of(u * rows + i * LANE, LANE)
            here = pl.ds(at, LANE)
            residual = x_buf[here, :].astype(F32) + (p_buf[here, :].astype(F32) + r_buf[here, :].astype(F32))
            unit, _ = norm_stats(residual)
            hidden = (unit * gain + shift).astype(BF16)
            h_ref[here, :] = hidden
            ht_buf[:, here] = hidden.T
            if u == 0:
                per = half_rows // LANE

                @pl.when(i // per == role)
                def _():
                    res_ref[pl.ds(pl.multiple_of((i % per) * LANE, LANE), LANE), :] = residual

            return carry

        lax.fori_loop(0, rows // LANE, norm, 0)
    writes = [pltpu.make_async_copy(s, t, sems.at[count + i]) for i, (s, t) in enumerate(((h_ref, h_any), (res_ref, res_any), (act_ref, act_any), (dup_ref, dup_any), (gu_ref, gu_any)))]
    writes[0].start()
    writes[1].start()
    for each in copies[8:]:
        each.wait()

    def block(i, carry):
        cols = pl.ds(pl.multiple_of(i * 256, 256), 256)
        act, slope = gelu_parts(mm(h_ref[...], up_buf[:, cols]))
        act = act.astype(BF16)
        act_ref[:, cols] = act[:rows]
        dup = (mm_nt(dy_buf[...], down_buf[cols, :]) * slope).astype(BF16)
        dup_ref[:, cols] = dup
        gd_ref[cols, :] = mm_tn(act, dy_buf[...]).astype(BF16)
        gu_ref[:, cols] = mm(ht_buf[...], dup).astype(BF16)
        return carry

    lax.fori_loop(0, quarter // 256, block, 0)
    pieces = {"d": gd_ref, "u": gu_ref}
    wire_sems = sems.at[pl.ds(count + 5, plan_sems(plan))]
    wire_copies(plan, inner, pieces, targets, wire_sems, "start")
    for each in writes[2:]:
        each.start()
    wire_copies(plan, inner, pieces, targets, wire_sems, "wait")
    for each in writes:
        each.wait()


def own_units(plan, scalars, facts, values, parts, came, dys, gains, shifts, w_up, w_down):
    rows, width = 2 * values[0].shape[0], values[0].shape[1]
    quarter = w_up.shape[1] // 4
    count = 8 + 2 * (quarter // LANE) + 4 + 5 + plan_sems(plan)
    big = lambda *s: pltpu.VMEM(s, BF16)
    shapes = plan_shapes(plan, width)
    return pl.pallas_call(
        functools.partial(own_kernel, plan),
        in_specs=[SMEM] * 3 + [HBM] * 12 + [VMEM] * 2 + [HBM] * 2,
        out_specs=[HBM] * (5 + len(shapes)),
        out_shape=[full((2 * rows, width), BF16), full((rows, quarter), BF16), full((2 * rows, quarter), BF16), full((rows // 2, width), F32), full((width, quarter), BF16)] + shapes,
        scratch_shapes=[big(2 * rows, width)] * 4
        + [big(width, quarter), big(quarter, width), big(width, 2 * rows), big(2 * rows, width), big(quarter, width), big(width, quarter), big(rows, quarter), big(2 * rows, quarter), pltpu.VMEM((rows // 2, width), F32), pltpu.SemaphoreType.DMA((count,))],
        compiler_params=params(60),
        cost_estimate=cost(20e9, 8e6),
        name="own_units",
    )(scalars, *facts, *values, parts[0], came[0], parts[1], came[1], *dys, gains, shifts, w_up, w_down)


def rest_kernel(scalars, h_any, dya, dyao, dyb, dybo, act_any, dup_any, res_ref, w_up, w_down, dh_ref, keep_ref, send_ref,
                h_buf, dy_buf, act_own, act_buf, dup_own, dup_buf, up_own, down_own, up_buf, down_buf, sems):
    role, x = scalars[0], scalars[1]
    rows = 2 * dya.shape[0]
    quarter = up_buf.shape[1]
    blocks = quarter // LANE
    copies = copy_all(
        [(h_any, h_buf)]
        + unit_copies(w_up, w_down, up_buf, down_buf, role + 2 * (1 - x))
        + both_halves(role, rows // 2, [(dya, dyao, dy_buf, 0), (dyb, dybo, dy_buf, rows)])
        + [(act_any, act_own), (dup_any, dup_own)]
        + unit_copies(w_up, w_down, up_own, down_own, role + 2 * x),
        sems,
    )
    first = 1 + 2 * blocks + 4
    for each in copies[:first]:
        each.wait()

    def block(i, carry):
        cols = pl.ds(pl.multiple_of(i * 256, 256), 256)
        act, slope = gelu_parts(mm(h_buf[...], up_buf[:, cols]))
        act_buf[:, cols] = act[:rows].astype(BF16)
        dup_buf[:, cols] = (mm_nt(dy_buf[...], down_buf[cols, :]) * slope).astype(BF16)
        return carry

    lax.fori_loop(0, quarter // 256, block, 0)
    for each in copies[first:]:
        each.wait()

    def back(i, carry):
        here = pl.ds(pl.multiple_of(i * 256, 256), 256)
        dh_ref[here, :] = (mm_nt(dup_own[here, :], up_own[...]) + mm_nt(dup_buf[here, :], up_buf[...])).astype(BF16)
        return carry

    lax.fori_loop(0, 2 * rows // 256, back, 0)
    keep = pl.ds(pl.multiple_of(role * (rows // 2), rows // 2), rows // 2)
    send = pl.ds(pl.multiple_of((1 - role) * (rows // 2), rows // 2), rows // 2)
    keep_ref[...] = res_ref[...] + (mm(act_own[keep, :], down_own[...]) + mm(act_buf[keep, :], down_buf[...]))
    send_ref[...] = (mm(act_own[send, :], down_own[...]) + mm(act_buf[send, :], down_buf[...])).astype(BF16)


def rest_units(scalars, hidden, dys, act, dup, residual, w_up, w_down):
    rows, width = 2 * dys[0].shape[0], dys[0].shape[1]
    quarter = w_up.shape[1] // 4
    count = 7 + 4 * (quarter // LANE)
    big = lambda *s: pltpu.VMEM(s, BF16)
    return pl.pallas_call(
        rest_kernel,
        in_specs=[SMEM] + [HBM] * 7 + [VMEM] + [HBM] * 2,
        out_specs=[VMEM] * 3,
        out_shape=[full((2 * rows, width), BF16), full((rows // 2, width), F32), full((rows // 2, width), BF16)],
        scratch_shapes=[big(2 * rows, width)] * 2 + [big(rows, quarter)] * 2 + [big(2 * rows, quarter)] * 2 + [big(width, quarter), big(quarter, width)] * 2 + [pltpu.SemaphoreType.DMA((count,))],
        compiler_params=params(60),
        cost_estimate=cost(20e9, 8e6),
        name="rest_units",
    )(scalars, hidden, *dys, act, dup, residual, w_up, w_down)


def pair_back(qkv, lse, datt, c, c_d, rows, half, length):
    q, k, v = (qkv[:, pl.ds(i * half + c, LANE)] for i in range(3))
    grad = datt[:, pl.ds(c_d, LANE)]
    scaled, plain = head_masks(BF16, 0.125), head_masks(BF16, 1.0)
    dq = []
    dk, dv = [0.0, 0.0], [0.0, 0.0]
    for group in range(2):
        here = slice(group * rows, (group + 1) * rows)
        dq_here = 0.0
        for h in range(2):
            query, above = q[here] * scaled[h], grad[here] * plain[h]
            log_total = lse(h, here)
            probs, dprobs = [], []
            delta = 0.0
            for which in range(group + 1):
                there = slice(which * rows, (which + 1) * rows)
                scores = live_scores(k[there], query, length) if which == 0 else mm_nt(k[there], query)
                prob = jnp.exp(scores - log_total)
                dprob = mm_nt(v[there], above)
                delta = delta + jnp.sum(prob * dprob, axis=0, keepdims=True)
                dv[which] = dv[which] + mm(prob.astype(BF16), above)
                probs.append(prob)
                dprobs.append(dprob)
            for which in range(group + 1):
                there = slice(which * rows, (which + 1) * rows)
                dscore = (probs[which] * (dprobs[which] - delta)).astype(BF16)
                dk[which] = dk[which] + mm(dscore, query)
                dq_here = dq_here + mm_tn(dscore, k[there] * scaled[h])
        dq.append(dq_here)
    return dq, dk, dv


def turn_kernel(plan, scalars, facts_a, facts_b, xa, xao, xb, xbo, pa, ra, pb, rb, dh_any, dhr_any, dya, dyao, dyb, dybo, gains_ref, shifts_ref, w_out, att_a, att_b, gu_any, *refs):
    dr_any, vec_ref, datt_any, go_any = refs[:4]
    targets = refs[4:-14]
    x_buf, p_buf, r_buf, dh_buf, dhr_buf, dy_buf, da_buf, o_buf, datt_buf, att_buf, gu_buf, dr_ref, go_ref, sems = refs[-14:]
    role, x, inner = scalars[0], scalars[1], scalars[2]
    rows, width = xa.shape
    rows2, half = 2 * rows, width // 2
    quarter = half // 2
    own = pl.multiple_of(x * quarter, LANE)
    col = pl.multiple_of(role * half, LANE)
    pairs = []
    for u, (xs, xo, ps, rs, dys, dyo) in enumerate(((xa, xao, pa, ra, dya, dyao), (xb, xbo, pb, rb, dyb, dybo))):
        here = pl.ds(u * rows2, rows2)
        pairs += both_halves(role, rows, [(xs, xo, x_buf, u * rows2), (dys, dyo, dy_buf, u * rows2)])
        pairs += [(ps, p_buf.at[here, :]), (rs, r_buf.at[here, :]), (dh_any.at[here, :], dh_buf.at[here, :]), (dhr_any.at[here, :], dhr_buf.at[here, :])]
    pairs.append((w_out.at[pl.ds(col, half), :], o_buf))
    for u, a in enumerate((att_a, att_b)):
        pairs.append((a.at[:, pl.ds(own, quarter)], att_buf.at[pl.ds(u * rows2, rows2), :]))
    pairs.append((gu_any, gu_buf))
    copies = copy_all(pairs, sems)
    count = len(pairs)
    vec_ref[...] = jnp.zeros_like(vec_ref)
    for u in range(2):
        gain, _ = table_rows(gains_ref, shifts_ref, (facts_a, facts_b)[u][1], 1)
        for i in range(8):
            copies[8 * u + i].wait()

        def norm(i, carry):
            here = pl.ds(pl.multiple_of(u * rows2 + i * LANE, LANE), LANE)
            residual = x_buf[here, :].astype(F32) + (p_buf[here, :].astype(F32) + r_buf[here, :].astype(F32))
            unit, rstd = norm_stats(residual)
            dh2 = dh_buf[here, :].astype(F32) + dhr_buf[here, :].astype(F32)
            grad = dy_buf[here, :].astype(F32) + norm_back(unit, rstd, gain, dh2)
            da_buf[here, :] = grad.astype(BF16)
            if u == 0:
                per = rows // LANE

                @pl.when(i // per == role)
                def _():
                    dr_ref[pl.ds(pl.multiple_of((i % per) * LANE, LANE), LANE), :] = grad
                    vec_ref[0:1, :] += jnp.sum(dh2 * unit, axis=0, keepdims=True)
                    vec_ref[1:2, :] += jnp.sum(dh2, axis=0, keepdims=True)

            return carry

        lax.fori_loop(0, rows2 // LANE, norm, 0)
    writes = [pltpu.make_async_copy(s, t, sems.at[count + i]) for i, (s, t) in enumerate(((dr_ref, dr_any), (go_ref, go_any), (datt_buf, datt_any)))]
    writes[0].start()
    for each in copies[16:]:
        each.wait()
    go_ref[...] = mm_tn(att_buf[...], da_buf[...]).astype(BF16)
    writes[1].start()
    wire_sems = sems.at[pl.ds(count + 3, max(1, plan_sems(plan)))]
    wire_copies(plan, inner, {"o": go_ref, "u": gu_buf}, targets, wire_sems, "start")
    datt_buf[...] = mm_nt(da_buf[...], o_buf[...]).astype(BF16)
    writes[2].start()
    wire_copies(plan, inner, {"o": go_ref, "u": gu_buf}, targets, wire_sems, "wait")
    for each in writes:
        each.wait()


def turn(plan, scalars, facts, values, parts, came, dh, dh_came, dys, gains, shifts, w_out, atts, grad_up):
    rows2, width = 2 * values[0].shape[0], values[0].shape[1]
    half = width // 2
    big = lambda *s: pltpu.VMEM(s, BF16)
    tokens = 2 * rows2
    shapes = plan_shapes(plan, width)
    return pl.pallas_call(
        functools.partial(turn_kernel, plan),
        in_specs=[SMEM] * 3 + [HBM] * 14 + [VMEM] * 2 + [HBM] * 4,
        out_specs=[HBM, VMEM, HBM, HBM] + [HBM] * len(shapes),
        out_shape=[full((rows2 // 2, width), F32), full((8, width), F32), full((tokens, half), BF16), full((half // 2, width), BF16)] + shapes,
        scratch_shapes=[big(tokens, width)] * 7
        + [big(half, width), big(tokens, half), big(tokens, half // 2), big(*grad_up.shape), pltpu.VMEM((rows2 // 2, width), F32), big(half // 2, width), pltpu.SemaphoreType.DMA((23 + max(1, plan_sems(plan)),))],
        compiler_params=params(60),
        cost_estimate=cost(12e9, 8e6),
        name="turn",
    )(scalars, *facts, *values, parts[0], came[0], parts[1], came[1], dh, dh_came, *dys, gains, shifts, w_out, *atts, grad_up)


def back_kernel(plan, scalars, facts_a, facts_b, datt_any, qkv_a, qkv_b, ht_a, ht_b, go_any, lse_a, lse_b, *refs):
    dqa_any = refs[0]
    targets = refs[1:-7]
    datt_buf, qkv_buf, ht_buf, dq_buf, gq_ref, go_buf, sems = refs[-7:]
    x, inner = scalars[1], scalars[2]
    tokens, half = datt_any.shape
    rows2 = tokens // 2
    rows, quarter = rows2 // 2, half // 2
    own = pl.multiple_of(x * quarter, LANE)
    lse = (lse_a, lse_b)
    first_half, second_half = pl.ds(0, rows2), pl.ds(rows2, rows2)
    pairs = []
    for here, q in ((first_half, qkv_a), (second_half, qkv_b)):
        pairs += [(q, qkv_buf.at[here, :]), (datt_any.at[here, :], datt_buf.at[here, :])]
    pairs += [(ht_a, ht_buf.at[:, first_half]), (ht_b, ht_buf.at[:, second_half]), (go_any, go_buf)]
    copies = copy_all(pairs, sems)
    count = len(pairs)
    for u in range(2):
        copies[2 * u].wait()
        copies[2 * u + 1].wait()
        base = u * rows2
        length = (facts_a, facts_b)[u][0]

        def one(at, carry):
            c = pl.multiple_of(own + at * LANE, LANE)
            to = pl.multiple_of(at * LANE, LANE)
            first = (own + at * LANE) // HEAD
            look = lambda h, here: lse[u][pl.ds(first + h, 1), here]
            dq, dk, dv = pair_back(qkv_buf.at[pl.ds(base, rows2), :], look, datt_buf.at[pl.ds(base, rows2), :], c, c, rows, half, length)
            for i, halves in enumerate((dq, dk, dv)):
                for g in range(2):
                    dq_buf[base + g * rows : base + (g + 1) * rows, pl.ds(i * quarter + to, LANE)] = halves[g].astype(BF16)
            return carry

        lax.fori_loop(0, quarter // LANE, one, 0)
    write = pltpu.make_async_copy(dq_buf.at[first_half, :], dqa_any, sems.at[count])
    write.start()
    for each in copies[4:]:
        each.wait()
    for i in range(3):
        cols = slice(i * quarter, (i + 1) * quarter)
        gq_ref[:, cols] = mm(ht_buf[...], dq_buf[:, cols]).astype(BF16)
    pieces = {"q": gq_ref, "o": go_buf}
    wire_sems = sems.at[pl.ds(count + 1, plan_sems(plan))]
    wire_copies(plan, inner, pieces, targets, wire_sems, "start")
    wire_copies(plan, inner, pieces, targets, wire_sems, "wait")
    write.wait()


def back(plan, scalars, facts, datt, qkvs, hts, grad_out, lses):
    tokens, half = datt.shape
    width = 2 * half
    big = lambda *s: pltpu.VMEM(s, BF16)
    shapes = plan_shapes(plan, width)
    return pl.pallas_call(
        functools.partial(back_kernel, plan),
        in_specs=[SMEM] * 3 + [HBM] * 6 + [VMEM] * 2,
        out_specs=[HBM] * (1 + len(shapes)),
        out_shape=[full((tokens // 2, 3 * half // 2), BF16)] + shapes,
        scratch_shapes=[big(tokens, half), big(tokens, 3 * half), big(width, tokens), big(tokens, 3 * half // 2), big(width, 3 * half // 2), big(*grad_out.shape), pltpu.SemaphoreType.DMA((8 + plan_sems(plan),))],
        compiler_params=params(60),
        cost_estimate=cost(14e9, 8e6),
        name="back",
    )(scalars, *facts, datt, *qkvs, *hts, grad_out, *lses)


def last_kernel(scalars, facts, qkv_ref, lse_ref, datt_ref, dqa_ref, w_qkv, keep_ref, send_ref, w_own, w_buf, dq_buf, sems):
    role, x, length = scalars[0], scalars[1], facts[0]
    rows2, half = qkv_ref.shape[0], datt_ref.shape[1]
    rows, quarter, width = rows2 // 2, half // 2, 2 * half
    mine = pl.multiple_of(x * quarter, LANE)
    other = pl.multiple_of((1 - x) * quarter, LANE)
    col = pl.multiple_of(role * half, LANE)
    copies = copy_all(
        [(w_qkv.at[:, pl.ds(i * width + col + from_, quarter)], to.at[:, pl.ds(i * quarter, quarter)]) for from_, to in ((mine, w_own), (other, w_buf)) for i in range(3)],
        sems,
    )

    def one(at, carry):
        c = pl.multiple_of(other + at * LANE, LANE)
        to = pl.multiple_of(at * LANE, LANE)
        first = (other + at * LANE) // HEAD
        look = lambda h, here: lse_ref[pl.ds(first + h, 1), here]
        dq, dk, dv = pair_back(qkv_ref, look, datt_ref, c, c, rows, half, length)
        for i, halves in enumerate((dq, dk, dv)):
            for g in range(2):
                dq_buf[g * rows : (g + 1) * rows, pl.ds(i * quarter + to, LANE)] = halves[g].astype(BF16)
        return carry

    lax.fori_loop(0, quarter // LANE, one, 0)
    for each in copies:
        each.wait()
    keep = pl.ds(pl.multiple_of(role * rows, rows), rows)
    send = pl.ds(pl.multiple_of((1 - role) * rows, rows), rows)
    keep_ref[...] = mm_nt(dqa_ref[keep, :], w_own[...]) + mm_nt(dq_buf[keep, :], w_buf[...])
    send_ref[...] = (mm_nt(dqa_ref[send, :], w_own[...]) + mm_nt(dq_buf[send, :], w_buf[...])).astype(BF16)


def last(scalars, facts, qkv, lse, datt, dqa, w_qkv):
    rows2, half = qkv.shape[0], datt.shape[1]
    width = 2 * half
    big = lambda *s: pltpu.VMEM(s, BF16)
    return pl.pallas_call(
        last_kernel,
        in_specs=[SMEM] * 2 + [VMEM] * 4 + [HBM],
        out_specs=[VMEM] * 2,
        out_shape=[full((rows2 // 2, width), F32), full((rows2 // 2, width), BF16)],
        scratch_shapes=[big(width, 3 * half // 2)] * 2 + [big(rows2, 3 * half // 2), pltpu.SemaphoreType.DMA((6,))],
        compiler_params=params(60),
        cost_estimate=cost(7e9, 8e6),
        name="last",
    )(scalars, facts, qkv, lse, datt, dqa, w_qkv)


class Layout:
    def __init__(self, width, ff, sections, members):
        self.width, self.ff, self.members = width, ff, members
        shapes = {"q": (width, 3 * width), "o": (width, width), "u": (width, ff), "d": (ff, width), "s": (4 * sections, width)}
        start, self.spans = 0, {}
        for name, (rows, columns) in shapes.items():
            self.spans[name] = (start, rows, columns)
            start += rows * columns
        self.total = start
        self.share = start // members
        self.segments = [self.parts_of(m) for m in range(members)]
        self.rows = max(s[-1]["at"] + s[-1]["wire"] for s in self.segments)

    def span(self, member, name):
        start, rows, columns = self.spans[name]
        low = max(member * self.share, start) - start
        high = min((member + 1) * self.share, start + rows * columns) - start
        return (low, high) if low < high else None

    def parts_of(self, member):
        parts, at = [], 0
        for name in ("q", "o", "u", "d"):
            found = self.span(member, name)
            if found is None:
                continue
            columns = self.spans[name][2]
            low, high = found[0] // columns, -(-found[1] // columns)
            if name == "o":
                held = [r % (self.width // 4) for r in range(low, high)]
                low, high = min(held), max(held) + 1
            if name == "d":
                held = [r // (4 * LANE) * LANE + r % LANE for r in range(low, high)]
                low, high = min(held), max(held) + 1
            low, high = low // 16 * 16, -(-high // 16) * 16
            count = high - low
            wire = -(-(3 * count // 4) // 16) * 16 if name == "q" else count
            parts.append({"name": name, "low": low, "high": high, "at": at, "wire": wire})
            at += wire
        return parts

    def table(self):
        rows = []
        for share in range(2 * self.members):
            entry = [share * (self.share // 2) // LANE]
            held = {p["name"]: p for p in self.segments[share // 2]}
            for name in ("q", "o", "u", "d"):
                p = held.get(name)
                entry += [p["low"], p["high"], p["at"], p["wire"]] if p else [0, 0, 0, 0]
            rows.append(entry + [0] * (24 - len(entry)))
        return np.asarray(rows, np.int32)

    def regions(self, member, low, high):
        found = []

        def cut(name, row, column, rows, columns, to_row, to_column):
            first, last = max(to_row, low), min(to_row + rows, high)
            if first < last:
                found.append((name, row + first - to_row, column, last - first, columns, first - low, to_column))

        for p in self.segments[member]:
            if p["name"] == "q":
                quarter = self.width // 4
                side = p["high"] - p["low"] - p["wire"]
                cut("q", p["low"], 0, p["wire"], 3 * quarter, p["at"], 0)
                for i in range(3):
                    cut("q", p["low"] + p["wire"], i * quarter, side, quarter, p["at"] + i * side, 3 * quarter)
            else:
                cut(p["name"], p["low"], 0, p["wire"], self.width, p["at"], 0)
        return found

    def plans(self):
        stage_of = {"u": 0, "d": 0, "o": 1, "q": 2}
        stages = ([], [], [])
        for block in reversed(range(self.members // 2)):
            edges = {0, self.rows}
            for member in (2 * block, 2 * block + 1):
                for p in self.segments[member]:
                    edges |= {p["at"], p["at"] + p["wire"]}
            edges = sorted(edges)
            runs = []
            for low, high in zip(edges, edges[1:]):
                found = [stage_of[f[0]] for member in (2 * block, 2 * block + 1) for f in self.regions(member, low, high)]
                stage = max(found) if found else runs[-1][2]
                if runs and (runs[-1][2] == stage or 2 in (stage, runs[-1][2])):
                    runs[-1][1], runs[-1][2] = high, max(stage, runs[-1][2])
                else:
                    runs.append([low, high, stage])
            for low, high, stage in runs:
                middle = low + (high - low) // 32 * 16
                for first, last in [(low, middle), (middle, high)] if stage == 2 else [(low, high)]:
                    regions = [self.regions(2 * block + i, first, last) for i in range(2)]
                    stages[stage].append({"block": block, "low": first, "high": last, "regions": regions, "most": max(map(len, regions))})
        return stages


def after(value, *first):
    return lax.optimization_barrier((value, *first))[0]


def add(left, right):
    return (left.astype(F32) + right.astype(F32)).astype(BF16)


def tree_pairs(block, level, count):
    size = 2 << level
    pairs = []
    for low in range(0, count, size):
        middle, high = low + size // 2, low + size
        left, right = min(max(block, low), middle - 1), min(max(block, middle), high - 1)
        source, target = (right, left) if block < middle else (left, right)
        pairs += [(2 * source + y, 2 * target + y) for y in range(2)]
    return pairs


def place_kernel(spans, table, *refs):
    quad, (small_ref, out_ref, wire, flat, sems) = refs[:-5], refs[-5:]
    me, unit0 = table[24], table[0]
    units = out_ref.shape[0]
    width = wire.shape[2]
    chunks = width // LANE
    front = 512
    x, role = me // 2, me % 2
    where = (me, role + 2 * (1 - x), (1 - role) + 2 * x, (1 - role) + 2 * (1 - x))
    per_piece = len(quad) // 4
    pairs = []
    for i, source in enumerate(quad):
        rows = source.shape[0]
        first = sum(s.shape[0] for s in quad[i // per_piece * per_piece : i])
        pairs.append((source, wire.at[where[i // per_piece], pl.ds(first, rows), :]))
    copies = copy_all(pairs, sems.at[pl.ds(1, len(pairs))])
    for each in copies:
        each.wait()

    def rows_of(name, per_row):
        at = 1 + 4 * "qoud".index(name)
        low, high = table[at], table[at + 1]
        base = unit0 - spans[name][0] // LANE
        first = jnp.maximum(low // 16, jnp.maximum(base, 0) // per_row // 16)
        last = jnp.minimum(high // 16, (jnp.maximum(base + units, 0) + per_row * 16 - 1) // (per_row * 16))
        return low, first, last, table[at + 2], table[at + 3], base

    low, first, last, at, n1, base = rows_of("q", 3 * chunks)
    n2 = table[2] - table[1] - n1

    def qkv(g, carry):
        row = g * 16 - low
        to = front + g * 16 * 3 * chunks - base
        beside = row >= n1
        half = chunks // 4
        for section in range(3):
            source = jnp.where(beside, at + section * n2 + row - n1, at + row)
            for h in range(half):
                column = pl.multiple_of(jnp.where(beside, 3 * width // 4 + h * LANE, section * (width // 4) + h * LANE), LANE)
                for piece in range(4):
                    unit = section * chunks + (piece % 2) * (chunks // 2) + (piece // 2) * half + h
                    flat[pl.ds(to + unit, 16, stride=3 * chunks), :] = wire[piece, pl.ds(pl.multiple_of(source, 16), 16), pl.ds(column, LANE)].astype(F32)
        return carry

    lax.fori_loop(first, jnp.maximum(first, last), qkv, 0)
    per = spans["u"][2] // LANE
    low, first, last, at, _, base = rows_of("u", per)

    def up(g, carry):
        source = pl.multiple_of(at + g * 16 - low, 16)
        to = front + g * 16 * per - base
        for h in range(chunks):
            for piece in range(4):
                flat[pl.ds(to + 4 * h + piece, 16, stride=per), :] = wire[piece, pl.ds(source, 16), h * LANE : (h + 1) * LANE].astype(F32)
        return carry

    lax.fori_loop(first, jnp.maximum(first, last), up, 0)

    for name in ("o", "d"):
        slot = 1 + 4 * "qoud".index(name)
        low, high, at = table[slot], table[slot + 1], table[slot + 2]
        base = unit0 - spans[name][0] // LANE

        def rows(g, carry):
            row = g * 16
            source = pl.multiple_of(at + row - low, 16)
            for piece in range(4):
                if name == "o":
                    line = (piece % 2) * (width // 2) + (piece // 2) * (width // 4) + row
                else:
                    line = (row // LANE) * (4 * LANE) + piece * LANE + row % LANE
                to = line * chunks - base

                @pl.when((to + 16 * chunks > 0) & (to < units))
                def _():
                    for h in range(chunks):
                        flat[pl.ds(front + to + h, 16, stride=chunks), :] = wire[piece, pl.ds(source, 16), h * LANE : (h + 1) * LANE].astype(F32)

            return carry

        lax.fori_loop(low // 16, high // 16, rows, 0)

    tail = spans["s"][0] // LANE - unit0

    @pl.when(tail < units)
    def _():
        for g in range(small_ref.shape[0] // 8):
            for h in range(chunks):
                flat[pl.ds(front + tail + g * 8 * chunks + h, 8, stride=chunks), :] = small_ref[g * 8 : (g + 1) * 8, h * LANE : (h + 1) * LANE]

    done = pltpu.make_async_copy(flat.at[pl.ds(front, units), :], out_ref, sems.at[0])
    done.start()
    done.wait()


def place(layout, table, quad, small):
    rows, width = layout.rows, layout.width
    units = layout.share // 2 // LANE
    quad = [part for piece in quad for part in piece]
    return pl.pallas_call(
        functools.partial(place_kernel, layout.spans),
        in_specs=[SMEM] + [HBM] * len(quad) + [VMEM],
        out_specs=HBM,
        out_shape=full((units, LANE), F32),
        scratch_shapes=[pltpu.VMEM((4, rows, width), BF16), pltpu.VMEM((-(-units // 8) * 8 + 1024, LANE), F32), pltpu.SemaphoreType.DMA((1 + len(quad),))],
        compiler_params=params(60),
        cost_estimate=cost(4e9, 8e6),
        name="place",
    )(table, *quad, small)


def local(frames, cotangent, w_qkv, w_out, w_up, w_down, gains, shifts, prompt_len, section):
    width, ff, sections = frames.shape[3], w_up.shape[1], gains.shape[0]
    role, group, member = lax.axis_index("role"), lax.axis_index("group"), lax.axis_index("member")
    x = group % 2
    members, groups = lax.axis_size("member"), lax.axis_size("group")
    layout = Layout(width, ff, sections, members)
    early, middle, late = layout.plans()
    outer, inner = member // 2, member % 2
    count = members // 2

    own_frames, own_cot = frames[0, 0], cotangent[0, 0]
    values = [own_frames, swap(own_frames, "role")]
    mate_frames = swap(own_frames, "group")
    facts = jnp.concatenate([prompt_len, section])
    mate_facts = swap(facts, "group")
    scalars = jnp.stack([role, x, inner]).astype(jnp.int32)

    levels = count.bit_length() - 1
    chunks = []

    def exchange(plan, arrays, *first):
        for i, chunk in enumerate(plan):
            keep, send = arrays[2 * i], arrays[2 * i + 1]
            chunks.append(dict(chunk, total=keep, came=swap(after(send, *first) if first else send, "member"), level=0))

    def climb(chunk):
        chunk["came"] = lax.ppermute(chunk["total"], "member", tree_pairs(chunk["block"], chunk["level"], count))
        chunk["level"] += 1

    def settle(chunk, *first):
        total = after(chunk["total"], *first) if first else chunk["total"]
        chunk["total"] = add(total, chunk["came"])

    first = attend(scalars, facts, values[:2], gains, shifts, w_qkv, w_out)
    mate_facts, mate_frames = after(mate_facts, first[3]), after(mate_frames, first[3])
    both = (facts, mate_facts)
    values += [mate_frames, swap(mate_frames, "role")]
    own_cot = after(own_cot, mate_frames)
    mate_cot = swap(own_cot, "group")
    dys = [own_cot, swap(own_cot, "role"), mate_cot, swap(mate_cot, "role")]
    second = attend(scalars, mate_facts, values[2:], gains, shifts, w_qkv, w_out)
    hts, qkvs, atts, parts, lses = zip(first, second)
    came = [after(swap(parts[0], "role"), parts[1]), swap(parts[1], "role")]
    hidden, act, dup, residual, grad_up, *wires = own_units(early, scalars, both, values, parts, came, dys, gains, shifts, w_up, w_down)
    exchange(early, wires)
    dh, out_keep, out_send = rest_units(scalars, hidden, dys, act, dup, residual, w_up, w_down)
    output = (out_keep + swap(out_send, "role").astype(F32)).astype(BF16)
    dh_came = swap(after(dh, chunks[0]["came"]), "role")
    settle(chunks[0], dh)
    climb(chunks[0])
    dr1, vec_two, datt, grad_out, *wires = turn(middle, scalars, both, values, parts, came, dh, dh_came, dys, gains, shifts, w_out, atts, grad_up)
    exchange(middle, wires)
    second_chunk = chunks[min(1, len(early) - 1)]
    if second_chunk is not chunks[0]:
        settle(second_chunk, datt)
        climb(second_chunk)
    dqa, *wires = back(late, scalars, both, after(datt, second_chunk["total"]), qkvs, hts, grad_out, lses)
    for chunk in chunks[: min(2, len(early))]:
        settle(chunk, dqa)
    exchange(late, wires, *(chunk["came"] for chunk in chunks[len(early) :]))
    dh1_keep, dh1_send = last(scalars, facts, qkvs[0], lses[0], after(datt, *(c["came"] for c in chunks[len(early) : -len(late)])), dqa, w_qkv)
    dh1_send = after(dh1_send, chunks[-len(late)]["came"])
    dh1 = dh1_keep + swap(dh1_send, "role").astype(F32)
    unit, rstd = norm_stats(own_frames.astype(F32))
    input_grad = dr1 + norm_back(unit, rstd, lax.dynamic_slice(gains, (facts[1], 0, 0), (1, 1, width))[0].astype(F32), dh1)

    vectors = jnp.stack([jnp.stack([jnp.sum(dh1 * unit, 0), vec_two[0]]), jnp.stack([jnp.sum(dh1, 0), vec_two[1]])])
    select = (jnp.arange(sections, dtype=jnp.int32) == facts[1]).astype(F32)
    small = select[None, :, None, None] * vectors[:, None]
    small = jnp.pad(small.reshape(4 * sections, width), ((0, -4 * sections % 8), (0, 0)))
    small_steps = []
    for axis in ("role", "group", "member"):
        distance = 1
        while distance < lax.axis_size(axis):
            small = small + swap(small, axis, distance)
            small_steps.append(small)
            distance *= 2

    for chunk in chunks[min(2, len(early)) :]:
        settle(chunk, dqa)
    joined = chunks[: min(2, len(early))]
    for chunk in chunks[min(2, len(early)) :]:
        before = joined[-1]
        mates = [c for c in joined if c["block"] == chunk["block"] and chunk["high"] == c["low"] and c["level"] == 0]
        mates += [c for c in joined if c["block"] == chunk["block"] and chunk["low"] == c["high"] and c["level"] == 0]
        if mates and chunk not in chunks[-len(late) :]:
            mate = mates[0]
            ends = sorted((mate, chunk), key=lambda c: c["low"])
            mate["total"] = jnp.concatenate([c["total"] for c in ends], 0)
            mate["low"], mate["high"] = ends[0]["low"], ends[1]["high"]
        else:
            joined.append(chunk)
    chunks = joined
    for chunk in chunks:
        if chunk["level"] == 0:
            climb(chunk)
            settle(chunk)
    for level in range(1, levels):
        for chunk in chunks:
            if level == levels - 1 and chunk in chunks[-2:]:
                chunk["total"] = after(chunk["total"], small_steps[-3 if chunk is chunks[-2] else -2])
            climb(chunk)
            settle(chunk)
    edges = [0, layout.rows // 32 * 16, layout.rows]
    quads = [[], [], [], []]
    for low, high in zip(edges, edges[1:]):
        final = jnp.zeros((high - low, width), BF16)
        for chunk in chunks:
            first, past = max(low, chunk["low"]), min(high, chunk["high"])
            if first >= past:
                continue
            here = chunk["total"][first - chunk["low"] : past - chunk["low"]]
            mine = outer == chunk["block"]
            part = jnp.where(mine, here, final[first - low : past - low])
            final = jnp.concatenate([final[: first - low], part, final[past - low :]], 0)
        distance = 2
        while distance < groups:
            final = add(final, swap(final, "group", distance))
            distance *= 2
        if high == layout.rows:
            final = after(final, small)
        mate = swap(final, "group")
        for into, value in zip(quads, (final, mate, swap(final, "role"), swap(mate, "role"))):
            into.append(value)
    table = lax.dynamic_slice(jnp.asarray(layout.table()), (2 * member + role, 0), (1, 24))[0]
    table = jnp.concatenate([table, (role + 2 * x)[None].astype(jnp.int32), jnp.zeros((7,), jnp.int32)])
    shard = place(layout, table, quads, small).reshape(-1)
    return output[None, None], input_grad[None, None], shard


def solution(mesh):
    rows = P(("group", "member"), "role", None, None)
    per_seq = P(("group", "member"))
    return jax.shard_map(
        local,
        mesh=mesh,
        in_specs=(rows, rows, P(), P(), P(), P(), P(), P(), per_seq, per_seq),
        out_specs=(rows, rows, P(("member", "role"))),
        check_vma=False,
    )
```

```python
import functools

import jax
import jax.numpy as jnp
import numpy as np
from jax import lax
from jax.experimental import pallas as pl
from jax.experimental.pallas import tpu as pltpu
from jax.sharding import PartitionSpec as P

HEADS = 16
LANE = 128
HEAD = 64
F32 = jnp.float32
BF16 = jnp.bfloat16


def dot(left, right, dims):
    return lax.dot_general(left, right, (dims, ((), ())), preferred_element_type=F32)


def mm(left, right):
    return dot(left, right, ((1,), (0,)))


def mm_nt(left, right):
    return dot(left, right, ((1,), (1,)))


def mm_tn(left, right):
    return dot(left, right, ((0,), (0,)))


def swap(value, axis, distance=1):
    count = lax.axis_size(axis)
    return lax.ppermute(value, axis, [(i, i ^ distance) for i in range(count)])


def norm_stats(values):
    center = values - jnp.mean(values, axis=-1, keepdims=True)
    rstd = lax.rsqrt(jnp.mean(center * center, axis=-1, keepdims=True) + 1e-05)
    return center * rstd, rstd


def norm_back(unit, rstd, gain, grad):
    grad_unit = grad * gain
    inner = grad_unit - jnp.mean(grad_unit, axis=-1, keepdims=True)
    return rstd * (inner - unit * jnp.mean(grad_unit * unit, axis=-1, keepdims=True))


def full(shape, dtype):
    return jax.ShapeDtypeStruct(shape, dtype)


def params(mib):
    return pltpu.CompilerParams(vmem_limit_bytes=mib * 2**20)


def cost(flops, moved):
    return pl.CostEstimate(flops=int(flops), bytes_accessed=int(moved), transcendentals=0)


HBM = pl.BlockSpec(memory_space=pltpu.HBM)
SMEM = pl.BlockSpec(memory_space=pltpu.SMEM)
VMEM = pl.BlockSpec(memory_space=pltpu.VMEM)


def copy_all(pairs, sems):
    copies = [pltpu.make_async_copy(source, target, sems.at[i]) for i, (source, target) in enumerate(pairs)]
    for each in copies:
        each.start()
    return copies


def head_masks(dtype, scale):
    lane = lax.broadcasted_iota(jnp.int32, (1, LANE), 1)
    return [jnp.where(lane // HEAD == h, scale, 0.0).astype(dtype) for h in range(2)]


def live_scores(key, query, length):
    scores = mm_nt(key, query)
    return jnp.where(lax.broadcasted_iota(jnp.int32, scores.shape, 0) < length, scores, -1e30)


def span_of(plan, name):
    rows = [edge for chunk in plan for regions in chunk["regions"] for r in regions if r[0] == name for edge in (r[1], r[1] + r[3])]
    return (min(rows), max(rows)) if rows else (0, 16)


def shifted(plan, name, by):
    move = lambda r: (r[0], r[1] - by, *r[2:]) if r[0] == name else r
    return [dict(chunk, regions=[[move(r) for r in regions] for regions in chunk["regions"]]) for chunk in plan]


def wire_copies(plan, inner, pieces, targets, sems, act, names="qoud"):
    for parity in range(2):

        @pl.when(inner == parity)
        def _():
            at = to = 0
            for chunk in plan:
                for regions in (chunk["regions"][parity], chunk["regions"][1 - parity]):
                    for i, (name, row, column, rows, columns, to_row, to_column) in enumerate(regions):
                        if name in names:
                            source = pieces[name].at[pl.ds(row, rows), pl.ds(column, columns)]
                            target = targets[to].at[pl.ds(to_row, rows), pl.ds(to_column, columns)]
                            getattr(pltpu.make_async_copy(source, target, sems.at[at + i]), act)()
                    at += chunk["most"]
                    to += 1


def plan_shapes(plan, width):
    return [full((chunk["high"] - chunk["low"], width), BF16) for chunk in plan for _ in range(2)]


def plan_sems(plan):
    return sum(2 * chunk["most"] for chunk in plan)


def table_rows(gains_ref, shifts_ref, section, which):
    return gains_ref[section, which : which + 1, :].astype(F32), shifts_ref[section, which : which + 1, :].astype(F32)


def attend_kernel(scalars, facts, own_any, other_any, gains_ref, shifts_ref, w_qkv, w_out, ht_any, qkv_any, att_any, part_any, lse_ref,
                  x_buf, w_buf, o_buf, h_buf, ht_ref, qkv_ref, att_ref, part_ref, sems):
    role, length = scalars[0], facts[0]
    gain, shift = table_rows(gains_ref, shifts_ref, facts[1], 0)
    width, half = w_out.shape[1], w_out.shape[0] // 2
    rows = own_any.shape[0]
    col = pl.multiple_of(role * half, LANE)
    mine, theirs = (pl.ds(pl.multiple_of(r * rows, rows), rows) for r in (role, 1 - role))
    copies = copy_all(
        [(own_any, x_buf.at[mine, :]), (other_any, x_buf.at[theirs, :])]
        + [(w_qkv.at[:, pl.ds(i * width + col, half)], w_buf.at[:, pl.ds(i * half, half)]) for i in range(3)]
        + [(w_out.at[pl.ds(col, half), :], o_buf)],
        sems,
    )
    copies[0].wait()
    copies[1].wait()
    for at in range(0, 2 * rows, LANE):
        unit, _ = norm_stats(x_buf[at : at + LANE, :].astype(F32))
        hidden = (unit * gain + shift).astype(BF16)
        h_buf[at : at + LANE, :] = hidden
        ht_ref[:, at : at + LANE] = hidden.T
    writes = [pltpu.make_async_copy(s, t, sems.at[6 + i]) for i, (s, t) in enumerate(((ht_ref, ht_any), (qkv_ref, qkv_any), (att_ref, att_any), (part_ref, part_any)))]
    writes[0].start()
    for i in range(3):
        copies[2 + i].wait()
        qkv_ref[:, i * half : (i + 1) * half] = mm(h_buf[...], w_buf[:, i * half : (i + 1) * half]).astype(BF16)
    writes[1].start()

    def pair(at, carry):
        c = pl.multiple_of(at * LANE, LANE)
        q, k, v = (qkv_ref[:, pl.ds(i * half + c, LANE)] for i in range(3))
        q_masks, v_masks = head_masks(BF16, 0.125), head_masks(BF16, 1.0)
        for group in range(2):
            total = 0.0
            for h in range(2):
                query = q[group * rows : (group + 1) * rows] * q_masks[h]
                scores = [live_scores(k[:rows], query, length)]
                if group:
                    scores.append(mm_nt(k[rows:], query))
                top = jnp.max(scores[0], axis=0, keepdims=True)
                if group:
                    top = jnp.maximum(top, jnp.max(scores[1], axis=0, keepdims=True))
                powers = [jnp.exp(s - top) for s in scores]
                below = sum(jnp.sum(p, axis=0, keepdims=True) for p in powers)
                lse_ref[pl.ds(2 * at + h, 1), group * rows : (group + 1) * rows] = top + jnp.log(below)
                inverse = 1.0 / below
                for which, p in enumerate(powers):
                    prob = (p * inverse).astype(BF16)
                    total = total + mm_tn(prob, v[which * rows : (which + 1) * rows] * v_masks[h])
            att_ref[group * rows : (group + 1) * rows, pl.ds(c, LANE)] = total.astype(BF16)
        return carry

    lax.fori_loop(0, half // LANE, pair, 0)
    writes[2].start()
    copies[5].wait()
    part_ref[...] = mm(att_ref[...], o_buf[...]).astype(BF16)
    writes[3].start()
    for each in writes:
        each.wait()


def attend(scalars, facts, halves, gains, shifts, w_qkv, w_out):
    rows, width = 2 * halves[0].shape[0], halves[0].shape[1]
    half = width // 2
    outs = [(width, rows), (rows, 3 * half), (rows, half), (rows, width)]
    return pl.pallas_call(
        attend_kernel,
        in_specs=[SMEM, SMEM, HBM, HBM, VMEM, VMEM, HBM, HBM],
        out_specs=[HBM] * 4 + [VMEM],
        out_shape=[full(s, BF16) for s in outs] + [full((half // HEAD, rows), F32)],
        scratch_shapes=[pltpu.VMEM((rows, width), BF16), pltpu.VMEM((width, 3 * half), BF16), pltpu.VMEM((half, width), BF16), pltpu.VMEM((rows, width), BF16)]
        + [pltpu.VMEM(s, BF16) for s in outs] + [pltpu.SemaphoreType.DMA((10,))],
        compiler_params=params(60),
        cost_estimate=cost(12e9, 8e6),
        name="attend",
    )(scalars, facts, *halves, gains, shifts, w_qkv, w_out)


def unit_copies(w_up, w_down, up_buf, down_buf, first):
    blocks = w_up.shape[1] // (4 * LANE)
    pairs = []
    for b in range(blocks):
        at = pl.multiple_of((4 * b + first) * LANE, LANE)
        pairs.append((w_up.at[:, pl.ds(at, LANE)], up_buf.at[:, pl.ds(b * LANE, LANE)]))
    for b in range(blocks):
        at = pl.multiple_of((4 * b + first) * LANE, LANE)
        pairs.append((w_down.at[pl.ds(at, LANE), :], down_buf.at[pl.ds(b * LANE, LANE), :]))
    return pairs


def gelu_parts(up):
    cdf = 0.5 + 0.5 * lax.erf(up * np.float32(0.5**0.5))
    slope = cdf + up * (jnp.exp(-0.5 * up * up) * np.float32(1 / np.sqrt(2 * np.pi)))
    return up * cdf, slope


def both_halves(role, rows, pairs):
    out = []
    for own, other, buffer, first in pairs:
        for source, r in ((own, role), (other, 1 - role)):
            out.append((source, buffer.at[pl.ds(pl.multiple_of(first + r * rows, rows), rows), :]))
    return out


def own_kernel(plan, kept, scalars, facts_a, facts_b, xa, xao, xb, xbo, pa, ra, pb, rb, dya, dyao, dyb, dybo, gains_ref, shifts_ref, w_up, w_down, *refs):
    h_any, act_any, dup_any, res_any, gu_any = refs[:5]
    targets = refs[5:-14]
    x_buf, p_buf, r_buf, dy_buf, up_buf, down_buf, ht_buf, h_ref, gd_ref, gu_ref, act_ref, dup_ref, res_ref, sems = refs[-14:]
    role, x, inner = scalars[0], scalars[1], scalars[2]
    half_rows = xa.shape[0]
    rows = 2 * half_rows
    quarter = up_buf.shape[1]
    sources = both_halves(role, half_rows, [(xa, xao, x_buf, 0)]) + [(pa, p_buf.at[pl.ds(0, rows), :]), (ra, r_buf.at[pl.ds(0, rows), :])]
    sources += both_halves(role, half_rows, [(xb, xbo, x_buf, rows)]) + [(pb, p_buf.at[pl.ds(rows, rows), :]), (rb, r_buf.at[pl.ds(rows, rows), :])]
    sources += unit_copies(w_up, w_down, up_buf, down_buf, role + 2 * x)
    sources += both_halves(role, half_rows, [(dya, dyao, dy_buf, 0), (dyb, dybo, dy_buf, rows)])
    copies = copy_all(sources, sems)
    count = len(sources)
    for u in range(2):
        gain, shift = table_rows(gains_ref, shifts_ref, (facts_a, facts_b)[u][1], 1)
        for i in range(4):
            copies[4 * u + i].wait()

        def norm(i, carry):
            at = pl.multiple_of(u * rows + i * LANE, LANE)
            here = pl.ds(at, LANE)
            residual = x_buf[here, :].astype(F32) + (p_buf[here, :].astype(F32) + r_buf[here, :].astype(F32))
            unit, _ = norm_stats(residual)
            hidden = (unit * gain + shift).astype(BF16)
            h_ref[here, :] = hidden
            ht_buf[:, here] = hidden.T
            if u == 0:
                per = half_rows // LANE

                @pl.when(i // per == role)
                def _():
                    res_ref[pl.ds(pl.multiple_of((i % per) * LANE, LANE), LANE), :] = residual

            return carry

        lax.fori_loop(0, rows // LANE, norm, 0)
    writes = [pltpu.make_async_copy(s, t, sems.at[count + i]) for i, (s, t) in enumerate(((h_ref, h_any), (res_ref, res_any), (act_ref, act_any), (dup_ref, dup_any), (gu_ref.at[pl.ds(kept[0], kept[1] - kept[0]), :], gu_any)))]
    writes[0].start()
    writes[1].start()
    for each in copies[8:]:
        each.wait()

    def block(i, carry):
        cols = pl.ds(pl.multiple_of(i * 256, 256), 256)
        act, slope = gelu_parts(mm(h_ref[...], up_buf[:, cols]))
        act = act.astype(BF16)
        act_ref[:, cols] = act[:rows]
        dup_ref[:, cols] = (mm_nt(dy_buf[...], down_buf[cols, :]) * slope).astype(BF16)
        gd_ref[cols, :] = mm_tn(act, dy_buf[...]).astype(BF16)
        return carry

    lax.fori_loop(0, quarter // 256, block, 0)
    pieces = {"d": gd_ref, "u": gu_ref}
    wire_sems = sems.at[pl.ds(count + 5, plan_sems(plan))]
    wire_copies(plan, inner, pieces, targets, wire_sems, "start", "d")
    writes[2].start()
    writes[3].start()

    def wide(i, carry):
        cols = pl.ds(pl.multiple_of(i * 256, 256), 256)
        gu_ref[:, cols] = mm(ht_buf[...], dup_ref[:, cols]).astype(BF16)
        return carry

    lax.fori_loop(0, quarter // 256, wide, 0)
    wire_copies(plan, inner, pieces, targets, wire_sems, "start", "u")
    writes[4].start()
    wire_copies(plan, inner, pieces, targets, wire_sems, "wait")
    for each in writes:
        each.wait()


def own_units(plan, kept, scalars, facts, values, parts, came, dys, gains, shifts, w_up, w_down):
    rows, width = 2 * values[0].shape[0], values[0].shape[1]
    quarter = w_up.shape[1] // 4
    count = 8 + 2 * (quarter // LANE) + 4 + 5 + plan_sems(plan)
    big = lambda *s: pltpu.VMEM(s, BF16)
    shapes = plan_shapes(plan, width)
    return pl.pallas_call(
        functools.partial(own_kernel, plan, kept),
        in_specs=[SMEM] * 3 + [HBM] * 12 + [VMEM] * 2 + [HBM] * 2,
        out_specs=[HBM] * (5 + len(shapes)),
        out_shape=[full((2 * rows, width), BF16), full((rows, quarter), BF16), full((2 * rows, quarter), BF16), full((rows // 2, width), F32), full((kept[1] - kept[0], quarter), BF16)] + shapes,
        scratch_shapes=[big(2 * rows, width)] * 4
        + [big(width, quarter), big(quarter, width), big(width, 2 * rows), big(2 * rows, width), big(quarter, width), big(width, quarter), big(rows, quarter), big(2 * rows, quarter), pltpu.VMEM((rows // 2, width), F32), pltpu.SemaphoreType.DMA((count,))],
        compiler_params=params(60),
        cost_estimate=cost(20e9, 8e6),
        name="own_units",
    )(scalars, *facts, *values, parts[0], came[0], parts[1], came[1], *dys, gains, shifts, w_up, w_down)


def rest_kernel(scalars, h_any, dya, dyao, dyb, dybo, act_any, dup_any, res_ref, w_up, w_down, dh_ref, keep_ref, send_ref,
                h_buf, dy_buf, act_own, act_buf, dup_own, dup_buf, up_own, down_own, up_buf, down_buf, sems):
    role, x = scalars[0], scalars[1]
    rows = 2 * dya.shape[0]
    quarter = up_buf.shape[1]
    blocks = quarter // LANE
    copies = copy_all(
        [(h_any, h_buf)]
        + unit_copies(w_up, w_down, up_buf, down_buf, role + 2 * (1 - x))
        + both_halves(role, rows // 2, [(dya, dyao, dy_buf, 0), (dyb, dybo, dy_buf, rows)])
        + [(act_any, act_own), (dup_any, dup_own)]
        + unit_copies(w_up, w_down, up_own, down_own, role + 2 * x),
        sems,
    )
    first = 1 + 2 * blocks + 4
    for each in copies[:first]:
        each.wait()

    def block(i, carry):
        cols = pl.ds(pl.multiple_of(i * 256, 256), 256)
        act, slope = gelu_parts(mm(h_buf[...], up_buf[:, cols]))
        act_buf[:, cols] = act[:rows].astype(BF16)
        dup_buf[:, cols] = (mm_nt(dy_buf[...], down_buf[cols, :]) * slope).astype(BF16)
        return carry

    lax.fori_loop(0, quarter // 256, block, 0)
    for each in copies[first:]:
        each.wait()

    def back(i, carry):
        here = pl.ds(pl.multiple_of(i * 256, 256), 256)
        dh_ref[here, :] = (mm_nt(dup_own[here, :], up_own[...]) + mm_nt(dup_buf[here, :], up_buf[...])).astype(BF16)
        return carry

    lax.fori_loop(0, 2 * rows // 256, back, 0)
    keep = pl.ds(pl.multiple_of(role * (rows // 2), rows // 2), rows // 2)
    send = pl.ds(pl.multiple_of((1 - role) * (rows // 2), rows // 2), rows // 2)
    keep_ref[...] = res_ref[...] + (mm(act_own[keep, :], down_own[...]) + mm(act_buf[keep, :], down_buf[...]))
    send_ref[...] = (mm(act_own[send, :], down_own[...]) + mm(act_buf[send, :], down_buf[...])).astype(BF16)


def rest_units(scalars, hidden, dys, act, dup, residual, w_up, w_down):
    rows, width = 2 * dys[0].shape[0], dys[0].shape[1]
    quarter = w_up.shape[1] // 4
    count = 7 + 4 * (quarter // LANE)
    big = lambda *s: pltpu.VMEM(s, BF16)
    return pl.pallas_call(
        rest_kernel,
        in_specs=[SMEM] + [HBM] * 7 + [VMEM] + [HBM] * 2,
        out_specs=[VMEM] * 3,
        out_shape=[full((2 * rows, width), BF16), full((rows // 2, width), F32), full((rows // 2, width), BF16)],
        scratch_shapes=[big(2 * rows, width)] * 2 + [big(rows, quarter)] * 2 + [big(2 * rows, quarter)] * 2 + [big(width, quarter), big(quarter, width)] * 2 + [pltpu.SemaphoreType.DMA((count,))],
        compiler_params=params(60),
        cost_estimate=cost(20e9, 8e6),
        name="rest_units",
    )(scalars, hidden, *dys, act, dup, residual, w_up, w_down)


def pair_back(qkv, lse, datt, c, c_d, rows, half, length):
    q, k, v = (qkv[:, pl.ds(i * half + c, LANE)] for i in range(3))
    grad = datt[:, pl.ds(c_d, LANE)]
    scaled, plain = head_masks(BF16, 0.125), head_masks(BF16, 1.0)
    dq = []
    dk, dv = [0.0, 0.0], [0.0, 0.0]
    for group in range(2):
        here = slice(group * rows, (group + 1) * rows)
        dq_here = 0.0
        for h in range(2):
            query, above = q[here] * scaled[h], grad[here] * plain[h]
            log_total = lse(h, here)
            probs, dprobs = [], []
            delta = 0.0
            for which in range(group + 1):
                there = slice(which * rows, (which + 1) * rows)
                scores = live_scores(k[there], query, length) if which == 0 else mm_nt(k[there], query)
                prob = jnp.exp(scores - log_total)
                dprob = mm_nt(v[there], above)
                delta = delta + jnp.sum(prob * dprob, axis=0, keepdims=True)
                dv[which] = dv[which] + mm(prob.astype(BF16), above)
                probs.append(prob)
                dprobs.append(dprob)
            for which in range(group + 1):
                there = slice(which * rows, (which + 1) * rows)
                dscore = (probs[which] * (dprobs[which] - delta)).astype(BF16)
                dk[which] = dk[which] + mm(dscore, query)
                dq_here = dq_here + mm_tn(dscore, k[there] * scaled[h])
        dq.append(dq_here)
    return dq, dk, dv


def turn_kernel(plan, scalars, facts_a, facts_b, xa, xao, xb, xbo, pa, ra, pb, rb, dh_any, dhr_any, dya, dyao, dyb, dybo, gains_ref, shifts_ref, w_out, att_a, att_b, gu_any, *refs):
    dr_any, vec_ref, datt_any, go_any = refs[:4]
    targets = refs[4:-14]
    x_buf, p_buf, r_buf, dh_buf, dhr_buf, dy_buf, da_buf, o_buf, datt_buf, att_buf, gu_buf, dr_ref, go_ref, sems = refs[-14:]
    role, x, inner = scalars[0], scalars[1], scalars[2]
    rows, width = xa.shape
    rows2, half = 2 * rows, width // 2
    quarter = half // 2
    own = pl.multiple_of(x * quarter, LANE)
    col = pl.multiple_of(role * half, LANE)
    pairs = []
    for u, (xs, xo, ps, rs, dys, dyo) in enumerate(((xa, xao, pa, ra, dya, dyao), (xb, xbo, pb, rb, dyb, dybo))):
        here = pl.ds(u * rows2, rows2)
        pairs += both_halves(role, rows, [(xs, xo, x_buf, u * rows2), (dys, dyo, dy_buf, u * rows2)])
        pairs += [(ps, p_buf.at[here, :]), (rs, r_buf.at[here, :]), (dh_any.at[here, :], dh_buf.at[here, :]), (dhr_any.at[here, :], dhr_buf.at[here, :])]
    pairs.append((w_out.at[pl.ds(col, half), :], o_buf))
    for u, a in enumerate((att_a, att_b)):
        pairs.append((a.at[:, pl.ds(own, quarter)], att_buf.at[pl.ds(u * rows2, rows2), :]))
    pairs.append((gu_any, gu_buf))
    copies = copy_all(pairs, sems)
    count = len(pairs)
    vec_ref[...] = jnp.zeros_like(vec_ref)
    for u in range(2):
        gain, _ = table_rows(gains_ref, shifts_ref, (facts_a, facts_b)[u][1], 1)
        for i in range(8):
            copies[8 * u + i].wait()

        def norm(i, carry):
            here = pl.ds(pl.multiple_of(u * rows2 + i * LANE, LANE), LANE)
            residual = x_buf[here, :].astype(F32) + (p_buf[here, :].astype(F32) + r_buf[here, :].astype(F32))
            unit, rstd = norm_stats(residual)
            dh2 = dh_buf[here, :].astype(F32) + dhr_buf[here, :].astype(F32)
            grad = dy_buf[here, :].astype(F32) + norm_back(unit, rstd, gain, dh2)
            da_buf[here, :] = grad.astype(BF16)
            if u == 0:
                per = rows // LANE

                @pl.when(i // per == role)
                def _():
                    dr_ref[pl.ds(pl.multiple_of((i % per) * LANE, LANE), LANE), :] = grad
                    vec_ref[0:1, :] += jnp.sum(dh2 * unit, axis=0, keepdims=True)
                    vec_ref[1:2, :] += jnp.sum(dh2, axis=0, keepdims=True)

            return carry

        lax.fori_loop(0, rows2 // LANE, norm, 0)
    writes = [pltpu.make_async_copy(s, t, sems.at[count + i]) for i, (s, t) in enumerate(((dr_ref, dr_any), (go_ref, go_any), (datt_buf, datt_any)))]
    writes[0].start()
    for each in copies[16:]:
        each.wait()
    go_ref[...] = mm_tn(att_buf[...], da_buf[...]).astype(BF16)
    writes[1].start()
    wire_sems = sems.at[pl.ds(count + 3, max(1, plan_sems(plan)))]
    wire_copies(plan, inner, {"o": go_ref, "u": gu_buf}, targets, wire_sems, "start")
    datt_buf[...] = mm_nt(da_buf[...], o_buf[...]).astype(BF16)
    writes[2].start()
    wire_copies(plan, inner, {"o": go_ref, "u": gu_buf}, targets, wire_sems, "wait")
    for each in writes:
        each.wait()


def turn(plan, scalars, facts, values, parts, came, dh, dh_came, dys, gains, shifts, w_out, atts, grad_up):
    rows2, width = 2 * values[0].shape[0], values[0].shape[1]
    half = width // 2
    big = lambda *s: pltpu.VMEM(s, BF16)
    tokens = 2 * rows2
    shapes = plan_shapes(plan, width)
    return pl.pallas_call(
        functools.partial(turn_kernel, plan),
        in_specs=[SMEM] * 3 + [HBM] * 14 + [VMEM] * 2 + [HBM] * 4,
        out_specs=[HBM, VMEM, HBM, HBM] + [HBM] * len(shapes),
        out_shape=[full((rows2 // 2, width), F32), full((8, width), F32), full((tokens, half), BF16), full((half // 2, width), BF16)] + shapes,
        scratch_shapes=[big(tokens, width)] * 7
        + [big(half, width), big(tokens, half), big(tokens, half // 2), big(*grad_up.shape), pltpu.VMEM((rows2 // 2, width), F32), big(half // 2, width), pltpu.SemaphoreType.DMA((23 + max(1, plan_sems(plan)),))],
        compiler_params=params(60),
        cost_estimate=cost(12e9, 8e6),
        name="turn",
    )(scalars, *facts, *values, parts[0], came[0], parts[1], came[1], dh, dh_came, *dys, gains, shifts, w_out, *atts, grad_up)


def back_kernel(plan, scalars, facts_a, facts_b, datt_any, qkv_a, qkv_b, ht_a, ht_b, go_any, lse_a, lse_b, *refs):
    dqa_any = refs[0]
    targets = refs[1:-7]
    datt_buf, qkv_buf, ht_buf, dq_buf, gq_ref, go_buf, sems = refs[-7:]
    x, inner = scalars[1], scalars[2]
    tokens, half = datt_any.shape
    rows2 = tokens // 2
    rows, quarter = rows2 // 2, half // 2
    own = pl.multiple_of(x * quarter, LANE)
    lse = (lse_a, lse_b)
    first_half, second_half = pl.ds(0, rows2), pl.ds(rows2, rows2)
    pairs = []
    for here, q in ((first_half, qkv_a), (second_half, qkv_b)):
        pairs += [(q, qkv_buf.at[here, :]), (datt_any.at[here, :], datt_buf.at[here, :])]
    pairs += [(ht_a, ht_buf.at[:, first_half]), (ht_b, ht_buf.at[:, second_half]), (go_any, go_buf)]
    copies = copy_all(pairs, sems)
    count = len(pairs)
    for u in range(2):
        copies[2 * u].wait()
        copies[2 * u + 1].wait()
        base = u * rows2
        length = (facts_a, facts_b)[u][0]

        def one(at, carry):
            c = pl.multiple_of(own + at * LANE, LANE)
            to = pl.multiple_of(at * LANE, LANE)
            first = (own + at * LANE) // HEAD
            look = lambda h, here: lse[u][pl.ds(first + h, 1), here]
            dq, dk, dv = pair_back(qkv_buf.at[pl.ds(base, rows2), :], look, datt_buf.at[pl.ds(base, rows2), :], c, c, rows, half, length)
            for i, halves in enumerate((dq, dk, dv)):
                for g in range(2):
                    dq_buf[base + g * rows : base + (g + 1) * rows, pl.ds(i * quarter + to, LANE)] = halves[g].astype(BF16)
            return carry

        lax.fori_loop(0, quarter // LANE, one, 0)
    write = pltpu.make_async_copy(dq_buf.at[first_half, :], dqa_any, sems.at[count])
    write.start()
    for each in copies[4:]:
        each.wait()
    for i in range(3):
        cols = slice(i * quarter, (i + 1) * quarter)
        gq_ref[:, cols] = mm(ht_buf[...], dq_buf[:, cols]).astype(BF16)
    pieces = {"q": gq_ref, "o": go_buf}
    wire_sems = sems.at[pl.ds(count + 1, plan_sems(plan))]
    wire_copies(plan, inner, pieces, targets, wire_sems, "start")
    wire_copies(plan, inner, pieces, targets, wire_sems, "wait")
    write.wait()


def back(plan, scalars, facts, datt, qkvs, hts, grad_out, lses):
    tokens, half = datt.shape
    width = 2 * half
    big = lambda *s: pltpu.VMEM(s, BF16)
    shapes = plan_shapes(plan, width)
    return pl.pallas_call(
        functools.partial(back_kernel, plan),
        in_specs=[SMEM] * 3 + [HBM] * 6 + [VMEM] * 2,
        out_specs=[HBM] * (1 + len(shapes)),
        out_shape=[full((tokens // 2, 3 * half // 2), BF16)] + shapes,
        scratch_shapes=[big(tokens, half), big(tokens, 3 * half), big(width, tokens), big(tokens, 3 * half // 2), big(width, 3 * half // 2), big(*grad_out.shape), pltpu.SemaphoreType.DMA((8 + plan_sems(plan),))],
        compiler_params=params(60),
        cost_estimate=cost(14e9, 8e6),
        name="back",
    )(scalars, *facts, datt, *qkvs, *hts, grad_out, *lses)


def last_kernel(scalars, facts, qkv_ref, lse_ref, datt_ref, dqa_ref, w_qkv, keep_ref, send_ref, w_own, w_buf, dq_buf, sems):
    role, x, length = scalars[0], scalars[1], facts[0]
    rows2, half = qkv_ref.shape[0], datt_ref.shape[1]
    rows, quarter, width = rows2 // 2, half // 2, 2 * half
    mine = pl.multiple_of(x * quarter, LANE)
    other = pl.multiple_of((1 - x) * quarter, LANE)
    col = pl.multiple_of(role * half, LANE)
    copies = copy_all(
        [(w_qkv.at[:, pl.ds(i * width + col + from_, quarter)], to.at[:, pl.ds(i * quarter, quarter)]) for from_, to in ((mine, w_own), (other, w_buf)) for i in range(3)],
        sems,
    )

    def one(at, carry):
        c = pl.multiple_of(other + at * LANE, LANE)
        to = pl.multiple_of(at * LANE, LANE)
        first = (other + at * LANE) // HEAD
        look = lambda h, here: lse_ref[pl.ds(first + h, 1), here]
        dq, dk, dv = pair_back(qkv_ref, look, datt_ref, c, c, rows, half, length)
        for i, halves in enumerate((dq, dk, dv)):
            for g in range(2):
                dq_buf[g * rows : (g + 1) * rows, pl.ds(i * quarter + to, LANE)] = halves[g].astype(BF16)
        return carry

    lax.fori_loop(0, quarter // LANE, one, 0)
    for each in copies:
        each.wait()
    keep = pl.ds(pl.multiple_of(role * rows, rows), rows)
    send = pl.ds(pl.multiple_of((1 - role) * rows, rows), rows)
    keep_ref[...] = mm_nt(dqa_ref[keep, :], w_own[...]) + mm_nt(dq_buf[keep, :], w_buf[...])
    send_ref[...] = (mm_nt(dqa_ref[send, :], w_own[...]) + mm_nt(dq_buf[send, :], w_buf[...])).astype(BF16)


def last(scalars, facts, qkv, lse, datt, dqa, w_qkv):
    rows2, half = qkv.shape[0], datt.shape[1]
    width = 2 * half
    big = lambda *s: pltpu.VMEM(s, BF16)
    return pl.pallas_call(
        last_kernel,
        in_specs=[SMEM] * 2 + [VMEM] * 4 + [HBM],
        out_specs=[VMEM] * 2,
        out_shape=[full((rows2 // 2, width), F32), full((rows2 // 2, width), BF16)],
        scratch_shapes=[big(width, 3 * half // 2)] * 2 + [big(rows2, 3 * half // 2), pltpu.SemaphoreType.DMA((6,))],
        compiler_params=params(60),
        cost_estimate=cost(7e9, 8e6),
        name="last",
    )(scalars, facts, qkv, lse, datt, dqa, w_qkv)


class Layout:
    def __init__(self, width, ff, sections, members):
        self.width, self.ff, self.members = width, ff, members
        shapes = {"q": (width, 3 * width), "o": (width, width), "u": (width, ff), "d": (ff, width), "s": (4 * sections, width)}
        start, self.spans = 0, {}
        for name, (rows, columns) in shapes.items():
            self.spans[name] = (start, rows, columns)
            start += rows * columns
        self.total = start
        self.share = start // members
        self.segments = [self.parts_of(m) for m in range(members)]
        self.rows = max(s[-1]["at"] + s[-1]["wire"] for s in self.segments)

    def span(self, member, name):
        start, rows, columns = self.spans[name]
        low = max(member * self.share, start) - start
        high = min((member + 1) * self.share, start + rows * columns) - start
        return (low, high) if low < high else None

    def parts_of(self, member):
        parts, at = [], 0
        for name in ("q", "o", "u", "d"):
            found = self.span(member, name)
            if found is None:
                continue
            columns = self.spans[name][2]
            low, high = found[0] // columns, -(-found[1] // columns)
            if name == "o":
                held = [r % (self.width // 4) for r in range(low, high)]
                low, high = min(held), max(held) + 1
            if name == "d":
                held = [r // (4 * LANE) * LANE + r % LANE for r in range(low, high)]
                low, high = min(held), max(held) + 1
            low, high = low // 16 * 16, -(-high // 16) * 16
            count = high - low
            wire = -(-(3 * count // 4) // 16) * 16 if name == "q" else count
            parts.append({"name": name, "low": low, "high": high, "at": at, "wire": wire})
            at += wire
        return parts

    def table(self):
        rows = []
        for share in range(2 * self.members):
            entry = [share * (self.share // 2) // LANE]
            held = {p["name"]: p for p in self.segments[share // 2]}
            for name in ("q", "o", "u", "d"):
                p = held.get(name)
                entry += [p["low"], p["high"], p["at"], p["wire"]] if p else [0, 0, 0, 0]
            rows.append(entry + [0] * (24 - len(entry)))
        return np.asarray(rows, np.int32)

    def regions(self, member, low, high):
        found = []

        def cut(name, row, column, rows, columns, to_row, to_column):
            first, last = max(to_row, low), min(to_row + rows, high)
            if first < last:
                found.append((name, row + first - to_row, column, last - first, columns, first - low, to_column))

        for p in self.segments[member]:
            if p["name"] == "q":
                quarter = self.width // 4
                side = p["high"] - p["low"] - p["wire"]
                cut("q", p["low"], 0, p["wire"], 3 * quarter, p["at"], 0)
                for i in range(3):
                    cut("q", p["low"] + p["wire"], i * quarter, side, quarter, p["at"] + i * side, 3 * quarter)
            else:
                cut(p["name"], p["low"], 0, p["wire"], self.width, p["at"], 0)
        return found

    def plans(self):
        stage_of = {"u": 0, "d": 0, "o": 1, "q": 2}
        stages = ([], [], [])
        for block in reversed(range(self.members // 2)):
            edges = {0, self.rows}
            for member in (2 * block, 2 * block + 1):
                for p in self.segments[member]:
                    edges |= {p["at"], p["at"] + p["wire"]}
            edges = sorted(edges)
            runs = []
            for low, high in zip(edges, edges[1:]):
                found = [stage_of[f[0]] for member in (2 * block, 2 * block + 1) for f in self.regions(member, low, high)]
                stage = max(found) if found else runs[-1][2]
                if runs and (runs[-1][2] == stage or 2 in (stage, runs[-1][2])):
                    runs[-1][1], runs[-1][2] = high, max(stage, runs[-1][2])
                else:
                    runs.append([low, high, stage])
            for low, high, stage in runs:
                middle = low + (high - low) // 32 * 16
                for first, last in [(low, middle), (middle, high)] if stage == 2 else [(low, high)]:
                    regions = [self.regions(2 * block + i, first, last) for i in range(2)]
                    stages[stage].append({"block": block, "low": first, "high": last, "regions": regions, "most": max(map(len, regions))})
        return stages


def after(value, *first):
    return lax.optimization_barrier((value, *first))[0]


def add(left, right):
    return (left.astype(F32) + right.astype(F32)).astype(BF16)


def tree_pairs(block, level, count):
    size = 2 << level
    pairs = []
    for low in range(0, count, size):
        middle, high = low + size // 2, low + size
        left, right = min(max(block, low), middle - 1), min(max(block, middle), high - 1)
        source, target = (right, left) if block < middle else (left, right)
        pairs += [(2 * source + y, 2 * target + y) for y in range(2)]
    return pairs


def place_kernel(spans, table, *refs):
    quad, (small_ref, out_ref, wire, flat, sems) = refs[:-5], refs[-5:]
    me, unit0 = table[24], table[0]
    units = out_ref.shape[0]
    width = wire.shape[2]
    chunks = width // LANE
    front = 512
    x, role = me // 2, me % 2
    where = (me, role + 2 * (1 - x), (1 - role) + 2 * x, (1 - role) + 2 * (1 - x))
    per_piece = len(quad) // 4
    pairs = []
    for i, source in enumerate(quad):
        rows = source.shape[0]
        first = sum(s.shape[0] for s in quad[i // per_piece * per_piece : i])
        pairs.append((source, wire.at[where[i // per_piece], pl.ds(first, rows), :]))
    copies = copy_all(pairs, sems.at[pl.ds(1, len(pairs))])
    for each in copies:
        each.wait()

    def rows_of(name, per_row):
        at = 1 + 4 * "qoud".index(name)
        low, high = table[at], table[at + 1]
        base = unit0 - spans[name][0] // LANE
        first = jnp.maximum(low // 16, jnp.maximum(base, 0) // per_row // 16)
        last = jnp.minimum(high // 16, (jnp.maximum(base + units, 0) + per_row * 16 - 1) // (per_row * 16))
        return low, first, last, table[at + 2], table[at + 3], base

    low, first, last, at, n1, base = rows_of("q", 3 * chunks)
    n2 = table[2] - table[1] - n1

    def qkv(g, carry):
        row = g * 16 - low
        to = front + g * 16 * 3 * chunks - base
        beside = row >= n1
        half = chunks // 4
        for section in range(3):
            source = jnp.where(beside, at + section * n2 + row - n1, at + row)
            for h in range(half):
                column = pl.multiple_of(jnp.where(beside, 3 * width // 4 + h * LANE, section * (width // 4) + h * LANE), LANE)
                for piece in range(4):
                    unit = section * chunks + (piece % 2) * (chunks // 2) + (piece // 2) * half + h
                    flat[pl.ds(to + unit, 16, stride=3 * chunks), :] = wire[piece, pl.ds(pl.multiple_of(source, 16), 16), pl.ds(column, LANE)].astype(F32)
        return carry

    lax.fori_loop(first, jnp.maximum(first, last), qkv, 0)
    per = spans["u"][2] // LANE
    low, first, last, at, _, base = rows_of("u", per)

    def up(g, carry):
        source = pl.multiple_of(at + g * 16 - low, 16)
        to = front + g * 16 * per - base
        for h in range(chunks):
            for piece in range(4):
                flat[pl.ds(to + 4 * h + piece, 16, stride=per), :] = wire[piece, pl.ds(source, 16), h * LANE : (h + 1) * LANE].astype(F32)
        return carry

    lax.fori_loop(first, jnp.maximum(first, last), up, 0)

    for name in ("o", "d"):
        slot = 1 + 4 * "qoud".index(name)
        low, high, at = table[slot], table[slot + 1], table[slot + 2]
        base = unit0 - spans[name][0] // LANE

        def rows(g, carry):
            row = g * 16
            source = pl.multiple_of(at + row - low, 16)
            for piece in range(4):
                if name == "o":
                    line = (piece % 2) * (width // 2) + (piece // 2) * (width // 4) + row
                else:
                    line = (row // LANE) * (4 * LANE) + piece * LANE + row % LANE
                to = line * chunks - base

                @pl.when((to + 16 * chunks > 0) & (to < units))
                def _():
                    for h in range(chunks):
                        flat[pl.ds(front + to + h, 16, stride=chunks), :] = wire[piece, pl.ds(source, 16), h * LANE : (h + 1) * LANE].astype(F32)

            return carry

        lax.fori_loop(low // 16, high // 16, rows, 0)

    tail = spans["s"][0] // LANE - unit0

    @pl.when(tail < units)
    def _():
        for g in range(small_ref.shape[0] // 8):
            for h in range(chunks):
                flat[pl.ds(front + tail + g * 8 * chunks + h, 8, stride=chunks), :] = small_ref[g * 8 : (g + 1) * 8, h * LANE : (h + 1) * LANE]

    done = pltpu.make_async_copy(flat.at[pl.ds(front, units), :], out_ref, sems.at[0])
    done.start()
    done.wait()


def place(layout, table, quad, small):
    rows, width = layout.rows, layout.width
    units = layout.share // 2 // LANE
    quad = [part for piece in quad for part in piece]
    return pl.pallas_call(
        functools.partial(place_kernel, layout.spans),
        in_specs=[SMEM] + [HBM] * len(quad) + [VMEM],
        out_specs=HBM,
        out_shape=full((units, LANE), F32),
        scratch_shapes=[pltpu.VMEM((4, rows, width), BF16), pltpu.VMEM((-(-units // 8) * 8 + 1024, LANE), F32), pltpu.SemaphoreType.DMA((1 + len(quad),))],
        compiler_params=params(60),
        cost_estimate=cost(4e9, 8e6),
        name="place",
    )(table, *quad, small)


def local(frames, cotangent, w_qkv, w_out, w_up, w_down, gains, shifts, prompt_len, section):
    width, ff, sections = frames.shape[3], w_up.shape[1], gains.shape[0]
    role, group, member = lax.axis_index("role"), lax.axis_index("group"), lax.axis_index("member")
    x = group % 2
    members, groups = lax.axis_size("member"), lax.axis_size("group")
    layout = Layout(width, ff, sections, members)
    early, middle, late = layout.plans()
    outer, inner = member // 2, member % 2
    count = members // 2

    own_frames, own_cot = frames[0, 0], cotangent[0, 0]
    values = [own_frames, swap(own_frames, "role")]
    mate_frames = swap(own_frames, "group")
    facts = jnp.concatenate([prompt_len, section])
    mate_facts = swap(facts, "group")
    scalars = jnp.stack([role, x, inner]).astype(jnp.int32)

    levels = count.bit_length() - 1
    kept = span_of(middle, "u")
    chunks = []

    def exchange(plan, arrays, *first):
        for i, chunk in enumerate(plan):
            keep, send = arrays[2 * i], arrays[2 * i + 1]
            chunks.append(dict(chunk, total=keep, came=swap(after(send, *first) if first else send, "member"), level=0))

    def climb(chunk):
        chunk["came"] = lax.ppermute(chunk["total"], "member", tree_pairs(chunk["block"], chunk["level"], count))
        chunk["level"] += 1

    def settle(chunk, *first):
        total = after(chunk["total"], *first) if first else chunk["total"]
        chunk["total"] = add(total, chunk["came"])

    first = attend(scalars, facts, values[:2], gains, shifts, w_qkv, w_out)
    mate_facts, mate_frames = after(mate_facts, first[3]), after(mate_frames, first[3])
    both = (facts, mate_facts)
    values += [mate_frames, swap(mate_frames, "role")]
    own_cot = after(own_cot, mate_frames)
    mate_cot = swap(own_cot, "group")
    dys = [own_cot, swap(own_cot, "role"), mate_cot, swap(mate_cot, "role")]
    second = attend(scalars, mate_facts, values[2:], gains, shifts, w_qkv, w_out)
    hts, qkvs, atts, parts, lses = zip(first, second)
    came = [after(swap(parts[0], "role"), parts[1]), swap(parts[1], "role")]
    hidden, act, dup, residual, grad_up, *wires = own_units(early, kept, scalars, both, values, parts, came, dys, gains, shifts, w_up, w_down)
    exchange(early, wires)
    dh, out_keep, out_send = rest_units(scalars, hidden, dys, act, dup, residual, w_up, w_down)
    output = (out_keep + swap(out_send, "role").astype(F32)).astype(BF16)
    dh_came = swap(after(dh, chunks[0]["came"]), "role")
    settle(chunks[0], dh)
    climb(chunks[0])
    dr1, vec_two, datt, grad_out, *wires = turn(shifted(middle, "u", kept[0]), scalars, both, values, parts, came, dh, dh_came, dys, gains, shifts, w_out, atts, grad_up)
    exchange(middle, wires)
    second_chunk = chunks[min(1, len(early) - 1)]
    if second_chunk is not chunks[0]:
        pass
    dqa, *wires = back(late, scalars, both, datt, qkvs, hts, grad_out, lses)
    exchange(late, wires, *(c["came"] for c in chunks[len(early) :]))
    if second_chunk is not chunks[0]:
        settle(second_chunk, dqa)
        climb(second_chunk)
    for chunk in chunks[: min(2, len(early))]:
        settle(chunk, dqa)
    joined = chunks[: min(2, len(early))]
    for chunk in chunks[min(2, len(early)) :]:
        settle(chunk, dqa)
        mates = [c for c in joined if c["block"] == chunk["block"] and c["level"] == 0 and (chunk["high"] == c["low"] or chunk["low"] == c["high"])]
        if mates and not any(chunk is c for c in chunks[-len(late) :]):
            ends = sorted((mates[0], chunk), key=lambda c: c["low"])
            mates[0]["total"] = jnp.concatenate([c["total"] for c in ends], 0)
            mates[0]["low"], mates[0]["high"] = ends[0]["low"], ends[1]["high"]
        else:
            joined.append(chunk)
    chunks = joined
    dh1_keep, dh1_send = last(scalars, facts, qkvs[0], lses[0], after(datt, chunks[-1]["total"]), dqa, w_qkv)
    dh1 = dh1_keep + swap(dh1_send, "role").astype(F32)
    unit, rstd = norm_stats(own_frames.astype(F32))
    input_grad = dr1 + norm_back(unit, rstd, lax.dynamic_slice(gains, (facts[1], 0, 0), (1, 1, width))[0].astype(F32), dh1)

    vectors = jnp.stack([jnp.stack([jnp.sum(dh1 * unit, 0), vec_two[0]]), jnp.stack([jnp.sum(dh1, 0), vec_two[1]])])
    select = (jnp.arange(sections, dtype=jnp.int32) == facts[1]).astype(F32)
    small = select[None, :, None, None] * vectors[:, None]
    small = jnp.pad(small.reshape(4 * sections, width), ((0, -4 * sections % 8), (0, 0)))
    small_steps = []
    for axis in ("role", "group", "member"):
        distance = 1
        while distance < lax.axis_size(axis):
            small = small + swap(small, axis, distance)
            small_steps.append(small)
            distance *= 2

    for chunk in chunks:
        if chunk["level"] == 0:
            climb(chunk)
            settle(chunk)
    for level in range(1, levels):
        for i, chunk in enumerate(chunks):
            if level == levels - 1 and i >= len(chunks) - 2:
                chunk["total"] = after(chunk["total"], small_steps[-3 if i == len(chunks) - 2 else -2])
            climb(chunk)
            settle(chunk)
    edges = [0, layout.rows // 32 * 16, layout.rows]
    quads = [[], [], [], []]
    for low, high in zip(edges, edges[1:]):
        final = jnp.zeros((high - low, width), BF16)
        for chunk in chunks:
            first, past = max(low, chunk["low"]), min(high, chunk["high"])
            if first >= past:
                continue
            here = chunk["total"][first - chunk["low"] : past - chunk["low"]]
            part = jnp.where(outer == chunk["block"], here, final[first - low : past - low])
            final = jnp.concatenate([final[: first - low], part, final[past - low :]], 0)
        distance = 2
        while distance < groups:
            final = add(final, swap(final, "group", distance))
            distance *= 2
        if high == layout.rows:
            final = after(final, small, quads[1][0])
        mate = swap(final, "group")
        for into, value in zip(quads, (final, mate, swap(final, "role"), swap(mate, "role"))):
            into.append(value)
    table = lax.dynamic_slice(jnp.asarray(layout.table()), (2 * member + role, 0), (1, 24))[0]
    table = jnp.concatenate([table, (role + 2 * x)[None].astype(jnp.int32), jnp.zeros((7,), jnp.int32)])
    shard = place(layout, table, quads, small).reshape(-1)
    return output[None, None], input_grad[None, None], shard


def solution(mesh):
    rows = P(("group", "member"), "role", None, None)
    per_seq = P(("group", "member"))
    return jax.shard_map(
        local,
        mesh=mesh,
        in_specs=(rows, rows, P(), P(), P(), P(), P(), P(), per_seq, per_seq),
        out_specs=(rows, rows, P(("member", "role"))),
        check_vma=False,
    )
```

```python
import functools

import jax
import jax.numpy as jnp
import numpy as np
from jax import lax
from jax.experimental import pallas as pl
from jax.experimental.pallas import tpu as pltpu
from jax.sharding import PartitionSpec as P

HEADS = 16
LANE = 128
HEAD = 64
F32 = jnp.float32
BF16 = jnp.bfloat16


def dot(left, right, dims):
    return lax.dot_general(left, right, (dims, ((), ())), preferred_element_type=F32)


def mm(left, right):
    return dot(left, right, ((1,), (0,)))


def mm_nt(left, right):
    return dot(left, right, ((1,), (1,)))


def mm_tn(left, right):
    return dot(left, right, ((0,), (0,)))


def swap(value, axis, distance=1):
    count = lax.axis_size(axis)
    return lax.ppermute(value, axis, [(i, i ^ distance) for i in range(count)])


def norm_stats(values):
    center = values - jnp.mean(values, axis=-1, keepdims=True)
    rstd = lax.rsqrt(jnp.mean(center * center, axis=-1, keepdims=True) + 1e-05)
    return center * rstd, rstd


def norm_back(unit, rstd, gain, grad):
    grad_unit = grad * gain
    inner = grad_unit - jnp.mean(grad_unit, axis=-1, keepdims=True)
    return rstd * (inner - unit * jnp.mean(grad_unit * unit, axis=-1, keepdims=True))


def full(shape, dtype):
    return jax.ShapeDtypeStruct(shape, dtype)


def params(mib):
    return pltpu.CompilerParams(vmem_limit_bytes=mib * 2**20)


def cost(flops, moved):
    return pl.CostEstimate(flops=int(flops), bytes_accessed=int(moved), transcendentals=0)


HBM = pl.BlockSpec(memory_space=pltpu.HBM)
SMEM = pl.BlockSpec(memory_space=pltpu.SMEM)
VMEM = pl.BlockSpec(memory_space=pltpu.VMEM)


def copy_all(pairs, sems):
    copies = [pltpu.make_async_copy(source, target, sems.at[i]) for i, (source, target) in enumerate(pairs)]
    for each in copies:
        each.start()
    return copies


def head_masks(dtype, scale):
    lane = lax.broadcasted_iota(jnp.int32, (1, LANE), 1)
    return [jnp.where(lane // HEAD == h, scale, 0.0).astype(dtype) for h in range(2)]


def live_scores(key, query, length):
    scores = mm_nt(key, query)
    return jnp.where(lax.broadcasted_iota(jnp.int32, scores.shape, 0) < length, scores, -1e30)


def span_of(plan, name):
    rows = [edge for chunk in plan for regions in chunk["regions"] for r in regions if r[0] == name for edge in (r[1], r[1] + r[3])]
    return (min(rows), max(rows)) if rows else (0, 16)


def shifted(plan, name, by):
    move = lambda r: (r[0], r[1] - by, *r[2:]) if r[0] == name else r
    return [dict(chunk, regions=[[move(r) for r in regions] for regions in chunk["regions"]]) for chunk in plan]


def wire_copies(plan, inner, pieces, targets, sems, act, names="qoud"):
    for parity in range(2):

        @pl.when(inner == parity)
        def _():
            at = to = 0
            for chunk in plan:
                for regions in (chunk["regions"][parity], chunk["regions"][1 - parity]):
                    for i, (name, row, column, rows, columns, to_row, to_column) in enumerate(regions):
                        if name in names:
                            source = pieces[name].at[pl.ds(row, rows), pl.ds(column, columns)]
                            target = targets[to].at[pl.ds(to_row, rows), pl.ds(to_column, columns)]
                            getattr(pltpu.make_async_copy(source, target, sems.at[at + i]), act)()
                    at += chunk["most"]
                    to += 1


def plan_shapes(plan, width):
    return [full((chunk["high"] - chunk["low"], width), BF16) for chunk in plan for _ in range(2)]


def plan_sems(plan):
    return sum(2 * chunk["most"] for chunk in plan)


def table_rows(gains_ref, shifts_ref, section, which):
    return gains_ref[section, which : which + 1, :].astype(F32), shifts_ref[section, which : which + 1, :].astype(F32)


def attend_kernel(scalars, facts, own_any, other_any, gains_ref, shifts_ref, w_qkv, w_out, ht_any, qkv_any, att_any, part_any, lse_ref,
                  x_buf, w_buf, o_buf, h_buf, ht_ref, qkv_ref, att_ref, part_ref, sems):
    role, length = scalars[0], facts[0]
    gain, shift = table_rows(gains_ref, shifts_ref, facts[1], 0)
    width, half = w_out.shape[1], w_out.shape[0] // 2
    rows = own_any.shape[0]
    col = pl.multiple_of(role * half, LANE)
    mine, theirs = (pl.ds(pl.multiple_of(r * rows, rows), rows) for r in (role, 1 - role))
    copies = copy_all(
        [(own_any, x_buf.at[mine, :]), (other_any, x_buf.at[theirs, :])]
        + [(w_qkv.at[:, pl.ds(i * width + col, half)], w_buf.at[:, pl.ds(i * half, half)]) for i in range(3)]
        + [(w_out.at[pl.ds(col, half), :], o_buf)],
        sems,
    )
    copies[0].wait()
    copies[1].wait()
    for at in range(0, 2 * rows, LANE):
        unit, _ = norm_stats(x_buf[at : at + LANE, :].astype(F32))
        hidden = (unit * gain + shift).astype(BF16)
        h_buf[at : at + LANE, :] = hidden
        ht_ref[:, at : at + LANE] = hidden.T
    writes = [pltpu.make_async_copy(s, t, sems.at[6 + i]) for i, (s, t) in enumerate(((ht_ref, ht_any), (qkv_ref, qkv_any), (att_ref, att_any), (part_ref, part_any)))]
    writes[0].start()
    for i in range(3):
        copies[2 + i].wait()
        qkv_ref[:, i * half : (i + 1) * half] = mm(h_buf[...], w_buf[:, i * half : (i + 1) * half]).astype(BF16)
    writes[1].start()

    def pair(at, carry):
        c = pl.multiple_of(at * LANE, LANE)
        q, k, v = (qkv_ref[:, pl.ds(i * half + c, LANE)] for i in range(3))
        q_masks, v_masks = head_masks(BF16, 0.125), head_masks(BF16, 1.0)
        for group in range(2):
            total = 0.0
            for h in range(2):
                query = q[group * rows : (group + 1) * rows] * q_masks[h]
                scores = [live_scores(k[:rows], query, length)]
                if group:
                    scores.append(mm_nt(k[rows:], query))
                top = jnp.max(scores[0], axis=0, keepdims=True)
                if group:
                    top = jnp.maximum(top, jnp.max(scores[1], axis=0, keepdims=True))
                powers = [jnp.exp(s - top) for s in scores]
                below = sum(jnp.sum(p, axis=0, keepdims=True) for p in powers)
                lse_ref[pl.ds(2 * at + h, 1), group * rows : (group + 1) * rows] = top + jnp.log(below)
                inverse = 1.0 / below
                for which, p in enumerate(powers):
                    prob = (p * inverse).astype(BF16)
                    total = total + mm_tn(prob, v[which * rows : (which + 1) * rows] * v_masks[h])
            att_ref[group * rows : (group + 1) * rows, pl.ds(c, LANE)] = total.astype(BF16)
        return carry

    lax.fori_loop(0, half // LANE, pair, 0)
    writes[2].start()
    copies[5].wait()
    part_ref[...] = mm(att_ref[...], o_buf[...]).astype(BF16)
    writes[3].start()
    for each in writes:
        each.wait()


def attend(scalars, facts, halves, gains, shifts, w_qkv, w_out):
    rows, width = 2 * halves[0].shape[0], halves[0].shape[1]
    half = width // 2
    outs = [(width, rows), (rows, 3 * half), (rows, half), (rows, width)]
    return pl.pallas_call(
        attend_kernel,
        in_specs=[SMEM, SMEM, HBM, HBM, VMEM, VMEM, HBM, HBM],
        out_specs=[HBM] * 4 + [VMEM],
        out_shape=[full(s, BF16) for s in outs] + [full((half // HEAD, rows), F32)],
        scratch_shapes=[pltpu.VMEM((rows, width), BF16), pltpu.VMEM((width, 3 * half), BF16), pltpu.VMEM((half, width), BF16), pltpu.VMEM((rows, width), BF16)]
        + [pltpu.VMEM(s, BF16) for s in outs] + [pltpu.SemaphoreType.DMA((10,))],
        compiler_params=params(60),
        cost_estimate=cost(12e9, 8e6),
        name="attend",
    )(scalars, facts, *halves, gains, shifts, w_qkv, w_out)


def unit_copies(w_up, w_down, up_buf, down_buf, first):
    blocks = w_up.shape[1] // (4 * LANE)
    pairs = []
    for b in range(blocks):
        at = pl.multiple_of((4 * b + first) * LANE, LANE)
        pairs.append((w_up.at[:, pl.ds(at, LANE)], up_buf.at[:, pl.ds(b * LANE, LANE)]))
    for b in range(blocks):
        at = pl.multiple_of((4 * b + first) * LANE, LANE)
        pairs.append((w_down.at[pl.ds(at, LANE), :], down_buf.at[pl.ds(b * LANE, LANE), :]))
    return pairs


def gelu_parts(up):
    cdf = 0.5 + 0.5 * lax.erf(up * np.float32(0.5**0.5))
    slope = cdf + up * (jnp.exp(-0.5 * up * up) * np.float32(1 / np.sqrt(2 * np.pi)))
    return up * cdf, slope


def both_halves(role, rows, pairs):
    out = []
    for own, other, buffer, first in pairs:
        for source, r in ((own, role), (other, 1 - role)):
            out.append((source, buffer.at[pl.ds(pl.multiple_of(first + r * rows, rows), rows), :]))
    return out


def own_kernel(plan, kept, scalars, facts_a, facts_b, xa, xao, xb, xbo, pa, ra, pb, rb, dya, dyao, dyb, dybo, gains_ref, shifts_ref, w_up, w_down, *refs):
    h_any, act_any, dup_any, res_any, gu_any = refs[:5]
    targets = refs[5:-14]
    x_buf, p_buf, r_buf, dy_buf, up_buf, down_buf, ht_buf, h_ref, gd_ref, gu_ref, act_ref, dup_ref, res_ref, sems = refs[-14:]
    role, x, inner = scalars[0], scalars[1], scalars[2]
    half_rows = xa.shape[0]
    rows = 2 * half_rows
    quarter = up_buf.shape[1]
    sources = both_halves(role, half_rows, [(xa, xao, x_buf, 0)]) + [(pa, p_buf.at[pl.ds(0, rows), :]), (ra, r_buf.at[pl.ds(0, rows), :])]
    sources += both_halves(role, half_rows, [(xb, xbo, x_buf, rows)]) + [(pb, p_buf.at[pl.ds(rows, rows), :]), (rb, r_buf.at[pl.ds(rows, rows), :])]
    sources += unit_copies(w_up, w_down, up_buf, down_buf, role + 2 * x)
    sources += both_halves(role, half_rows, [(dya, dyao, dy_buf, 0), (dyb, dybo, dy_buf, rows)])
    copies = copy_all(sources, sems)
    count = len(sources)
    for u in range(2):
        gain, shift = table_rows(gains_ref, shifts_ref, (facts_a, facts_b)[u][1], 1)
        for i in range(4):
            copies[4 * u + i].wait()

        def norm(i, carry):
            at = pl.multiple_of(u * rows + i * LANE, LANE)
            here = pl.ds(at, LANE)
            residual = x_buf[here, :].astype(F32) + (p_buf[here, :].astype(F32) + r_buf[here, :].astype(F32))
            unit, _ = norm_stats(residual)
            hidden = (unit * gain + shift).astype(BF16)
            h_ref[here, :] = hidden
            ht_buf[:, here] = hidden.T
            if u == 0:
                per = half_rows // LANE

                @pl.when(i // per == role)
                def _():
                    res_ref[pl.ds(pl.multiple_of((i % per) * LANE, LANE), LANE), :] = residual

            return carry

        lax.fori_loop(0, rows // LANE, norm, 0)
    writes = [pltpu.make_async_copy(s, t, sems.at[count + i]) for i, (s, t) in enumerate(((h_ref, h_any), (res_ref, res_any), (act_ref, act_any), (dup_ref, dup_any), (gu_ref.at[pl.ds(kept[0], kept[1] - kept[0]), :], gu_any)))]
    writes[0].start()
    writes[1].start()
    for each in copies[8:]:
        each.wait()

    def block(i, carry):
        cols = pl.ds(pl.multiple_of(i * 256, 256), 256)
        act, slope = gelu_parts(mm(h_ref[...], up_buf[:, cols]))
        act = act.astype(BF16)
        act_ref[:, cols] = act[:rows]
        dup_ref[:, cols] = (mm_nt(dy_buf[...], down_buf[cols, :]) * slope).astype(BF16)
        gd_ref[cols, :] = mm_tn(act, dy_buf[...]).astype(BF16)
        return carry

    lax.fori_loop(0, quarter // 256, block, 0)
    pieces = {"d": gd_ref, "u": gu_ref}
    wire_sems = sems.at[pl.ds(count + 5, plan_sems(plan))]
    wire_copies(plan, inner, pieces, targets, wire_sems, "start", "d")
    writes[2].start()
    writes[3].start()

    def wide(i, carry):
        cols = pl.ds(pl.multiple_of(i * 256, 256), 256)
        gu_ref[:, cols] = mm(ht_buf[...], dup_ref[:, cols]).astype(BF16)
        return carry

    lax.fori_loop(0, quarter // 256, wide, 0)
    wire_copies(plan, inner, pieces, targets, wire_sems, "start", "u")
    writes[4].start()
    wire_copies(plan, inner, pieces, targets, wire_sems, "wait")
    for each in writes:
        each.wait()


def own_units(plan, kept, scalars, facts, values, parts, came, dys, gains, shifts, w_up, w_down):
    rows, width = 2 * values[0].shape[0], values[0].shape[1]
    quarter = w_up.shape[1] // 4
    count = 8 + 2 * (quarter // LANE) + 4 + 5 + plan_sems(plan)
    big = lambda *s: pltpu.VMEM(s, BF16)
    shapes = plan_shapes(plan, width)
    return pl.pallas_call(
        functools.partial(own_kernel, plan, kept),
        in_specs=[SMEM] * 3 + [HBM] * 12 + [VMEM] * 2 + [HBM] * 2,
        out_specs=[HBM] * (5 + len(shapes)),
        out_shape=[full((2 * rows, width), BF16), full((rows, quarter), BF16), full((2 * rows, quarter), BF16), full((rows // 2, width), F32), full((kept[1] - kept[0], quarter), BF16)] + shapes,
        scratch_shapes=[big(2 * rows, width)] * 4
        + [big(width, quarter), big(quarter, width), big(width, 2 * rows), big(2 * rows, width), big(quarter, width), big(width, quarter), big(rows, quarter), big(2 * rows, quarter), pltpu.VMEM((rows // 2, width), F32), pltpu.SemaphoreType.DMA((count,))],
        compiler_params=params(60),
        cost_estimate=cost(20e9, 8e6),
        name="own_units",
    )(scalars, *facts, *values, parts[0], came[0], parts[1], came[1], *dys, gains, shifts, w_up, w_down)


def rest_kernel(scalars, h_any, dya, dyao, dyb, dybo, act_any, dup_any, res_ref, w_up, w_down, dh_ref, keep_ref, send_ref,
                h_buf, dy_buf, act_own, act_buf, dup_own, dup_buf, up_own, down_own, up_buf, down_buf, sems):
    role, x = scalars[0], scalars[1]
    rows = 2 * dya.shape[0]
    quarter = up_buf.shape[1]
    blocks = quarter // LANE
    copies = copy_all(
        [(h_any, h_buf)]
        + unit_copies(w_up, w_down, up_buf, down_buf, role + 2 * (1 - x))
        + both_halves(role, rows // 2, [(dya, dyao, dy_buf, 0), (dyb, dybo, dy_buf, rows)])
        + [(act_any, act_own), (dup_any, dup_own)]
        + unit_copies(w_up, w_down, up_own, down_own, role + 2 * x),
        sems,
    )
    first = 1 + 2 * blocks + 4
    for each in copies[:first]:
        each.wait()

    def block(i, carry):
        cols = pl.ds(pl.multiple_of(i * 256, 256), 256)
        act, slope = gelu_parts(mm(h_buf[...], up_buf[:, cols]))
        act_buf[:, cols] = act[:rows].astype(BF16)
        dup_buf[:, cols] = (mm_nt(dy_buf[...], down_buf[cols, :]) * slope).astype(BF16)
        return carry

    lax.fori_loop(0, quarter // 256, block, 0)
    for each in copies[first:]:
        each.wait()

    def back(i, carry):
        here = pl.ds(pl.multiple_of(i * 256, 256), 256)
        dh_ref[here, :] = (mm_nt(dup_own[here, :], up_own[...]) + mm_nt(dup_buf[here, :], up_buf[...])).astype(BF16)
        return carry

    lax.fori_loop(0, 2 * rows // 256, back, 0)
    keep = pl.ds(pl.multiple_of(role * (rows // 2), rows // 2), rows // 2)
    send = pl.ds(pl.multiple_of((1 - role) * (rows // 2), rows // 2), rows // 2)
    keep_ref[...] = res_ref[...] + (mm(act_own[keep, :], down_own[...]) + mm(act_buf[keep, :], down_buf[...]))
    send_ref[...] = (mm(act_own[send, :], down_own[...]) + mm(act_buf[send, :], down_buf[...])).astype(BF16)


def rest_units(scalars, hidden, dys, act, dup, residual, w_up, w_down):
    rows, width = 2 * dys[0].shape[0], dys[0].shape[1]
    quarter = w_up.shape[1] // 4
    count = 7 + 4 * (quarter // LANE)
    big = lambda *s: pltpu.VMEM(s, BF16)
    return pl.pallas_call(
        rest_kernel,
        in_specs=[SMEM] + [HBM] * 7 + [VMEM] + [HBM] * 2,
        out_specs=[VMEM] * 3,
        out_shape=[full((2 * rows, width), BF16), full((rows // 2, width), F32), full((rows // 2, width), BF16)],
        scratch_shapes=[big(2 * rows, width)] * 2 + [big(rows, quarter)] * 2 + [big(2 * rows, quarter)] * 2 + [big(width, quarter), big(quarter, width)] * 2 + [pltpu.SemaphoreType.DMA((count,))],
        compiler_params=params(60),
        cost_estimate=cost(20e9, 8e6),
        name="rest_units",
    )(scalars, hidden, *dys, act, dup, residual, w_up, w_down)


def pair_back(qkv, lse, datt, c, c_d, rows, half, length):
    q, k, v = (qkv[:, pl.ds(i * half + c, LANE)] for i in range(3))
    grad = datt[:, pl.ds(c_d, LANE)]
    scaled, plain = head_masks(BF16, 0.125), head_masks(BF16, 1.0)
    dq = []
    dk, dv = [0.0, 0.0], [0.0, 0.0]
    for group in range(2):
        here = slice(group * rows, (group + 1) * rows)
        dq_here = 0.0
        for h in range(2):
            query, above = q[here] * scaled[h], grad[here] * plain[h]
            log_total = lse(h, here)
            probs, dprobs = [], []
            delta = 0.0
            for which in range(group + 1):
                there = slice(which * rows, (which + 1) * rows)
                scores = live_scores(k[there], query, length) if which == 0 else mm_nt(k[there], query)
                prob = jnp.exp(scores - log_total)
                dprob = mm_nt(v[there], above)
                delta = delta + jnp.sum(prob * dprob, axis=0, keepdims=True)
                dv[which] = dv[which] + mm(prob.astype(BF16), above)
                probs.append(prob)
                dprobs.append(dprob)
            for which in range(group + 1):
                there = slice(which * rows, (which + 1) * rows)
                dscore = (probs[which] * (dprobs[which] - delta)).astype(BF16)
                dk[which] = dk[which] + mm(dscore, query)
                dq_here = dq_here + mm_tn(dscore, k[there] * scaled[h])
        dq.append(dq_here)
    return dq, dk, dv


def turn_kernel(plan, scalars, facts_a, facts_b, xa, xao, xb, xbo, pa, ra, pb, rb, dh_any, dhr_any, dya, dyao, dyb, dybo, gains_ref, shifts_ref, w_out, att_a, att_b, gu_any, *refs):
    dr_any, vec_ref, datt_any, go_any = refs[:4]
    targets = refs[4:-14]
    x_buf, p_buf, r_buf, dh_buf, dhr_buf, dy_buf, da_buf, o_buf, datt_buf, att_buf, gu_buf, dr_ref, go_ref, sems = refs[-14:]
    role, x, inner = scalars[0], scalars[1], scalars[2]
    rows, width = xa.shape
    rows2, half = 2 * rows, width // 2
    quarter = half // 2
    own = pl.multiple_of(x * quarter, LANE)
    col = pl.multiple_of(role * half, LANE)
    pairs = []
    for u, (xs, xo, ps, rs, dys, dyo) in enumerate(((xa, xao, pa, ra, dya, dyao), (xb, xbo, pb, rb, dyb, dybo))):
        here = pl.ds(u * rows2, rows2)
        pairs += both_halves(role, rows, [(xs, xo, x_buf, u * rows2), (dys, dyo, dy_buf, u * rows2)])
        pairs += [(ps, p_buf.at[here, :]), (rs, r_buf.at[here, :]), (dh_any.at[here, :], dh_buf.at[here, :]), (dhr_any.at[here, :], dhr_buf.at[here, :])]
    pairs.append((w_out.at[pl.ds(col, half), :], o_buf))
    for u, a in enumerate((att_a, att_b)):
        pairs.append((a.at[:, pl.ds(own, quarter)], att_buf.at[pl.ds(u * rows2, rows2), :]))
    pairs.append((gu_any, gu_buf))
    copies = copy_all(pairs, sems)
    count = len(pairs)
    vec_ref[...] = jnp.zeros_like(vec_ref)
    for u in range(2):
        gain, _ = table_rows(gains_ref, shifts_ref, (facts_a, facts_b)[u][1], 1)
        for i in range(8):
            copies[8 * u + i].wait()

        def norm(i, carry):
            here = pl.ds(pl.multiple_of(u * rows2 + i * LANE, LANE), LANE)
            residual = x_buf[here, :].astype(F32) + (p_buf[here, :].astype(F32) + r_buf[here, :].astype(F32))
            unit, rstd = norm_stats(residual)
            dh2 = dh_buf[here, :].astype(F32) + dhr_buf[here, :].astype(F32)
            grad = dy_buf[here, :].astype(F32) + norm_back(unit, rstd, gain, dh2)
            da_buf[here, :] = grad.astype(BF16)
            if u == 0:
                per = rows // LANE

                @pl.when(i // per == role)
                def _():
                    dr_ref[pl.ds(pl.multiple_of((i % per) * LANE, LANE), LANE), :] = grad
                    vec_ref[0:1, :] += jnp.sum(dh2 * unit, axis=0, keepdims=True)
                    vec_ref[1:2, :] += jnp.sum(dh2, axis=0, keepdims=True)

            return carry

        lax.fori_loop(0, rows2 // LANE, norm, 0)
    writes = [pltpu.make_async_copy(s, t, sems.at[count + i]) for i, (s, t) in enumerate(((dr_ref, dr_any), (go_ref, go_any), (datt_buf, datt_any)))]
    writes[0].start()
    for each in copies[16:]:
        each.wait()
    go_ref[...] = mm_tn(att_buf[...], da_buf[...]).astype(BF16)
    writes[1].start()
    wire_sems = sems.at[pl.ds(count + 3, max(1, plan_sems(plan)))]
    wire_copies(plan, inner, {"o": go_ref, "u": gu_buf}, targets, wire_sems, "start")
    datt_buf[...] = mm_nt(da_buf[...], o_buf[...]).astype(BF16)
    writes[2].start()
    wire_copies(plan, inner, {"o": go_ref, "u": gu_buf}, targets, wire_sems, "wait")
    for each in writes:
        each.wait()


def turn(plan, scalars, facts, values, parts, came, dh, dh_came, dys, gains, shifts, w_out, atts, grad_up):
    rows2, width = 2 * values[0].shape[0], values[0].shape[1]
    half = width // 2
    big = lambda *s: pltpu.VMEM(s, BF16)
    tokens = 2 * rows2
    shapes = plan_shapes(plan, width)
    return pl.pallas_call(
        functools.partial(turn_kernel, plan),
        in_specs=[SMEM] * 3 + [HBM] * 14 + [VMEM] * 2 + [HBM] * 4,
        out_specs=[HBM, VMEM, HBM, HBM] + [HBM] * len(shapes),
        out_shape=[full((rows2 // 2, width), F32), full((8, width), F32), full((tokens, half), BF16), full((half // 2, width), BF16)] + shapes,
        scratch_shapes=[big(tokens, width)] * 7
        + [big(half, width), big(tokens, half), big(tokens, half // 2), big(*grad_up.shape), pltpu.VMEM((rows2 // 2, width), F32), big(half // 2, width), pltpu.SemaphoreType.DMA((23 + max(1, plan_sems(plan)),))],
        compiler_params=params(60),
        cost_estimate=cost(12e9, 8e6),
        name="turn",
    )(scalars, *facts, *values, parts[0], came[0], parts[1], came[1], dh, dh_came, *dys, gains, shifts, w_out, *atts, grad_up)


def back_kernel(plan, scalars, facts_a, facts_b, datt_any, qkv_a, qkv_b, ht_a, ht_b, go_any, lse_a, lse_b, *refs):
    dqa_any = refs[0]
    targets = refs[1:-7]
    datt_buf, qkv_buf, ht_buf, dq_buf, gq_ref, go_buf, sems = refs[-7:]
    x, inner = scalars[1], scalars[2]
    tokens, half = datt_any.shape
    rows2 = tokens // 2
    rows, quarter = rows2 // 2, half // 2
    own = pl.multiple_of(x * quarter, LANE)
    lse = (lse_a, lse_b)
    first_half, second_half = pl.ds(0, rows2), pl.ds(rows2, rows2)
    pairs = []
    for here, q in ((first_half, qkv_a), (second_half, qkv_b)):
        pairs += [(q, qkv_buf.at[here, :]), (datt_any.at[here, :], datt_buf.at[here, :])]
    pairs += [(ht_a, ht_buf.at[:, first_half]), (ht_b, ht_buf.at[:, second_half]), (go_any, go_buf)]
    copies = copy_all(pairs, sems)
    count = len(pairs)
    for u in range(2):
        copies[2 * u].wait()
        copies[2 * u + 1].wait()
        base = u * rows2
        length = (facts_a, facts_b)[u][0]

        def one(at, carry):
            c = pl.multiple_of(own + at * LANE, LANE)
            to = pl.multiple_of(at * LANE, LANE)
            first = (own + at * LANE) // HEAD
            look = lambda h, here: lse[u][pl.ds(first + h, 1), here]
            dq, dk, dv = pair_back(qkv_buf.at[pl.ds(base, rows2), :], look, datt_buf.at[pl.ds(base, rows2), :], c, c, rows, half, length)
            for i, halves in enumerate((dq, dk, dv)):
                for g in range(2):
                    dq_buf[base + g * rows : base + (g + 1) * rows, pl.ds(i * quarter + to, LANE)] = halves[g].astype(BF16)
            return carry

        lax.fori_loop(0, quarter // LANE, one, 0)
    write = pltpu.make_async_copy(dq_buf.at[first_half, :], dqa_any, sems.at[count])
    write.start()
    for each in copies[4:]:
        each.wait()
    for i in range(3):
        cols = slice(i * quarter, (i + 1) * quarter)
        gq_ref[:, cols] = mm(ht_buf[...], dq_buf[:, cols]).astype(BF16)
    pieces = {"q": gq_ref, "o": go_buf}
    wire_sems = sems.at[pl.ds(count + 1, plan_sems(plan))]
    wire_copies(plan, inner, pieces, targets, wire_sems, "start")
    wire_copies(plan, inner, pieces, targets, wire_sems, "wait")
    write.wait()


def back(plan, scalars, facts, datt, qkvs, hts, grad_out, lses):
    tokens, half = datt.shape
    width = 2 * half
    big = lambda *s: pltpu.VMEM(s, BF16)
    shapes = plan_shapes(plan, width)
    return pl.pallas_call(
        functools.partial(back_kernel, plan),
        in_specs=[SMEM] * 3 + [HBM] * 6 + [VMEM] * 2,
        out_specs=[HBM] * (1 + len(shapes)),
        out_shape=[full((tokens // 2, 3 * half // 2), BF16)] + shapes,
        scratch_shapes=[big(tokens, half), big(tokens, 3 * half), big(width, tokens), big(tokens, 3 * half // 2), big(width, 3 * half // 2), big(*grad_out.shape), pltpu.SemaphoreType.DMA((8 + plan_sems(plan),))],
        compiler_params=params(60),
        cost_estimate=cost(14e9, 8e6),
        name="back",
    )(scalars, *facts, datt, *qkvs, *hts, grad_out, *lses)


def last_kernel(scalars, facts, qkv_ref, lse_ref, datt_ref, dqa_ref, w_qkv, keep_ref, send_ref, w_own, w_buf, dq_buf, sems):
    role, x, length = scalars[0], scalars[1], facts[0]
    rows2, half = qkv_ref.shape[0], datt_ref.shape[1]
    rows, quarter, width = rows2 // 2, half // 2, 2 * half
    mine = pl.multiple_of(x * quarter, LANE)
    other = pl.multiple_of((1 - x) * quarter, LANE)
    col = pl.multiple_of(role * half, LANE)
    copies = copy_all(
        [(w_qkv.at[:, pl.ds(i * width + col + from_, quarter)], to.at[:, pl.ds(i * quarter, quarter)]) for from_, to in ((mine, w_own), (other, w_buf)) for i in range(3)],
        sems,
    )

    def one(at, carry):
        c = pl.multiple_of(other + at * LANE, LANE)
        to = pl.multiple_of(at * LANE, LANE)
        first = (other + at * LANE) // HEAD
        look = lambda h, here: lse_ref[pl.ds(first + h, 1), here]
        dq, dk, dv = pair_back(qkv_ref, look, datt_ref, c, c, rows, half, length)
        for i, halves in enumerate((dq, dk, dv)):
            for g in range(2):
                dq_buf[g * rows : (g + 1) * rows, pl.ds(i * quarter + to, LANE)] = halves[g].astype(BF16)
        return carry

    lax.fori_loop(0, quarter // LANE, one, 0)
    for each in copies:
        each.wait()
    keep = pl.ds(pl.multiple_of(role * rows, rows), rows)
    send = pl.ds(pl.multiple_of((1 - role) * rows, rows), rows)
    keep_ref[...] = mm_nt(dqa_ref[keep, :], w_own[...]) + mm_nt(dq_buf[keep, :], w_buf[...])
    send_ref[...] = (mm_nt(dqa_ref[send, :], w_own[...]) + mm_nt(dq_buf[send, :], w_buf[...])).astype(BF16)


def last(scalars, facts, qkv, lse, datt, dqa, w_qkv):
    rows2, half = qkv.shape[0], datt.shape[1]
    width = 2 * half
    big = lambda *s: pltpu.VMEM(s, BF16)
    return pl.pallas_call(
        last_kernel,
        in_specs=[SMEM] * 2 + [VMEM] * 4 + [HBM],
        out_specs=[VMEM] * 2,
        out_shape=[full((rows2 // 2, width), F32), full((rows2 // 2, width), BF16)],
        scratch_shapes=[big(width, 3 * half // 2)] * 2 + [big(rows2, 3 * half // 2), pltpu.SemaphoreType.DMA((6,))],
        compiler_params=params(60),
        cost_estimate=cost(7e9, 8e6),
        name="last",
    )(scalars, facts, qkv, lse, datt, dqa, w_qkv)


class Layout:
    def __init__(self, width, ff, sections, members):
        self.width, self.ff, self.members = width, ff, members
        shapes = {"q": (width, 3 * width), "o": (width, width), "u": (width, ff), "d": (ff, width), "s": (4 * sections, width)}
        start, self.spans = 0, {}
        for name, (rows, columns) in shapes.items():
            self.spans[name] = (start, rows, columns)
            start += rows * columns
        self.total = start
        self.share = start // members
        self.segments = [self.parts_of(m) for m in range(members)]
        self.rows = max(s[-1]["at"] + s[-1]["wire"] for s in self.segments)

    def span(self, member, name):
        start, rows, columns = self.spans[name]
        low = max(member * self.share, start) - start
        high = min((member + 1) * self.share, start + rows * columns) - start
        return (low, high) if low < high else None

    def parts_of(self, member):
        parts, at = [], 0
        for name in ("q", "o", "u", "d"):
            found = self.span(member, name)
            if found is None:
                continue
            columns = self.spans[name][2]
            low, high = found[0] // columns, -(-found[1] // columns)
            if name == "o":
                held = [r % (self.width // 4) for r in range(low, high)]
                low, high = min(held), max(held) + 1
            if name == "d":
                held = [r // (4 * LANE) * LANE + r % LANE for r in range(low, high)]
                low, high = min(held), max(held) + 1
            low, high = low // 16 * 16, -(-high // 16) * 16
            count = high - low
            wire = -(-(3 * count // 4) // 16) * 16 if name == "q" else count
            parts.append({"name": name, "low": low, "high": high, "at": at, "wire": wire})
            at += wire
        return parts

    def table(self):
        rows = []
        for share in range(2 * self.members):
            entry = [share * (self.share // 2) // LANE]
            held = {p["name"]: p for p in self.segments[share // 2]}
            for name in ("q", "o", "u", "d"):
                p = held.get(name)
                entry += [p["low"], p["high"], p["at"], p["wire"]] if p else [0, 0, 0, 0]
            rows.append(entry + [0] * (24 - len(entry)))
        return np.asarray(rows, np.int32)

    def regions(self, member, low, high):
        found = []

        def cut(name, row, column, rows, columns, to_row, to_column):
            first, last = max(to_row, low), min(to_row + rows, high)
            if first < last:
                found.append((name, row + first - to_row, column, last - first, columns, first - low, to_column))

        for p in self.segments[member]:
            if p["name"] == "q":
                quarter = self.width // 4
                side = p["high"] - p["low"] - p["wire"]
                cut("q", p["low"], 0, p["wire"], 3 * quarter, p["at"], 0)
                for i in range(3):
                    cut("q", p["low"] + p["wire"], i * quarter, side, quarter, p["at"] + i * side, 3 * quarter)
            else:
                cut(p["name"], p["low"], 0, p["wire"], self.width, p["at"], 0)
        return found

    def plans(self):
        stage_of = {"u": 0, "d": 0, "o": 1, "q": 2}
        stages = ([], [], [])
        for block in reversed(range(self.members // 2)):
            edges = {0, self.rows}
            for member in (2 * block, 2 * block + 1):
                for p in self.segments[member]:
                    edges |= {p["at"], p["at"] + p["wire"]}
            edges = sorted(edges)
            runs = []
            for low, high in zip(edges, edges[1:]):
                found = [stage_of[f[0]] for member in (2 * block, 2 * block + 1) for f in self.regions(member, low, high)]
                stage = max(found) if found else runs[-1][2]
                if runs and (runs[-1][2] == stage or 2 in (stage, runs[-1][2])):
                    runs[-1][1], runs[-1][2] = high, max(stage, runs[-1][2])
                else:
                    runs.append([low, high, stage])
            for low, high, stage in runs:
                middle = low + (high - low) * 5 // 8 // 16 * 16
                for first, last in [(low, middle), (middle, high)] if stage == 2 else [(low, high)]:
                    regions = [self.regions(2 * block + i, first, last) for i in range(2)]
                    stages[stage].append({"block": block, "low": first, "high": last, "regions": regions, "most": max(map(len, regions))})
        return stages


def after(value, *first):
    return lax.optimization_barrier((value, *first))[0]


def add(left, right):
    return (left.astype(F32) + right.astype(F32)).astype(BF16)


def tree_pairs(block, level, count):
    size = 2 << level
    pairs = []
    for low in range(0, count, size):
        middle, high = low + size // 2, low + size
        left, right = min(max(block, low), middle - 1), min(max(block, middle), high - 1)
        source, target = (right, left) if block < middle else (left, right)
        pairs += [(2 * source + y, 2 * target + y) for y in range(2)]
    return pairs


def place_kernel(spans, table, *refs):
    quad, (small_ref, out_ref, wire, flat, sems) = refs[:-5], refs[-5:]
    me, unit0 = table[24], table[0]
    units = out_ref.shape[0]
    width = wire.shape[2]
    chunks = width // LANE
    front = 512
    x, role = me // 2, me % 2
    where = (me, role + 2 * (1 - x), (1 - role) + 2 * x, (1 - role) + 2 * (1 - x))
    per_piece = len(quad) // 4
    pairs = []
    for i, source in enumerate(quad):
        rows = source.shape[0]
        first = sum(s.shape[0] for s in quad[i // per_piece * per_piece : i])
        pairs.append((source, wire.at[where[i // per_piece], pl.ds(first, rows), :]))
    copies = copy_all(pairs, sems.at[pl.ds(1, len(pairs))])
    for each in copies:
        each.wait()

    def rows_of(name, per_row):
        at = 1 + 4 * "qoud".index(name)
        low, high = table[at], table[at + 1]
        base = unit0 - spans[name][0] // LANE
        first = jnp.maximum(low // 16, jnp.maximum(base, 0) // per_row // 16)
        last = jnp.minimum(high // 16, (jnp.maximum(base + units, 0) + per_row * 16 - 1) // (per_row * 16))
        return low, first, last, table[at + 2], table[at + 3], base

    low, first, last, at, n1, base = rows_of("q", 3 * chunks)
    n2 = table[2] - table[1] - n1

    def qkv(g, carry):
        row = g * 16 - low
        to = front + g * 16 * 3 * chunks - base
        beside = row >= n1
        half = chunks // 4
        for section in range(3):
            source = jnp.where(beside, at + section * n2 + row - n1, at + row)
            for h in range(half):
                column = pl.multiple_of(jnp.where(beside, 3 * width // 4 + h * LANE, section * (width // 4) + h * LANE), LANE)
                for piece in range(4):
                    unit = section * chunks + (piece % 2) * (chunks // 2) + (piece // 2) * half + h
                    flat[pl.ds(to + unit, 16, stride=3 * chunks), :] = wire[piece, pl.ds(pl.multiple_of(source, 16), 16), pl.ds(column, LANE)].astype(F32)
        return carry

    lax.fori_loop(first, jnp.maximum(first, last), qkv, 0)
    per = spans["u"][2] // LANE
    low, first, last, at, _, base = rows_of("u", per)

    def up(g, carry):
        source = pl.multiple_of(at + g * 16 - low, 16)
        to = front + g * 16 * per - base
        for h in range(chunks):
            for piece in range(4):
                flat[pl.ds(to + 4 * h + piece, 16, stride=per), :] = wire[piece, pl.ds(source, 16), h * LANE : (h + 1) * LANE].astype(F32)
        return carry

    lax.fori_loop(first, jnp.maximum(first, last), up, 0)

    for name in ("o", "d"):
        slot = 1 + 4 * "qoud".index(name)
        low, high, at = table[slot], table[slot + 1], table[slot + 2]
        base = unit0 - spans[name][0] // LANE

        def rows(g, carry):
            row = g * 16
            source = pl.multiple_of(at + row - low, 16)
            for piece in range(4):
                if name == "o":
                    line = (piece % 2) * (width // 2) + (piece // 2) * (width // 4) + row
                else:
                    line = (row // LANE) * (4 * LANE) + piece * LANE + row % LANE
                to = line * chunks - base

                @pl.when((to + 16 * chunks > 0) & (to < units))
                def _():
                    for h in range(chunks):
                        flat[pl.ds(front + to + h, 16, stride=chunks), :] = wire[piece, pl.ds(source, 16), h * LANE : (h + 1) * LANE].astype(F32)

            return carry

        lax.fori_loop(low // 16, high // 16, rows, 0)

    tail = spans["s"][0] // LANE - unit0

    @pl.when(tail < units)
    def _():
        for g in range(small_ref.shape[0] // 8):
            for h in range(chunks):
                flat[pl.ds(front + tail + g * 8 * chunks + h, 8, stride=chunks), :] = small_ref[g * 8 : (g + 1) * 8, h * LANE : (h + 1) * LANE]

    done = pltpu.make_async_copy(flat.at[pl.ds(front, units), :], out_ref, sems.at[0])
    done.start()
    done.wait()


def place(layout, table, quad, small):
    rows, width = layout.rows, layout.width
    units = layout.share // 2 // LANE
    quad = [part for piece in quad for part in piece]
    return pl.pallas_call(
        functools.partial(place_kernel, layout.spans),
        in_specs=[SMEM] + [HBM] * len(quad) + [VMEM],
        out_specs=HBM,
        out_shape=full((units, LANE), F32),
        scratch_shapes=[pltpu.VMEM((4, rows, width), BF16), pltpu.VMEM((-(-units // 8) * 8 + 1024, LANE), F32), pltpu.SemaphoreType.DMA((1 + len(quad),))],
        compiler_params=params(60),
        cost_estimate=cost(4e9, 8e6),
        name="place",
    )(table, *quad, small)


def local(frames, cotangent, w_qkv, w_out, w_up, w_down, gains, shifts, prompt_len, section):
    width, ff, sections = frames.shape[3], w_up.shape[1], gains.shape[0]
    role, group, member = lax.axis_index("role"), lax.axis_index("group"), lax.axis_index("member")
    x = group % 2
    members, groups = lax.axis_size("member"), lax.axis_size("group")
    layout = Layout(width, ff, sections, members)
    early, middle, late = layout.plans()
    outer, inner = member // 2, member % 2
    count = members // 2

    own_frames, own_cot = frames[0, 0], cotangent[0, 0]
    values = [own_frames, swap(own_frames, "role")]
    mate_frames = swap(own_frames, "group")
    facts = jnp.concatenate([prompt_len, section])
    mate_facts = swap(facts, "group")
    scalars = jnp.stack([role, x, inner]).astype(jnp.int32)

    levels = count.bit_length() - 1
    kept = span_of(middle, "u")
    chunks = []

    def exchange(plan, arrays, *first):
        for i, chunk in enumerate(plan):
            keep, send = arrays[2 * i], arrays[2 * i + 1]
            chunks.append(dict(chunk, total=keep, came=swap(after(send, *first) if first else send, "member"), level=0))

    def climb(chunk):
        chunk["came"] = lax.ppermute(chunk["total"], "member", tree_pairs(chunk["block"], chunk["level"], count))
        chunk["level"] += 1

    def settle(chunk, *first):
        total = after(chunk["total"], *first) if first else chunk["total"]
        chunk["total"] = add(total, chunk["came"])

    first = attend(scalars, facts, values[:2], gains, shifts, w_qkv, w_out)
    mate_facts, mate_frames = after(mate_facts, first[3]), after(mate_frames, first[3])
    both = (facts, mate_facts)
    values += [mate_frames, swap(mate_frames, "role")]
    own_cot = after(own_cot, mate_frames)
    mate_cot = swap(own_cot, "group")
    dys = [own_cot, swap(own_cot, "role"), mate_cot, swap(mate_cot, "role")]
    second = attend(scalars, mate_facts, values[2:], gains, shifts, w_qkv, w_out)
    hts, qkvs, atts, parts, lses = zip(first, second)
    came = [after(swap(parts[0], "role"), parts[1]), swap(parts[1], "role")]
    hidden, act, dup, residual, grad_up, *wires = own_units(early, kept, scalars, both, values, parts, came, dys, gains, shifts, w_up, w_down)
    exchange(early, wires)
    dh, out_keep, out_send = rest_units(scalars, hidden, dys, act, dup, residual, w_up, w_down)
    output = (out_keep + swap(out_send, "role").astype(F32)).astype(BF16)
    dh_came = swap(after(dh, chunks[0]["came"]), "role")
    settle(chunks[0], dh)
    climb(chunks[0])
    dr1, vec_two, datt, grad_out, *wires = turn(shifted(middle, "u", kept[0]), scalars, both, values, parts, came, dh, dh_came, dys, gains, shifts, w_out, atts, grad_up)
    exchange(middle, wires)
    second_chunk = chunks[min(1, len(early) - 1)]
    if second_chunk is not chunks[0]:
        pass
    dqa, *wires = back(late, scalars, both, datt, qkvs, hts, grad_out, lses)
    exchange(late, wires, *(c["came"] for c in chunks[len(early) :]))
    if second_chunk is not chunks[0]:
        settle(second_chunk, dqa)
        climb(second_chunk)
    for chunk in chunks[: min(2, len(early))]:
        settle(chunk, dqa)
    joined = chunks[: min(2, len(early))]
    for chunk in chunks[min(2, len(early)) :]:
        settle(chunk, dqa)
        mates = [c for c in joined if c["block"] == chunk["block"] and c["level"] == 0 and (chunk["high"] == c["low"] or chunk["low"] == c["high"])]
        if mates and not any(chunk is c for c in chunks[-len(late) :]):
            ends = sorted((mates[0], chunk), key=lambda c: c["low"])
            mates[0]["total"] = jnp.concatenate([c["total"] for c in ends], 0)
            mates[0]["low"], mates[0]["high"] = ends[0]["low"], ends[1]["high"]
        else:
            joined.append(chunk)
    chunks = joined
    dh1_keep, dh1_send = last(scalars, facts, qkvs[0], lses[0], after(datt, chunks[-1]["total"]), dqa, w_qkv)
    dh1 = dh1_keep + swap(dh1_send, "role").astype(F32)
    unit, rstd = norm_stats(own_frames.astype(F32))
    input_grad = dr1 + norm_back(unit, rstd, lax.dynamic_slice(gains, (facts[1], 0, 0), (1, 1, width))[0].astype(F32), dh1)

    vectors = jnp.stack([jnp.stack([jnp.sum(dh1 * unit, 0), vec_two[0]]), jnp.stack([jnp.sum(dh1, 0), vec_two[1]])])
    select = (jnp.arange(sections, dtype=jnp.int32) == facts[1]).astype(F32)
    small = select[None, :, None, None] * vectors[:, None]
    small = jnp.pad(small.reshape(4 * sections, width), ((0, -4 * sections % 8), (0, 0)))
    small_steps = []
    for axis in ("role", "group", "member"):
        distance = 1
        while distance < lax.axis_size(axis):
            small = small + swap(small, axis, distance)
            small_steps.append(small)
            distance *= 2

    for chunk in chunks:
        if chunk["level"] == 0:
            climb(chunk)
            settle(chunk)
    for level in range(1, levels):
        for i, chunk in enumerate(chunks):
            if level == levels - 1 and i >= len(chunks) - 2:
                chunk["total"] = after(chunk["total"], small_steps[-3 if i == len(chunks) - 2 else -2])
            climb(chunk)
            settle(chunk)
    edges = [0, layout.rows * 5 // 8 // 16 * 16, layout.rows]
    quads = [[], [], [], []]
    for low, high in zip(edges, edges[1:]):
        final = jnp.zeros((high - low, width), BF16)
        for chunk in chunks:
            first, past = max(low, chunk["low"]), min(high, chunk["high"])
            if first >= past:
                continue
            here = chunk["total"][first - chunk["low"] : past - chunk["low"]]
            part = jnp.where(outer == chunk["block"], here, final[first - low : past - low])
            final = jnp.concatenate([final[: first - low], part, final[past - low :]], 0)
        distance = 2
        while distance < groups:
            final = add(final, swap(final, "group", distance))
            distance *= 2
        if high == layout.rows:
            final = after(final, small, quads[1][0])
        mate = swap(final, "group")
        for into, value in zip(quads, (final, mate, swap(final, "role"), swap(mate, "role"))):
            into.append(value)
    table = lax.dynamic_slice(jnp.asarray(layout.table()), (2 * member + role, 0), (1, 24))[0]
    table = jnp.concatenate([table, (role + 2 * x)[None].astype(jnp.int32), jnp.zeros((7,), jnp.int32)])
    shard = place(layout, table, quads, small).reshape(-1)
    return output[None, None], input_grad[None, None], shard


def solution(mesh):
    rows = P(("group", "member"), "role", None, None)
    per_seq = P(("group", "member"))
    return jax.shard_map(
        local,
        mesh=mesh,
        in_specs=(rows, rows, P(), P(), P(), P(), P(), P(), per_seq, per_seq),
        out_specs=(rows, rows, P(("member", "role"))),
        check_vma=False,
    )
```

```python
import functools

import jax
import jax.numpy as jnp
import numpy as np
from jax import lax
from jax.experimental import pallas as pl
from jax.experimental.pallas import tpu as pltpu
from jax.sharding import PartitionSpec as P

HEADS = 16
LANE = 128
HEAD = 64
F32 = jnp.float32
BF16 = jnp.bfloat16


def dot(left, right, dims):
    return lax.dot_general(left, right, (dims, ((), ())), preferred_element_type=F32)


def mm(left, right):
    return dot(left, right, ((1,), (0,)))


def mm_nt(left, right):
    return dot(left, right, ((1,), (1,)))


def mm_tn(left, right):
    return dot(left, right, ((0,), (0,)))


def swap(value, axis, distance=1):
    count = lax.axis_size(axis)
    return lax.ppermute(value, axis, [(i, i ^ distance) for i in range(count)])


def norm_stats(values):
    center = values - jnp.mean(values, axis=-1, keepdims=True)
    rstd = lax.rsqrt(jnp.mean(center * center, axis=-1, keepdims=True) + 1e-05)
    return center * rstd, rstd


def norm_back(unit, rstd, gain, grad):
    grad_unit = grad * gain
    inner = grad_unit - jnp.mean(grad_unit, axis=-1, keepdims=True)
    return rstd * (inner - unit * jnp.mean(grad_unit * unit, axis=-1, keepdims=True))


def full(shape, dtype):
    return jax.ShapeDtypeStruct(shape, dtype)


def params(mib):
    return pltpu.CompilerParams(vmem_limit_bytes=mib * 2**20)


def cost(flops, moved):
    return pl.CostEstimate(flops=int(flops), bytes_accessed=int(moved), transcendentals=0)


HBM = pl.BlockSpec(memory_space=pltpu.HBM)
SMEM = pl.BlockSpec(memory_space=pltpu.SMEM)
VMEM = pl.BlockSpec(memory_space=pltpu.VMEM)


def copy_all(pairs, sems):
    copies = [pltpu.make_async_copy(source, target, sems.at[i]) for i, (source, target) in enumerate(pairs)]
    for each in copies:
        each.start()
    return copies


def head_masks(dtype, scale):
    lane = lax.broadcasted_iota(jnp.int32, (1, LANE), 1)
    return [jnp.where(lane // HEAD == h, scale, 0.0).astype(dtype) for h in range(2)]


def live_scores(key, query, length):
    scores = mm_nt(key, query)
    return jnp.where(lax.broadcasted_iota(jnp.int32, scores.shape, 0) < length, scores, -1e30)


def span_of(plan, name):
    rows = [edge for chunk in plan for regions in chunk["regions"] for r in regions if r[0] == name for edge in (r[1], r[1] + r[3])]
    return (min(rows), max(rows)) if rows else (0, 16)


def shifted(plan, name, by):
    move = lambda r: (r[0], r[1] - by, *r[2:]) if r[0] == name else r
    return [dict(chunk, regions=[[move(r) for r in regions] for regions in chunk["regions"]]) for chunk in plan]


def wire_copies(plan, inner, pieces, targets, sems, act, names="qoud"):
    for parity in range(2):

        @pl.when(inner == parity)
        def _():
            at = to = 0
            for chunk in plan:
                for regions in (chunk["regions"][parity], chunk["regions"][1 - parity]):
                    for i, (name, row, column, rows, columns, to_row, to_column) in enumerate(regions):
                        if name in names:
                            source = pieces[name].at[pl.ds(row, rows), pl.ds(column, columns)]
                            target = targets[to].at[pl.ds(to_row, rows), pl.ds(to_column, columns)]
                            getattr(pltpu.make_async_copy(source, target, sems.at[at + i]), act)()
                    at += chunk["most"]
                    to += 1


def plan_shapes(plan, width):
    return [full((chunk["high"] - chunk["low"], width), BF16) for chunk in plan for _ in range(2)]


def plan_sems(plan):
    return sum(2 * chunk["most"] for chunk in plan)


def table_rows(gains_ref, shifts_ref, section, which):
    return gains_ref[section, which : which + 1, :].astype(F32), shifts_ref[section, which : which + 1, :].astype(F32)


def attend_kernel(scalars, facts, own_any, other_any, gains_ref, shifts_ref, w_qkv, w_out, ht_any, qkv_any, att_any, part_any, lse_ref,
                  x_buf, w_buf, o_buf, h_buf, ht_ref, qkv_ref, att_ref, part_ref, sems):
    role, length = scalars[0], facts[0]
    gain, shift = table_rows(gains_ref, shifts_ref, facts[1], 0)
    width, half = w_out.shape[1], w_out.shape[0] // 2
    rows = own_any.shape[0]
    col = pl.multiple_of(role * half, LANE)
    mine, theirs = (pl.ds(pl.multiple_of(r * rows, rows), rows) for r in (role, 1 - role))
    copies = copy_all(
        [(own_any, x_buf.at[mine, :]), (other_any, x_buf.at[theirs, :])]
        + [(w_qkv.at[:, pl.ds(i * width + col, half)], w_buf.at[:, pl.ds(i * half, half)]) for i in range(3)]
        + [(w_out.at[pl.ds(col, half), :], o_buf)],
        sems,
    )
    copies[0].wait()
    copies[1].wait()
    for at in range(0, 2 * rows, LANE):
        unit, _ = norm_stats(x_buf[at : at + LANE, :].astype(F32))
        hidden = (unit * gain + shift).astype(BF16)
        h_buf[at : at + LANE, :] = hidden
        ht_ref[:, at : at + LANE] = hidden.T
    writes = [pltpu.make_async_copy(s, t, sems.at[6 + i]) for i, (s, t) in enumerate(((ht_ref, ht_any), (qkv_ref, qkv_any), (att_ref, att_any), (part_ref, part_any)))]
    writes[0].start()
    for i in range(3):
        copies[2 + i].wait()
        qkv_ref[:, i * half : (i + 1) * half] = mm(h_buf[...], w_buf[:, i * half : (i + 1) * half]).astype(BF16)
    writes[1].start()

    def pair(at, carry):
        c = pl.multiple_of(at * LANE, LANE)
        q, k, v = (qkv_ref[:, pl.ds(i * half + c, LANE)] for i in range(3))
        q_masks, v_masks = head_masks(BF16, 0.125), head_masks(BF16, 1.0)
        for group in range(2):
            total = 0.0
            for h in range(2):
                query = q[group * rows : (group + 1) * rows] * q_masks[h]
                scores = [live_scores(k[:rows], query, length)]
                if group:
                    scores.append(mm_nt(k[rows:], query))
                top = jnp.max(scores[0], axis=0, keepdims=True)
                if group:
                    top = jnp.maximum(top, jnp.max(scores[1], axis=0, keepdims=True))
                powers = [jnp.exp(s - top) for s in scores]
                below = sum(jnp.sum(p, axis=0, keepdims=True) for p in powers)
                lse_ref[pl.ds(2 * at + h, 1), group * rows : (group + 1) * rows] = top + jnp.log(below)
                inverse = 1.0 / below
                for which, p in enumerate(powers):
                    prob = (p * inverse).astype(BF16)
                    total = total + mm_tn(prob, v[which * rows : (which + 1) * rows] * v_masks[h])
            att_ref[group * rows : (group + 1) * rows, pl.ds(c, LANE)] = total.astype(BF16)
        return carry

    lax.fori_loop(0, half // LANE, pair, 0)
    writes[2].start()
    copies[5].wait()
    part_ref[...] = mm(att_ref[...], o_buf[...]).astype(BF16)
    writes[3].start()
    for each in writes:
        each.wait()


def attend(scalars, facts, halves, gains, shifts, w_qkv, w_out):
    rows, width = 2 * halves[0].shape[0], halves[0].shape[1]
    half = width // 2
    outs = [(width, rows), (rows, 3 * half), (rows, half), (rows, width)]
    return pl.pallas_call(
        attend_kernel,
        in_specs=[SMEM, SMEM, HBM, HBM, VMEM, VMEM, HBM, HBM],
        out_specs=[HBM] * 4 + [VMEM],
        out_shape=[full(s, BF16) for s in outs] + [full((half // HEAD, rows), F32)],
        scratch_shapes=[pltpu.VMEM((rows, width), BF16), pltpu.VMEM((width, 3 * half), BF16), pltpu.VMEM((half, width), BF16), pltpu.VMEM((rows, width), BF16)]
        + [pltpu.VMEM(s, BF16) for s in outs] + [pltpu.SemaphoreType.DMA((10,))],
        compiler_params=params(60),
        cost_estimate=cost(12e9, 8e6),
        name="attend",
    )(scalars, facts, *halves, gains, shifts, w_qkv, w_out)


def unit_copies(w_up, w_down, up_buf, down_buf, first):
    blocks = w_up.shape[1] // (4 * LANE)
    pairs = []
    for b in range(blocks):
        at = pl.multiple_of((4 * b + first) * LANE, LANE)
        pairs.append((w_up.at[:, pl.ds(at, LANE)], up_buf.at[:, pl.ds(b * LANE, LANE)]))
    for b in range(blocks):
        at = pl.multiple_of((4 * b + first) * LANE, LANE)
        pairs.append((w_down.at[pl.ds(at, LANE), :], down_buf.at[pl.ds(b * LANE, LANE), :]))
    return pairs


def gelu_parts(up):
    cdf = 0.5 + 0.5 * lax.erf(up * np.float32(0.5**0.5))
    slope = cdf + up * (jnp.exp(-0.5 * up * up) * np.float32(1 / np.sqrt(2 * np.pi)))
    return up * cdf, slope


def both_halves(role, rows, pairs):
    out = []
    for own, other, buffer, first in pairs:
        for source, r in ((own, role), (other, 1 - role)):
            out.append((source, buffer.at[pl.ds(pl.multiple_of(first + r * rows, rows), rows), :]))
    return out


def own_kernel(plan, kept, scalars, facts_a, facts_b, xa, xao, xb, xbo, pa, ra, pb, rb, dya, dyao, dyb, dybo, gains_ref, shifts_ref, w_up, w_down, *refs):
    h_any, act_any, dup_any, res_any, gu_any = refs[:5]
    targets = refs[5:-14]
    x_buf, p_buf, r_buf, dy_buf, up_buf, down_buf, ht_buf, h_ref, gd_ref, gu_ref, act_ref, dup_ref, res_ref, sems = refs[-14:]
    role, x, inner = scalars[0], scalars[1], scalars[2]
    half_rows = xa.shape[0]
    rows = 2 * half_rows
    quarter = up_buf.shape[1]
    sources = both_halves(role, half_rows, [(xa, xao, x_buf, 0)]) + [(pa, p_buf.at[pl.ds(0, rows), :]), (ra, r_buf.at[pl.ds(0, rows), :])]
    sources += both_halves(role, half_rows, [(xb, xbo, x_buf, rows)]) + [(pb, p_buf.at[pl.ds(rows, rows), :]), (rb, r_buf.at[pl.ds(rows, rows), :])]
    sources += unit_copies(w_up, w_down, up_buf, down_buf, role + 2 * x)
    sources += both_halves(role, half_rows, [(dya, dyao, dy_buf, 0), (dyb, dybo, dy_buf, rows)])
    copies = copy_all(sources, sems)
    count = len(sources)
    for u in range(2):
        gain, shift = table_rows(gains_ref, shifts_ref, (facts_a, facts_b)[u][1], 1)
        for i in range(4):
            copies[4 * u + i].wait()

        def norm(i, carry):
            at = pl.multiple_of(u * rows + i * LANE, LANE)
            here = pl.ds(at, LANE)
            residual = x_buf[here, :].astype(F32) + (p_buf[here, :].astype(F32) + r_buf[here, :].astype(F32))
            unit, _ = norm_stats(residual)
            hidden = (unit * gain + shift).astype(BF16)
            h_ref[here, :] = hidden
            ht_buf[:, here] = hidden.T
            if u == 0:
                per = half_rows // LANE

                @pl.when(i // per == role)
                def _():
                    res_ref[pl.ds(pl.multiple_of((i % per) * LANE, LANE), LANE), :] = residual

            return carry

        lax.fori_loop(0, rows // LANE, norm, 0)
    writes = [pltpu.make_async_copy(s, t, sems.at[count + i]) for i, (s, t) in enumerate(((h_ref, h_any), (res_ref, res_any), (act_ref, act_any), (dup_ref, dup_any), (gu_ref.at[pl.ds(kept[0], kept[1] - kept[0]), :], gu_any)))]
    writes[0].start()
    writes[1].start()
    for each in copies[8:]:
        each.wait()

    def block(i, carry):
        cols = pl.ds(pl.multiple_of(i * 256, 256), 256)
        act, slope = gelu_parts(mm(h_ref[...], up_buf[:, cols]))
        act = act.astype(BF16)
        act_ref[:, cols] = act[:rows]
        dup_ref[:, cols] = (mm_nt(dy_buf[...], down_buf[cols, :]) * slope).astype(BF16)
        gd_ref[cols, :] = mm_tn(act, dy_buf[...]).astype(BF16)
        return carry

    lax.fori_loop(0, quarter // 256, block, 0)
    pieces = {"d": gd_ref, "u": gu_ref}
    wire_sems = sems.at[pl.ds(count + 5, plan_sems(plan))]
    wire_copies(plan, inner, pieces, targets, wire_sems, "start", "d")
    writes[2].start()
    writes[3].start()

    def wide(i, carry):
        cols = pl.ds(pl.multiple_of(i * 256, 256), 256)
        gu_ref[:, cols] = mm(ht_buf[...], dup_ref[:, cols]).astype(BF16)
        return carry

    lax.fori_loop(0, quarter // 256, wide, 0)
    wire_copies(plan, inner, pieces, targets, wire_sems, "start", "u")
    writes[4].start()
    wire_copies(plan, inner, pieces, targets, wire_sems, "wait")
    for each in writes:
        each.wait()


def own_units(plan, kept, scalars, facts, values, parts, came, dys, gains, shifts, w_up, w_down):
    rows, width = 2 * values[0].shape[0], values[0].shape[1]
    quarter = w_up.shape[1] // 4
    count = 8 + 2 * (quarter // LANE) + 4 + 5 + plan_sems(plan)
    big = lambda *s: pltpu.VMEM(s, BF16)
    shapes = plan_shapes(plan, width)
    return pl.pallas_call(
        functools.partial(own_kernel, plan, kept),
        in_specs=[SMEM] * 3 + [HBM] * 12 + [VMEM] * 2 + [HBM] * 2,
        out_specs=[HBM] * (5 + len(shapes)),
        out_shape=[full((2 * rows, width), BF16), full((rows, quarter), BF16), full((2 * rows, quarter), BF16), full((rows // 2, width), F32), full((kept[1] - kept[0], quarter), BF16)] + shapes,
        scratch_shapes=[big(2 * rows, width)] * 4
        + [big(width, quarter), big(quarter, width), big(width, 2 * rows), big(2 * rows, width), big(quarter, width), big(width, quarter), big(rows, quarter), big(2 * rows, quarter), pltpu.VMEM((rows // 2, width), F32), pltpu.SemaphoreType.DMA((count,))],
        compiler_params=params(60),
        cost_estimate=cost(20e9, 8e6),
        name="own_units",
    )(scalars, *facts, *values, parts[0], came[0], parts[1], came[1], *dys, gains, shifts, w_up, w_down)


def rest_kernel(scalars, h_any, dya, dyao, dyb, dybo, act_any, dup_any, res_ref, w_up, w_down, dh_ref, keep_ref, send_ref,
                h_buf, dy_buf, act_own, act_buf, dup_own, dup_buf, up_own, down_own, up_buf, down_buf, sems):
    role, x = scalars[0], scalars[1]
    rows = 2 * dya.shape[0]
    quarter = up_buf.shape[1]
    blocks = quarter // LANE
    copies = copy_all(
        [(h_any, h_buf)]
        + unit_copies(w_up, w_down, up_buf, down_buf, role + 2 * (1 - x))
        + both_halves(role, rows // 2, [(dya, dyao, dy_buf, 0), (dyb, dybo, dy_buf, rows)])
        + [(act_any, act_own), (dup_any, dup_own)]
        + unit_copies(w_up, w_down, up_own, down_own, role + 2 * x),
        sems,
    )
    first = 1 + 2 * blocks + 4
    for each in copies[:first]:
        each.wait()

    def block(i, carry):
        cols = pl.ds(pl.multiple_of(i * 256, 256), 256)
        act, slope = gelu_parts(mm(h_buf[...], up_buf[:, cols]))
        act_buf[:, cols] = act[:rows].astype(BF16)
        dup_buf[:, cols] = (mm_nt(dy_buf[...], down_buf[cols, :]) * slope).astype(BF16)
        return carry

    lax.fori_loop(0, quarter // 256, block, 0)
    for each in copies[first:]:
        each.wait()

    def back(i, carry):
        here = pl.ds(pl.multiple_of(i * 256, 256), 256)
        dh_ref[here, :] = (mm_nt(dup_own[here, :], up_own[...]) + mm_nt(dup_buf[here, :], up_buf[...])).astype(BF16)
        return carry

    lax.fori_loop(0, 2 * rows // 256, back, 0)
    keep = pl.ds(pl.multiple_of(role * (rows // 2), rows // 2), rows // 2)
    send = pl.ds(pl.multiple_of((1 - role) * (rows // 2), rows // 2), rows // 2)
    keep_ref[...] = res_ref[...] + (mm(act_own[keep, :], down_own[...]) + mm(act_buf[keep, :], down_buf[...]))
    send_ref[...] = (mm(act_own[send, :], down_own[...]) + mm(act_buf[send, :], down_buf[...])).astype(BF16)


def rest_units(scalars, hidden, dys, act, dup, residual, w_up, w_down):
    rows, width = 2 * dys[0].shape[0], dys[0].shape[1]
    quarter = w_up.shape[1] // 4
    count = 7 + 4 * (quarter // LANE)
    big = lambda *s: pltpu.VMEM(s, BF16)
    return pl.pallas_call(
        rest_kernel,
        in_specs=[SMEM] + [HBM] * 7 + [VMEM] + [HBM] * 2,
        out_specs=[VMEM] * 3,
        out_shape=[full((2 * rows, width), BF16), full((rows // 2, width), F32), full((rows // 2, width), BF16)],
        scratch_shapes=[big(2 * rows, width)] * 2 + [big(rows, quarter)] * 2 + [big(2 * rows, quarter)] * 2 + [big(width, quarter), big(quarter, width)] * 2 + [pltpu.SemaphoreType.DMA((count,))],
        compiler_params=params(60),
        cost_estimate=cost(20e9, 8e6),
        name="rest_units",
    )(scalars, hidden, *dys, act, dup, residual, w_up, w_down)


def pair_back(qkv, lse, datt, c, c_d, rows, half, length):
    q, k, v = (qkv[:, pl.ds(i * half + c, LANE)] for i in range(3))
    grad = datt[:, pl.ds(c_d, LANE)]
    scaled, plain = head_masks(BF16, 0.125), head_masks(BF16, 1.0)
    dq = []
    dk, dv = [0.0, 0.0], [0.0, 0.0]
    for group in range(2):
        here = slice(group * rows, (group + 1) * rows)
        dq_here = 0.0
        for h in range(2):
            query, above = q[here] * scaled[h], grad[here] * plain[h]
            log_total = lse(h, here)
            probs, dprobs = [], []
            delta = 0.0
            for which in range(group + 1):
                there = slice(which * rows, (which + 1) * rows)
                scores = live_scores(k[there], query, length) if which == 0 else mm_nt(k[there], query)
                prob = jnp.exp(scores - log_total)
                dprob = mm_nt(v[there], above)
                delta = delta + jnp.sum(prob * dprob, axis=0, keepdims=True)
                dv[which] = dv[which] + mm(prob.astype(BF16), above)
                probs.append(prob)
                dprobs.append(dprob)
            for which in range(group + 1):
                there = slice(which * rows, (which + 1) * rows)
                dscore = (probs[which] * (dprobs[which] - delta)).astype(BF16)
                dk[which] = dk[which] + mm(dscore, query)
                dq_here = dq_here + mm_tn(dscore, k[there] * scaled[h])
        dq.append(dq_here)
    return dq, dk, dv


def turn_kernel(plan, scalars, facts_a, facts_b, xa, xao, xb, xbo, pa, ra, pb, rb, dh_any, dhr_any, dya, dyao, dyb, dybo, gains_ref, shifts_ref, w_out, att_a, att_b, gu_any, *refs):
    dr_any, vec_ref, datt_any, go_any = refs[:4]
    targets = refs[4:-14]
    x_buf, p_buf, r_buf, dh_buf, dhr_buf, dy_buf, da_buf, o_buf, datt_buf, att_buf, gu_buf, dr_ref, go_ref, sems = refs[-14:]
    role, x, inner = scalars[0], scalars[1], scalars[2]
    rows, width = xa.shape
    rows2, half = 2 * rows, width // 2
    quarter = half // 2
    own = pl.multiple_of(x * quarter, LANE)
    col = pl.multiple_of(role * half, LANE)
    pairs = []
    for u, (xs, xo, ps, rs, dys, dyo) in enumerate(((xa, xao, pa, ra, dya, dyao), (xb, xbo, pb, rb, dyb, dybo))):
        here = pl.ds(u * rows2, rows2)
        pairs += both_halves(role, rows, [(xs, xo, x_buf, u * rows2), (dys, dyo, dy_buf, u * rows2)])
        pairs += [(ps, p_buf.at[here, :]), (rs, r_buf.at[here, :]), (dh_any.at[here, :], dh_buf.at[here, :]), (dhr_any.at[here, :], dhr_buf.at[here, :])]
    pairs.append((w_out.at[pl.ds(col, half), :], o_buf))
    for u, a in enumerate((att_a, att_b)):
        pairs.append((a.at[:, pl.ds(own, quarter)], att_buf.at[pl.ds(u * rows2, rows2), :]))
    pairs.append((gu_any, gu_buf))
    copies = copy_all(pairs, sems)
    count = len(pairs)
    vec_ref[...] = jnp.zeros_like(vec_ref)
    for u in range(2):
        gain, _ = table_rows(gains_ref, shifts_ref, (facts_a, facts_b)[u][1], 1)
        for i in range(8):
            copies[8 * u + i].wait()

        def norm(i, carry):
            here = pl.ds(pl.multiple_of(u * rows2 + i * LANE, LANE), LANE)
            residual = x_buf[here, :].astype(F32) + (p_buf[here, :].astype(F32) + r_buf[here, :].astype(F32))
            unit, rstd = norm_stats(residual)
            dh2 = dh_buf[here, :].astype(F32) + dhr_buf[here, :].astype(F32)
            grad = dy_buf[here, :].astype(F32) + norm_back(unit, rstd, gain, dh2)
            da_buf[here, :] = grad.astype(BF16)
            if u == 0:
                per = rows // LANE

                @pl.when(i // per == role)
                def _():
                    dr_ref[pl.ds(pl.multiple_of((i % per) * LANE, LANE), LANE), :] = grad
                    vec_ref[0:1, :] += jnp.sum(dh2 * unit, axis=0, keepdims=True)
                    vec_ref[1:2, :] += jnp.sum(dh2, axis=0, keepdims=True)

            return carry

        lax.fori_loop(0, rows2 // LANE, norm, 0)
    writes = [pltpu.make_async_copy(s, t, sems.at[count + i]) for i, (s, t) in enumerate(((dr_ref, dr_any), (go_ref, go_any), (datt_buf, datt_any)))]
    writes[0].start()
    for each in copies[16:]:
        each.wait()
    go_ref[...] = mm_tn(att_buf[...], da_buf[...]).astype(BF16)
    writes[1].start()
    wire_sems = sems.at[pl.ds(count + 3, max(1, plan_sems(plan)))]
    wire_copies(plan, inner, {"o": go_ref, "u": gu_buf}, targets, wire_sems, "start")
    datt_buf[...] = mm_nt(da_buf[...], o_buf[...]).astype(BF16)
    writes[2].start()
    wire_copies(plan, inner, {"o": go_ref, "u": gu_buf}, targets, wire_sems, "wait")
    for each in writes:
        each.wait()


def turn(plan, scalars, facts, values, parts, came, dh, dh_came, dys, gains, shifts, w_out, atts, grad_up):
    rows2, width = 2 * values[0].shape[0], values[0].shape[1]
    half = width // 2
    big = lambda *s: pltpu.VMEM(s, BF16)
    tokens = 2 * rows2
    shapes = plan_shapes(plan, width)
    return pl.pallas_call(
        functools.partial(turn_kernel, plan),
        in_specs=[SMEM] * 3 + [HBM] * 14 + [VMEM] * 2 + [HBM] * 4,
        out_specs=[HBM, VMEM, HBM, HBM] + [HBM] * len(shapes),
        out_shape=[full((rows2 // 2, width), F32), full((8, width), F32), full((tokens, half), BF16), full((half // 2, width), BF16)] + shapes,
        scratch_shapes=[big(tokens, width)] * 7
        + [big(half, width), big(tokens, half), big(tokens, half // 2), big(*grad_up.shape), pltpu.VMEM((rows2 // 2, width), F32), big(half // 2, width), pltpu.SemaphoreType.DMA((23 + max(1, plan_sems(plan)),))],
        compiler_params=params(60),
        cost_estimate=cost(12e9, 8e6),
        name="turn",
    )(scalars, *facts, *values, parts[0], came[0], parts[1], came[1], dh, dh_came, *dys, gains, shifts, w_out, *atts, grad_up)


def back_kernel(plan, scalars, facts_a, facts_b, datt_any, qkv_a, qkv_b, ht_a, ht_b, go_any, lse_a, lse_b, *refs):
    dqa_any = refs[0]
    targets = refs[1:-7]
    datt_buf, qkv_buf, ht_buf, dq_buf, gq_ref, go_buf, sems = refs[-7:]
    x, inner = scalars[1], scalars[2]
    tokens, half = datt_any.shape
    rows2 = tokens // 2
    rows, quarter = rows2 // 2, half // 2
    own = pl.multiple_of(x * quarter, LANE)
    lse = (lse_a, lse_b)
    first_half, second_half = pl.ds(0, rows2), pl.ds(rows2, rows2)
    pairs = []
    for here, q in ((first_half, qkv_a), (second_half, qkv_b)):
        pairs += [(q, qkv_buf.at[here, :]), (datt_any.at[here, :], datt_buf.at[here, :])]
    pairs += [(ht_a, ht_buf.at[:, first_half]), (ht_b, ht_buf.at[:, second_half]), (go_any, go_buf)]
    copies = copy_all(pairs, sems)
    count = len(pairs)
    for u in range(2):
        copies[2 * u].wait()
        copies[2 * u + 1].wait()
        base = u * rows2
        length = (facts_a, facts_b)[u][0]

        def one(at, carry):
            c = pl.multiple_of(own + at * LANE, LANE)
            to = pl.multiple_of(at * LANE, LANE)
            first = (own + at * LANE) // HEAD
            look = lambda h, here: lse[u][pl.ds(first + h, 1), here]
            dq, dk, dv = pair_back(qkv_buf.at[pl.ds(base, rows2), :], look, datt_buf.at[pl.ds(base, rows2), :], c, c, rows, half, length)
            for i, halves in enumerate((dq, dk, dv)):
                for g in range(2):
                    dq_buf[base + g * rows : base + (g + 1) * rows, pl.ds(i * quarter + to, LANE)] = halves[g].astype(BF16)
            return carry

        lax.fori_loop(0, quarter // LANE, one, 0)
    write = pltpu.make_async_copy(dq_buf.at[first_half, :], dqa_any, sems.at[count])
    write.start()
    for each in copies[4:]:
        each.wait()
    for i in range(3):
        cols = slice(i * quarter, (i + 1) * quarter)
        gq_ref[:, cols] = mm(ht_buf[...], dq_buf[:, cols]).astype(BF16)
    pieces = {"q": gq_ref, "o": go_buf}
    wire_sems = sems.at[pl.ds(count + 1, plan_sems(plan))]
    wire_copies(plan, inner, pieces, targets, wire_sems, "start")
    wire_copies(plan, inner, pieces, targets, wire_sems, "wait")
    write.wait()


def back(plan, scalars, facts, datt, qkvs, hts, grad_out, lses):
    tokens, half = datt.shape
    width = 2 * half
    big = lambda *s: pltpu.VMEM(s, BF16)
    shapes = plan_shapes(plan, width)
    return pl.pallas_call(
        functools.partial(back_kernel, plan),
        in_specs=[SMEM] * 3 + [HBM] * 6 + [VMEM] * 2,
        out_specs=[HBM] * (1 + len(shapes)),
        out_shape=[full((tokens // 2, 3 * half // 2), BF16)] + shapes,
        scratch_shapes=[big(tokens, half), big(tokens, 3 * half), big(width, tokens), big(tokens, 3 * half // 2), big(width, 3 * half // 2), big(*grad_out.shape), pltpu.SemaphoreType.DMA((8 + plan_sems(plan),))],
        compiler_params=params(60),
        cost_estimate=cost(14e9, 8e6),
        name="back",
    )(scalars, *facts, datt, *qkvs, *hts, grad_out, *lses)


def last_kernel(scalars, facts, qkv_ref, lse_ref, datt_ref, dqa_ref, w_qkv, keep_ref, send_ref, w_own, w_buf, dq_buf, sems):
    role, x, length = scalars[0], scalars[1], facts[0]
    rows2, half = qkv_ref.shape[0], datt_ref.shape[1]
    rows, quarter, width = rows2 // 2, half // 2, 2 * half
    mine = pl.multiple_of(x * quarter, LANE)
    other = pl.multiple_of((1 - x) * quarter, LANE)
    col = pl.multiple_of(role * half, LANE)
    copies = copy_all(
        [(w_qkv.at[:, pl.ds(i * width + col + from_, quarter)], to.at[:, pl.ds(i * quarter, quarter)]) for from_, to in ((mine, w_own), (other, w_buf)) for i in range(3)],
        sems,
    )

    def one(at, carry):
        c = pl.multiple_of(other + at * LANE, LANE)
        to = pl.multiple_of(at * LANE, LANE)
        first = (other + at * LANE) // HEAD
        look = lambda h, here: lse_ref[pl.ds(first + h, 1), here]
        dq, dk, dv = pair_back(qkv_ref, look, datt_ref, c, c, rows, half, length)
        for i, halves in enumerate((dq, dk, dv)):
            for g in range(2):
                dq_buf[g * rows : (g + 1) * rows, pl.ds(i * quarter + to, LANE)] = halves[g].astype(BF16)
        return carry

    lax.fori_loop(0, quarter // LANE, one, 0)
    for each in copies:
        each.wait()
    keep = pl.ds(pl.multiple_of(role * rows, rows), rows)
    send = pl.ds(pl.multiple_of((1 - role) * rows, rows), rows)
    keep_ref[...] = mm_nt(dqa_ref[keep, :], w_own[...]) + mm_nt(dq_buf[keep, :], w_buf[...])
    send_ref[...] = (mm_nt(dqa_ref[send, :], w_own[...]) + mm_nt(dq_buf[send, :], w_buf[...])).astype(BF16)


def last(scalars, facts, qkv, lse, datt, dqa, w_qkv):
    rows2, half = qkv.shape[0], datt.shape[1]
    width = 2 * half
    big = lambda *s: pltpu.VMEM(s, BF16)
    return pl.pallas_call(
        last_kernel,
        in_specs=[SMEM] * 2 + [VMEM] * 4 + [HBM],
        out_specs=[VMEM] * 2,
        out_shape=[full((rows2 // 2, width), F32), full((rows2 // 2, width), BF16)],
        scratch_shapes=[big(width, 3 * half // 2)] * 2 + [big(rows2, 3 * half // 2), pltpu.SemaphoreType.DMA((6,))],
        compiler_params=params(60),
        cost_estimate=cost(7e9, 8e6),
        name="last",
    )(scalars, facts, qkv, lse, datt, dqa, w_qkv)


class Layout:
    def __init__(self, width, ff, sections, members):
        self.width, self.ff, self.members = width, ff, members
        shapes = {"q": (width, 3 * width), "o": (width, width), "u": (width, ff), "d": (ff, width), "s": (4 * sections, width)}
        start, self.spans = 0, {}
        for name, (rows, columns) in shapes.items():
            self.spans[name] = (start, rows, columns)
            start += rows * columns
        self.total = start
        self.share = start // members
        self.segments = [self.parts_of(m) for m in range(members)]
        self.rows = max(s[-1]["at"] + s[-1]["wire"] for s in self.segments)

    def span(self, member, name):
        start, rows, columns = self.spans[name]
        low = max(member * self.share, start) - start
        high = min((member + 1) * self.share, start + rows * columns) - start
        return (low, high) if low < high else None

    def parts_of(self, member):
        parts, at = [], 0
        for name in ("q", "o", "u", "d"):
            found = self.span(member, name)
            if found is None:
                continue
            columns = self.spans[name][2]
            low, high = found[0] // columns, -(-found[1] // columns)
            if name == "o":
                held = [r % (self.width // 4) for r in range(low, high)]
                low, high = min(held), max(held) + 1
            if name == "d":
                held = [r // (4 * LANE) * LANE + r % LANE for r in range(low, high)]
                low, high = min(held), max(held) + 1
            low, high = low // 16 * 16, -(-high // 16) * 16
            count = high - low
            wire = -(-(3 * count // 4) // 16) * 16 if name == "q" else count
            parts.append({"name": name, "low": low, "high": high, "at": at, "wire": wire})
            at += wire
        return parts

    def table(self):
        rows = []
        for share in range(2 * self.members):
            entry = [share * (self.share // 2) // LANE]
            held = {p["name"]: p for p in self.segments[share // 2]}
            for name in ("q", "o", "u", "d"):
                p = held.get(name)
                entry += [p["low"], p["high"], p["at"], p["wire"]] if p else [0, 0, 0, 0]
            rows.append(entry + [0] * (24 - len(entry)))
        return np.asarray(rows, np.int32)

    def regions(self, member, low, high):
        found = []

        def cut(name, row, column, rows, columns, to_row, to_column):
            first, last = max(to_row, low), min(to_row + rows, high)
            if first < last:
                found.append((name, row + first - to_row, column, last - first, columns, first - low, to_column))

        for p in self.segments[member]:
            if p["name"] == "q":
                quarter = self.width // 4
                side = p["high"] - p["low"] - p["wire"]
                cut("q", p["low"], 0, p["wire"], 3 * quarter, p["at"], 0)
                for i in range(3):
                    cut("q", p["low"] + p["wire"], i * quarter, side, quarter, p["at"] + i * side, 3 * quarter)
            else:
                cut(p["name"], p["low"], 0, p["wire"], self.width, p["at"], 0)
        return found

    def plans(self):
        stage_of = {"u": 0, "d": 0, "o": 1, "q": 2}
        stages = ([], [], [])
        for block in reversed(range(self.members // 2)):
            edges = {0, self.rows}
            for member in (2 * block, 2 * block + 1):
                for p in self.segments[member]:
                    edges |= {p["at"], p["at"] + p["wire"]}
            edges = sorted(edges)
            runs = []
            for low, high in zip(edges, edges[1:]):
                found = [stage_of[f[0]] for member in (2 * block, 2 * block + 1) for f in self.regions(member, low, high)]
                stage = max(found) if found else runs[-1][2]
                if runs and (runs[-1][2] == stage or 2 in (stage, runs[-1][2])):
                    runs[-1][1], runs[-1][2] = high, max(stage, runs[-1][2])
                else:
                    runs.append([low, high, stage])
            for low, high, stage in runs:
                middle = low + (high - low) * 21 // 32 // 16 * 16
                for first, last in [(low, middle), (middle, high)] if stage == 2 else [(low, high)]:
                    regions = [self.regions(2 * block + i, first, last) for i in range(2)]
                    stages[stage].append({"block": block, "low": first, "high": last, "regions": regions, "most": max(map(len, regions))})
        return stages


def after(value, *first):
    return lax.optimization_barrier((value, *first))[0]


def add(left, right):
    return (left.astype(F32) + right.astype(F32)).astype(BF16)


def tree_pairs(block, level, count):
    size = 2 << level
    pairs = []
    for low in range(0, count, size):
        middle, high = low + size // 2, low + size
        left, right = min(max(block, low), middle - 1), min(max(block, middle), high - 1)
        source, target = (right, left) if block < middle else (left, right)
        pairs += [(2 * source + y, 2 * target + y) for y in range(2)]
    return pairs


def place_kernel(spans, table, *refs):
    quad, (small_ref, out_ref, wire, flat, sems) = refs[:-5], refs[-5:]
    me, unit0 = table[24], table[0]
    units = out_ref.shape[0]
    width = wire.shape[2]
    chunks = width // LANE
    front = 512
    x, role = me // 2, me % 2
    where = (me, role + 2 * (1 - x), (1 - role) + 2 * x, (1 - role) + 2 * (1 - x))
    per_piece = len(quad) // 4
    pairs = []
    for i, source in enumerate(quad):
        rows = source.shape[0]
        first = sum(s.shape[0] for s in quad[i // per_piece * per_piece : i])
        pairs.append((source, wire.at[where[i // per_piece], pl.ds(first, rows), :]))
    copies = copy_all(pairs, sems.at[pl.ds(1, len(pairs))])
    for each in copies:
        each.wait()

    def rows_of(name, per_row):
        at = 1 + 4 * "qoud".index(name)
        low, high = table[at], table[at + 1]
        base = unit0 - spans[name][0] // LANE
        first = jnp.maximum(low // 16, jnp.maximum(base, 0) // per_row // 16)
        last = jnp.minimum(high // 16, (jnp.maximum(base + units, 0) + per_row * 16 - 1) // (per_row * 16))
        return low, first, last, table[at + 2], table[at + 3], base

    low, first, last, at, n1, base = rows_of("q", 3 * chunks)
    n2 = table[2] - table[1] - n1

    def qkv(g, carry):
        row = g * 16 - low
        to = front + g * 16 * 3 * chunks - base
        beside = row >= n1
        half = chunks // 4
        for section in range(3):
            source = jnp.where(beside, at + section * n2 + row - n1, at + row)
            for h in range(half):
                column = pl.multiple_of(jnp.where(beside, 3 * width // 4 + h * LANE, section * (width // 4) + h * LANE), LANE)
                for piece in range(4):
                    unit = section * chunks + (piece % 2) * (chunks // 2) + (piece // 2) * half + h
                    flat[pl.ds(to + unit, 16, stride=3 * chunks), :] = wire[piece, pl.ds(pl.multiple_of(source, 16), 16), pl.ds(column, LANE)].astype(F32)
        return carry

    lax.fori_loop(first, jnp.maximum(first, last), qkv, 0)
    per = spans["u"][2] // LANE
    low, first, last, at, _, base = rows_of("u", per)

    def up(g, carry):
        source = pl.multiple_of(at + g * 16 - low, 16)
        to = front + g * 16 * per - base
        for h in range(chunks):
            for piece in range(4):
                flat[pl.ds(to + 4 * h + piece, 16, stride=per), :] = wire[piece, pl.ds(source, 16), h * LANE : (h + 1) * LANE].astype(F32)
        return carry

    lax.fori_loop(first, jnp.maximum(first, last), up, 0)

    for name in ("o", "d"):
        slot = 1 + 4 * "qoud".index(name)
        low, high, at = table[slot], table[slot + 1], table[slot + 2]
        base = unit0 - spans[name][0] // LANE

        def rows(g, carry):
            row = g * 16
            source = pl.multiple_of(at + row - low, 16)
            for piece in range(4):
                if name == "o":
                    line = (piece % 2) * (width // 2) + (piece // 2) * (width // 4) + row
                else:
                    line = (row // LANE) * (4 * LANE) + piece * LANE + row % LANE
                to = line * chunks - base

                @pl.when((to + 16 * chunks > 0) & (to < units))
                def _():
                    for h in range(chunks):
                        flat[pl.ds(front + to + h, 16, stride=chunks), :] = wire[piece, pl.ds(source, 16), h * LANE : (h + 1) * LANE].astype(F32)

            return carry

        lax.fori_loop(low // 16, high // 16, rows, 0)

    tail = spans["s"][0] // LANE - unit0

    @pl.when(tail < units)
    def _():
        for g in range(small_ref.shape[0] // 8):
            for h in range(chunks):
                flat[pl.ds(front + tail + g * 8 * chunks + h, 8, stride=chunks), :] = small_ref[g * 8 : (g + 1) * 8, h * LANE : (h + 1) * LANE]

    done = pltpu.make_async_copy(flat.at[pl.ds(front, units), :], out_ref, sems.at[0])
    done.start()
    done.wait()


def place(layout, table, quad, small):
    rows, width = layout.rows, layout.width
    units = layout.share // 2 // LANE
    quad = [part for piece in quad for part in piece]
    return pl.pallas_call(
        functools.partial(place_kernel, layout.spans),
        in_specs=[SMEM] + [HBM] * len(quad) + [VMEM],
        out_specs=HBM,
        out_shape=full((units, LANE), F32),
        scratch_shapes=[pltpu.VMEM((4, rows, width), BF16), pltpu.VMEM((-(-units // 8) * 8 + 1024, LANE), F32), pltpu.SemaphoreType.DMA((1 + len(quad),))],
        compiler_params=params(60),
        cost_estimate=cost(4e9, 8e6),
        name="place",
    )(table, *quad, small)


def local(frames, cotangent, w_qkv, w_out, w_up, w_down, gains, shifts, prompt_len, section):
    width, ff, sections = frames.shape[3], w_up.shape[1], gains.shape[0]
    role, group, member = lax.axis_index("role"), lax.axis_index("group"), lax.axis_index("member")
    x = group % 2
    members, groups = lax.axis_size("member"), lax.axis_size("group")
    layout = Layout(width, ff, sections, members)
    early, middle, late = layout.plans()
    outer, inner = member // 2, member % 2
    count = members // 2

    own_frames, own_cot = frames[0, 0], cotangent[0, 0]
    values = [own_frames, swap(own_frames, "role")]
    mate_frames = swap(own_frames, "group")
    facts = jnp.concatenate([prompt_len, section])
    mate_facts = swap(facts, "group")
    scalars = jnp.stack([role, x, inner]).astype(jnp.int32)

    levels = count.bit_length() - 1
    kept = span_of(middle, "u")
    chunks = []

    def exchange(plan, arrays, *first):
        for i, chunk in enumerate(plan):
            keep, send = arrays[2 * i], arrays[2 * i + 1]
            chunks.append(dict(chunk, total=keep, came=swap(after(send, *first) if first else send, "member"), level=0))

    def climb(chunk):
        chunk["came"] = lax.ppermute(chunk["total"], "member", tree_pairs(chunk["block"], chunk["level"], count))
        chunk["level"] += 1

    def settle(chunk, *first):
        total = after(chunk["total"], *first) if first else chunk["total"]
        chunk["total"] = add(total, chunk["came"])

    first = attend(scalars, facts, values[:2], gains, shifts, w_qkv, w_out)
    mate_facts, mate_frames = after(mate_facts, first[3]), after(mate_frames, first[3])
    both = (facts, mate_facts)
    values += [mate_frames, swap(mate_frames, "role")]
    own_cot = after(own_cot, mate_frames)
    mate_cot = swap(own_cot, "group")
    dys = [own_cot, swap(own_cot, "role"), mate_cot, swap(mate_cot, "role")]
    second = attend(scalars, mate_facts, values[2:], gains, shifts, w_qkv, w_out)
    hts, qkvs, atts, parts, lses = zip(first, second)
    came = [after(swap(parts[0], "role"), parts[1]), swap(parts[1], "role")]
    hidden, act, dup, residual, grad_up, *wires = own_units(early, kept, scalars, both, values, parts, came, dys, gains, shifts, w_up, w_down)
    exchange(early, wires)
    dh, out_keep, out_send = rest_units(scalars, hidden, dys, act, dup, residual, w_up, w_down)
    output = (out_keep + swap(out_send, "role").astype(F32)).astype(BF16)
    dh_came = swap(after(dh, chunks[0]["came"]), "role")
    settle(chunks[0], dh)
    climb(chunks[0])
    dr1, vec_two, datt, grad_out, *wires = turn(shifted(middle, "u", kept[0]), scalars, both, values, parts, came, dh, dh_came, dys, gains, shifts, w_out, atts, grad_up)
    exchange(middle, wires)
    second_chunk = chunks[min(1, len(early) - 1)]
    if second_chunk is not chunks[0]:
        pass
    dqa, *wires = back(late, scalars, both, datt, qkvs, hts, grad_out, lses)
    exchange(late, wires, *(c["came"] for c in chunks[len(early) :]))
    if second_chunk is not chunks[0]:
        settle(second_chunk, dqa)
        climb(second_chunk)
    for chunk in chunks[: min(2, len(early))]:
        settle(chunk, dqa)
    joined = chunks[: min(2, len(early))]
    for chunk in chunks[min(2, len(early)) :]:
        settle(chunk, dqa)
        mates = [c for c in joined if c["block"] == chunk["block"] and c["level"] == 0 and (chunk["high"] == c["low"] or chunk["low"] == c["high"])]
        if mates and not any(chunk is c for c in chunks[-len(late) :]):
            ends = sorted((mates[0], chunk), key=lambda c: c["low"])
            mates[0]["total"] = jnp.concatenate([c["total"] for c in ends], 0)
            mates[0]["low"], mates[0]["high"] = ends[0]["low"], ends[1]["high"]
        else:
            joined.append(chunk)
    chunks = joined
    dh1_keep, dh1_send = last(scalars, facts, qkvs[0], lses[0], after(datt, chunks[-1]["total"]), dqa, w_qkv)
    dh1 = dh1_keep + swap(dh1_send, "role").astype(F32)
    unit, rstd = norm_stats(own_frames.astype(F32))
    input_grad = dr1 + norm_back(unit, rstd, lax.dynamic_slice(gains, (facts[1], 0, 0), (1, 1, width))[0].astype(F32), dh1)

    vectors = jnp.stack([jnp.stack([jnp.sum(dh1 * unit, 0), vec_two[0]]), jnp.stack([jnp.sum(dh1, 0), vec_two[1]])])
    select = (jnp.arange(sections, dtype=jnp.int32) == facts[1]).astype(F32)
    small = select[None, :, None, None] * vectors[:, None]
    small = jnp.pad(small.reshape(4 * sections, width), ((0, -4 * sections % 8), (0, 0)))
    small_steps = []
    for axis in ("role", "group", "member"):
        distance = 1
        while distance < lax.axis_size(axis):
            small = small + swap(small, axis, distance)
            small_steps.append(small)
            distance *= 2

    for chunk in chunks:
        if chunk["level"] == 0:
            climb(chunk)
            settle(chunk)
    for level in range(1, levels):
        for i, chunk in enumerate(chunks):
            if level == levels - 1 and i >= len(chunks) - 2:
                chunk["total"] = after(chunk["total"], small_steps[-3 if i == len(chunks) - 2 else -2])
            climb(chunk)
            settle(chunk)
    edges = [0, layout.rows * 21 // 32 // 16 * 16, layout.rows]
    quads = [[], [], [], []]
    for low, high in zip(edges, edges[1:]):
        final = jnp.zeros((high - low, width), BF16)
        for chunk in chunks:
            first, past = max(low, chunk["low"]), min(high, chunk["high"])
            if first >= past:
                continue
            here = chunk["total"][first - chunk["low"] : past - chunk["low"]]
            part = jnp.where(outer == chunk["block"], here, final[first - low : past - low])
            final = jnp.concatenate([final[: first - low], part, final[past - low :]], 0)
        distance = 2
        while distance < groups:
            final = add(final, swap(final, "group", distance))
            distance *= 2
        if high == layout.rows:
            final = after(final, small, quads[1][0])
        mate = swap(final, "group")
        for into, value in zip(quads, (final, mate, swap(final, "role"), swap(mate, "role"))):
            into.append(value)
    table = lax.dynamic_slice(jnp.asarray(layout.table()), (2 * member + role, 0), (1, 24))[0]
    table = jnp.concatenate([table, (role + 2 * x)[None].astype(jnp.int32), jnp.zeros((7,), jnp.int32)])
    shard = place(layout, table, quads, small).reshape(-1)
    return output[None, None], input_grad[None, None], shard


def solution(mesh):
    rows = P(("group", "member"), "role", None, None)
    per_seq = P(("group", "member"))
    return jax.shard_map(
        local,
        mesh=mesh,
        in_specs=(rows, rows, P(), P(), P(), P(), P(), P(), per_seq, per_seq),
        out_specs=(rows, rows, P(("member", "role"))),
        check_vma=False,
    )
```
